256 devices in a mesh: scen: 4 (over x_hi, core), tm: 64 (over z, x_lo, y).
Axes of the slice: x: 4 (x_hi: 2, x_lo: 2; x = x_hi * 2 + x_lo), y: 4, z: 8, core: 2. Of those that a mesh axis runs over, the one named last changes fastest.
Arguments:
- weights: float32 [512, 8, 128, 128], P('tm'), may hold values from 0.0002 to 0.04
- pattern: int32 [512, 8], P('tm'), may hold values 0 or 1
- shift_reg: float32 [512, 128], P('tm'), may hold values from 0.2 to 2
- rhs: float32 [512, 256, 128], P('tm', 'scen'), parts along dimension 1, may hold values from -24 to 24
Outputs:
- solution: float32 [512, 256, 128], P('tm', 'scen'), parts along dimension 1
- residual: float32 [512, 256, 128], P('tm', 'scen'), parts along dimension 1
The draws below stay inside these ranges and needn't reach their ends.
There are 4 independent parts, one for each index of `scen`. The reference program is written for one: setup_inputs(seed, part) draws one part's arguments, and reference() takes and returns one part's arrays. A program takes and returns all parts, laid end to end along the dimension named above; an argument that names none is the same for every part. Nothing has to cross between parts.
All inputs are finite; a program needn't handle non-finite values. No bound on the sum of `pattern` on one device may be relied on, other than what follows from the above.
Results may differ from the reference program's by a relative error of at most 0.0003.
Values sent between devices are 32-bit elements; how exact they have to be, the bound alone decides.
No kernel may reach another device: no remote copies, remote signals or barrier semaphores. Data moves between devices by JAX's collectives and lax.ppermute only.
A program may use at most 64 MiB of HBM per device.

```python
import math
import jax
import jax.numpy as jnp
from jax import lax

NODES = 128
OFFSETS = 8
RHS = 64
ITERS = 3
NBLOCKS = 512


def place_ends(result, own_key, least, largest):
    shape = result.shape
    index_at = [jax.random.randint(jax.random.fold_in(own_key, axis), (), 0, shape[axis]) for axis in range(len(shape))]
    result = result.at[tuple(index_at)].set(least)
    longest = shape.index(max(shape))
    index_at[longest] = (index_at[longest] + 1) % shape[longest]
    return result.at[tuple(index_at)].set(largest)


def block_scale(stream_key, dims, pieces, least, largest):
    level, own = 1.0, jax.random.fold_in(stream_key, 6)
    for dim, parts in pieces:
        heights = jnp.exp(jax.random.uniform(jax.random.fold_in(own, dim), (parts,), jnp.float32, least / len(pieces), largest / len(pieces)))
        level = level * jnp.repeat(heights, dims[dim] // parts).reshape([-1 if axis == dim else 1 for axis in range(len(dims))])
    return level


def scatter_about(own_key, dims, scale, most, shards=(), held_as=jnp.bfloat16):
    result = scale * jax.random.normal(own_key, dims, jnp.float32)
    if shards:
        result = result * block_scale(own_key, dims, shards, -0.22, 0.18)
    return jnp.clip(result, -most, most).astype(held_as)


def setup_inputs(seed: int = 0, part: int = 0) -> dict:
    splits = jax.random.split(jax.random.key(seed), 5)
    part_keys = jax.random.split(jax.random.fold_in(splits[4], part), 5)
    weights = jnp.clip(jnp.exp(math.log(0.04) - 5.2983174 * jax.random.uniform(splits[0], (NBLOCKS, OFFSETS, NODES, NODES), jnp.float32) ** block_scale(splits[0], (NBLOCKS, OFFSETS, NODES, NODES), ((0, 64),), -0.2, 0.2)), 0.0002, 0.04)
    pattern = place_ends((jax.random.randint(splits[1], (NBLOCKS, OFFSETS), 0, 4) < 3).astype(jnp.int32), jax.random.fold_in(splits[1], 1), 0, 1)
    shift_reg = jnp.clip(jnp.exp(math.log(2.0) - 2.3025851 * jax.random.uniform(splits[2], (NBLOCKS, NODES), jnp.float32) ** block_scale(splits[2], (NBLOCKS, NODES), ((0, 64),), -0.2, 0.2)), 0.2, 2.0)
    rhs = scatter_about(part_keys[3], (NBLOCKS, RHS, NODES), 4.0, 24.0, ((0, 64),), jnp.float32)
    return {"weights": weights, "pattern": pattern, "shift_reg": shift_reg, "rhs": rhs}


def operate(vector, masked, diag):
    total = diag[:, None, :] * vector
    for k in range(OFFSETS):
        ahead = jnp.roll(vector, -(k + 1), axis=0)
        total = total - jnp.einsum("trj,tij->tri", ahead, masked[:, k], precision=lax.Precision.HIGHEST)
        behind = jnp.roll(vector, k + 1, axis=0)
        earlier = jnp.roll(masked[:, k], k + 1, axis=0)
        total = total - jnp.einsum("tri,tij->trj", behind, earlier, precision=lax.Precision.HIGHEST)
    return total


def inner(first, second):
    return jnp.sum(first * second, axis=(0, 2))


def reference(weights, pattern, shift_reg, rhs):
    masked = weights * pattern.astype(jnp.float32)[:, :, None, None]
    rowsum = jnp.sum(masked, axis=(1, 3))
    colsum = jnp.sum(masked, axis=2)
    inflow = jnp.zeros_like(rowsum)
    for k in range(OFFSETS):
        inflow = inflow + jnp.roll(colsum[:, k], k + 1, axis=0)
    diag = rowsum + inflow + shift_reg
    solution = jnp.zeros_like(rhs)
    residual = rhs
    precond = residual / diag[:, None, :]
    direction = precond
    norm_now = inner(residual, precond)
    for step in range(ITERS):
        image = operate(direction, masked, diag)
        alpha = norm_now / inner(direction, image)
        solution = solution + alpha[None, :, None] * direction
        residual = residual - alpha[None, :, None] * image
        precond = residual / diag[:, None, :]
        norm_next = inner(residual, precond)
        direction = precond + (norm_next / norm_now)[None, :, None] * direction
        norm_now = norm_next
    return solution, residual
```

```python
import functools

import jax
import jax.numpy as jnp
from jax import lax
from jax.experimental import pallas as pl
from jax.experimental.pallas import tpu as pltpu
from jax.sharding import PartitionSpec as P

F32 = jnp.float32
BF16 = jnp.bfloat16
MIB = 1024 * 1024
N = 128
T = 8
R = 64
VMEM = pl.BlockSpec(memory_space=pltpu.VMEM)
SMEM = pl.BlockSpec(memory_space=pltpu.SMEM)

BAND = (T // 2, 2 * N, (T + 1) * N)


def call(body, outs, specs=None, scratch=(), limit=16, flops=0, moved=0):
    return pl.pallas_call(
        body,
        out_shape=outs,
        in_specs=specs,
        out_specs=jax.tree.map(lambda _: VMEM, outs),
        scratch_shapes=list(scratch),
        compiler_params=pltpu.CompilerParams(vmem_limit_bytes=limit * MIB),
        cost_estimate=pl.CostEstimate(flops=flops, bytes_accessed=moved, transcendentals=0),
    )


def shape(*dims, dtype=F32):
    return jax.ShapeDtypeStruct(dims, dtype)


def dot(a, b):
    return lax.dot_general(a, b, (((1,), (0,)), ((), ())), preferred_element_type=F32)


def dot_t(a, b):
    return lax.dot_general(a, b, (((1,), (1,)), ((), ())), preferred_element_type=F32)


def two_sum(a, b):
    s = a + b
    t = s - a
    return s, (a - (s - t)) + (b - t)


def dd_add(a, b):
    s, e = two_sum(a[0], b[0])
    return s, e + (a[1] + b[1])


def halves(a):
    t = a * 4097.0
    h = t - (t - a)
    return h, a - h


def two_prod(a, b):
    p = a * b
    ah, al = halves(a)
    bh, bl = halves(b)
    return p, ((ah * bh - p) + ah * bl + al * bh) + al * bl


def sums_kernel(pattern, weights, reg, high, low, own, ahead, buf, cols, sems):
    def copy(t):
        return pltpu.make_async_copy(weights.at[t], buf.at[t], sems.at[t])

    for t in range(T):
        copy(t).start()
    cols[...] = jnp.zeros_like(cols)
    zero = jnp.zeros((N, N), BF16)
    for a in range(T // 2):
        for piece in (high, low):
            piece[a, N : 2 * N, 0:N] = zero
            piece[a, 0:N, T * N : (T + 1) * N] = zero

    def step(a, carry):
        for half in range(2):
            t = 2 * a + half
            copy(t).wait()
            rows = jnp.zeros((N, N), F32)
            for k in range(T):
                m = buf[t, k] * pattern[t, k].astype(F32)
                rows = rows + m
                cols[t + k + 1] += jnp.sum(m.reshape(N // 8, 8, N), axis=0)
                h = m.astype(BF16)
                place = slice((k + half) * N, (k + half + 1) * N)
                high[a, half * N : (half + 1) * N, place] = h
                low[a, half * N : (half + 1) * N, place] = (m - h.astype(F32)).astype(BF16)
            own[pl.ds(t, 1), :] = reg[pl.ds(t, 1), :] + jnp.sum(rows.T, axis=0, keepdims=True)
        return carry

    lax.fori_loop(0, T // 2, step, 0)
    inflow = jnp.sum(cols[...], axis=1)
    own[...] += inflow[:T]
    ahead[...] = inflow[T:]


def sums(pattern, weights, reg):
    return call(
        sums_kernel,
        (shape(*BAND, dtype=BF16), shape(*BAND, dtype=BF16), shape(T, N), shape(T, N)),
        [SMEM, pl.BlockSpec(memory_space=pl.ANY), VMEM],
        [pltpu.VMEM((T, T, N, N), F32), pltpu.VMEM((2 * T, 8, N), F32), pltpu.SemaphoreType.DMA((T,))],
        flops=8 * T * T * N * N,
        moved=4 * T * T * N * N,
    )(pattern, weights, reg)


def put_pieces(pieces, t, value):
    h = value.astype(BF16)
    pieces[0:R, t * N : (t + 1) * N] = h
    pieces[R : 2 * R, t * N : (t + 1) * N] = (value - h.astype(F32)).astype(BF16)


def product(pieces, cols, high, low, mult):
    both = mult(pieces[:, cols], high)
    return (both[:R] + mult(pieces[0:R, cols], low)) + both[R:]


def to_next(pieces, high, low, out):
    for b in range(T // 2):
        total = None
        for a in range(b, T // 2):
            at = slice((7 + 2 * b - 2 * a) * N, (9 + 2 * b - 2 * a) * N)
            term = product(pieces, slice(a * 2 * N, (a + 1) * 2 * N), high[a, :, at], low[a, :, at], dot)
            total = term if total is None else total + term
        out[2 * b] = total[:, :N]
        out[2 * b + 1] = total[:, N:]


def within(pieces, high, low, out):
    out[0] = jnp.zeros((R, N), F32)
    for p in range(T // 2):
        total = None
        width = 2 * N if p < T // 2 - 1 else N
        for a in range(p + 1):
            at = slice(2 * (p - a) * N, 2 * (p - a) * N + width)
            term = product(pieces, slice(a * 2 * N, (a + 1) * 2 * N), high[a, :, at], low[a, :, at], dot)
            total = term if total is None else total + term
        out[2 * p + 1] = total[:, :N]
        if width > N:
            out[2 * p + 2] = total[:, N:]
    for a in range(T // 2):
        at = slice(0, (7 - 2 * a) * N)
        term = product(pieces, slice((2 * a + 1) * N, T * N), high[a, :, at], low[a, :, at], dot_t)
        out[2 * a] += term[:, :N]
        out[2 * a + 1] += term[:, N:]


def from_next(pieces, high, low, out):
    for a in range(T // 2):
        at = slice((7 - 2 * a) * N, (T + 1) * N)
        term = product(pieces, slice(0, (2 * a + 2) * N), high[a, :, at], low[a, :, at], dot_t)
        out[2 * a] += term[:, :N]
        out[2 * a + 1] += term[:, N:]


def moments(first, second):
    high = low = jnp.zeros((R, N), F32)
    for t in range(T):
        high, err = two_sum(high, first[t] * second[t])
        low = low + err
    return high, low


PIECES = pltpu.VMEM((2 * R, T * N), BF16)
ONE_WAY = 2 * 3 * 40 * R * N * N


def start_kernel(rhs, own, arrived, high, low, diag, vec, out, pieces):
    diag[...] = own[...] + arrived[...]
    for t in range(T):
        value = rhs[t] / diag[t : t + 1, :]
        vec[t] = value
        put_pieces(pieces, t, value)
    to_next(pieces, high, low, out)


def start(rhs, own, arrived, high, low):
    return call(
        start_kernel,
        (shape(T, N), shape(T, R, N), shape(T, R, N)),
        [VMEM] * 5,
        [PIECES],
        flops=ONE_WAY,
    )(rhs, own, arrived, high, low)


def contrib_kernel(vec, high, low, out, pieces):
    for t in range(T):
        put_pieces(pieces, t, vec[t])
    to_next(pieces, high, low, out)


def contrib(vec, high, low):
    return call(contrib_kernel, shape(T, R, N), [VMEM] * 3, [PIECES], flops=ONE_WAY)(vec, high, low)


def local_kernel(count, *refs):
    vecs, (image, high, low, out, found, pieces) = refs[:count], refs[count:]
    for t in range(T):
        put_pieces(pieces, t, vecs[-1][t])
    within(pieces, high, low, out)
    for i, vec in enumerate(vecs):
        h, l = moments(vec, image)
        found[i, 0] = h
        found[i, 1] = l


def local(vecs, image, high, low):
    return call(
        functools.partial(local_kernel, len(vecs)),
        (shape(T, R, N), shape(len(vecs), 2, R, N)),
        [VMEM] * (len(vecs) + 3),
        [PIECES],
        flops=2 * ONE_WAY,
    )(*vecs, image, high, low)


def finish_first_kernel(rhs_next, own_next, ahead, high, low, partial, out, pieces):
    scale = own_next[...] + ahead[...]
    for t in range(T):
        put_pieces(pieces, t, rhs_next[t] / scale[t : t + 1, :])
    out[...] = partial[...]
    from_next(pieces, high, low, out)


def finish_first(rhs_next, own_next, ahead, high, low, partial):
    return call(finish_first_kernel, shape(T, R, N), [VMEM] * 6, [PIECES], flops=ONE_WAY)(
        rhs_next, own_next, ahead, high, low, partial
    )


def finish_kernel(vec_next, high, low, partial, out, pieces):
    for t in range(T):
        put_pieces(pieces, t, vec_next[t])
    out[...] = partial[...]
    from_next(pieces, high, low, out)


def finish(vec_next, high, low, partial):
    return call(finish_kernel, shape(T, R, N), [VMEM] * 4, [PIECES], flops=ONE_WAY)(vec_next, high, low, partial)


def fold(found):
    high, low = (jnp.concatenate([f[i] for f in found], axis=0).T for i in range(2))
    value = (high[:N], low[:N])
    size = N
    while size > 8:
        size //= 2
        value = dd_add(tuple(v[:size] for v in value), tuple(v[size:] for v in value))
    for turn in (4, 2, 1):
        value = dd_add(value, tuple(pltpu.roll(v, turn, 0) for v in value))
    return value


def gram_kernel(v0, v1, v2, image, m0, m1, m2, out):
    last = [moments(v, image) for v in (v0, v1, v2)]
    every = [(m[i, 0], m[i, 1]) for m in (m0, m1, m2) for i in range(m.shape[0])] + last + last[-1:]
    out[...] = jnp.zeros_like(out)
    for q in range(5):
        h, l = fold(every[2 * q : 2 * q + 2])
        out[q : q + 1, :] = h[0:1]
        out[8 + q : 9 + q, :] = l[0:1]


def gram(vecs, image, found):
    return call(gram_kernel, shape(16, 2 * R), [VMEM] * 7)(*vecs, image, *found)


def solve(matrix, right):
    (a00, a01, a02), (a10, a11, a12), (a20, a21, a22) = matrix
    b0, b1, b2 = right
    inv0 = 1.0 / a00
    f1, f2 = a10 * inv0, a20 * inv0
    c11, c12, e1 = a11 - f1 * a01, a12 - f1 * a02, b1 - f1 * b0
    c21, c22, e2 = a21 - f2 * a01, a22 - f2 * a02, b2 - f2 * b0
    inv1 = 1.0 / c11
    g = c21 * inv1
    x2 = (e2 - g * e1) / (c22 - g * c12)
    x1 = (e1 - c12 * x2) * inv1
    x0 = (b0 - a01 * x1 - a02 * x2) * inv0
    return x0, x1, x2


def result_kernel(sums_ref, v0, v1, v2, y0, y1, y2, y3, sol, res):
    flat = []
    for q in range(5):
        h, l = sums_ref[q : q + 1, :], sums_ref[8 + q : 9 + q, :]
        flat += [(h, l), (pltpu.roll(h, R, 1), pltpu.roll(l, R, 1))]
    g00, g01, g11, g02, g12, g22, g03, g13, g23 = flat[:9]
    full = ((g00, g01, g02, g03), (g01, g11, g12, g13), (g02, g12, g22, g23))
    minus = lambda a, b: dd_add(a, (-b[0], -b[1]))
    matrix = [[minus(row[j], row[j + 1]) for j in range(3)] for row in full]
    right = [row[1] for row in full]
    near = [[m[0] + m[1] for m in row] for row in matrix]
    coef = [jnp.zeros_like(g00[0])] * 3
    for _ in range(3):
        left = []
        for row, value in zip(matrix, right):
            for m, c in zip(row, coef):
                p, e = two_prod(m[0], c)
                value = minus(value, (p, e + m[1] * c))
            left.append(value[0] + value[1])
        coef = [c + s for c, s in zip(coef, solve(near, left))]
    rows = jnp.concatenate([c[:, :N] for c in coef] + [jnp.zeros((N - 3, N), F32)], axis=0).T
    d0, d1, d2 = (jnp.broadcast_to(rows[:R, i : i + 1], (R, N)) for i in range(3))
    for t in range(T):
        sol[t] = v0[t] + (d0 * v0[t] + d1 * v1[t] + d2 * v2[t])
        first, second = y1[t], y2[t]
        res[t] = first - (d0 * (y0[t] - first) + d1 * (first - second) + d2 * (second - y3[t]))


def result(total, vecs, images):
    return call(result_kernel, (shape(T, R, N), shape(T, R, N)), [VMEM] * 8)(total, *vecs, *images)


def shift(value, steps):
    count = lax.axis_size("tm")
    return lax.ppermute(value, "tm", [(i, (i + steps) % count) for i in range(count)])


def pair_add(values):
    total = (values[0][:8], values[0][8:])
    for value in values[1:]:
        total = dd_add(total, (value[:8], value[8:]))
    return jnp.concatenate(total, axis=0)


def sum_all(value):
    count = lax.axis_size("tm")
    run = 4
    others = [
        lax.ppermute(value, "tm", [(i, i - i % run + (i + s) % run) for i in range(count)]) for s in range(1, run)
    ]
    value = pair_add([value] + others)
    groups = [[i for i in range(j, count, run)] for j in range(run)]
    size = count // run
    spread = lax.all_to_all(
        jnp.broadcast_to(value[None], (size,) + value.shape), "tm", 0, 0, axis_index_groups=groups
    )
    return pair_add([spread[i] for i in range(size)])


def shards(weights, pattern, shift_reg, rhs):
    rhs_next = shift(rhs, -1)
    high, low, own, ahead = sums(pattern, weights, shift_reg)
    arrived = shift(ahead, 1)
    own_next = shift(own, -1)
    diag, vec, out = start(rhs, own, arrived, high, low)
    arrived = shift(out, 1)
    vecs, images, found = [vec], [rhs], []
    partial, part = local(vecs, rhs, high, low)
    found.append(part)
    partial = finish_first(rhs_next, own_next, ahead, high, low, partial)
    for step in range(1, 3):
        image = partial + arrived
        vec = image / diag[:, None, :]
        vec_next = shift(vec, -1)
        out = contrib(vec, high, low)
        arrived = shift(out, 1)
        vecs.append(vec)
        images.append(image)
        partial, part = local(vecs, image, high, low)
        found.append(part)
        partial = finish(vec_next, high, low, partial)
    image = partial + arrived
    images.append(image)
    total = sum_all(gram(vecs, image, found))
    return result(total, vecs, images)


def solution(mesh):
    return jax.shard_map(
        shards,
        mesh=mesh,
        in_specs=(P("tm", None, None, None), P("tm", None), P("tm", None), P("tm", "scen", None)),
        out_specs=(P("tm", "scen", None), P("tm", "scen", None)),
        check_vma=False,
    )
```

```python
import functools

import jax
import jax.numpy as jnp
from jax import lax
from jax.experimental import pallas as pl
from jax.experimental.pallas import tpu as pltpu
from jax.sharding import PartitionSpec as P

F32 = jnp.float32
BF16 = jnp.bfloat16
MIB = 1024 * 1024
N = 128
T = 8
R = 64
VMEM = pl.BlockSpec(memory_space=pltpu.VMEM)
HBM = pl.BlockSpec(memory_space=pltpu.HBM)

BAND = (T // 2, 2 * N, (T + 1) * N)


def call(body, outs, specs=None, scratch=(), limit=16, flops=0, moved=0):
    return pl.pallas_call(
        body,
        out_shape=outs,
        in_specs=specs,
        out_specs=jax.tree.map(lambda _: VMEM, outs),
        scratch_shapes=list(scratch),
        compiler_params=pltpu.CompilerParams(vmem_limit_bytes=limit * MIB),
        cost_estimate=pl.CostEstimate(flops=flops, bytes_accessed=moved, transcendentals=0),
    )


def in_hbm(value):
    return pltpu.with_memory_space_constraint(value, pltpu.HBM)


def shape(*dims, dtype=F32):
    return jax.ShapeDtypeStruct(dims, dtype)


def dot(a, b):
    return lax.dot_general(a, b, (((1,), (0,)), ((), ())), preferred_element_type=F32)


def dot_t(a, b):
    return lax.dot_general(a, b, (((1,), (1,)), ((), ())), preferred_element_type=F32)


def two_sum(a, b):
    s = a + b
    t = s - a
    return s, (a - (s - t)) + (b - t)


def dd_add(a, b):
    s, e = two_sum(a[0], b[0])
    return s, e + (a[1] + b[1])


def halves(a):
    t = a * 4097.0
    h = t - (t - a)
    return h, a - h


def two_prod(a, b):
    p = a * b
    ah, al = halves(a)
    bh, bl = halves(b)
    return p, ((ah * bh - p) + ah * bl + al * bh) + al * bl


def ahead_kernel(pattern, weights, ahead, mask, buf, cols, sems):
    head = pltpu.make_async_copy(pattern, mask, sems.at[T])
    head.start()
    copies = []
    for t in range(T):
        some = slice(T - 1 - t, T)
        copies.append(pltpu.make_async_copy(weights.at[t, some], buf.at[t, some], sems.at[t]))
    for copy in copies:
        copy.start()
    cols[...] = jnp.zeros_like(cols)
    head.wait()
    for t in range(T):
        copies[t].wait()

        def step(k, carry):
            m = buf[t, k] * mask[t, k].astype(F32)
            cols[t + k + 1 - T] += jnp.sum(m.reshape(N // 8, 8, N), axis=0)
            return carry

        lax.fori_loop(T - 1 - t, T, step, 0)
    ahead[...] = jnp.sum(cols[...], axis=1)


def ahead_sums(pattern, weights):
    pattern, weights = in_hbm(pattern), in_hbm(weights)
    return call(
        ahead_kernel,
        shape(T, N),
        [HBM, HBM],
        [
            pltpu.SMEM((T, T), jnp.int32),
            pltpu.VMEM((T, T, N, N), F32),
            pltpu.VMEM((T, 8, N), F32),
            pltpu.SemaphoreType.DMA((T + 1,)),
        ],
        flops=4 * T * T * N * N,
        moved=4 * T * T * N * N,
    )(pattern, weights)


def band_kernel(pattern, weights, reg, high, low, own, mask, buf, cols, extra, sems):
    def copy(t):
        return pltpu.make_async_copy(weights.at[t], buf.at[t], sems.at[t])

    head = pltpu.make_async_copy(pattern, mask, sems.at[T])
    tail = pltpu.make_async_copy(reg, extra, sems.at[T + 1])
    head.start()
    for t in range(T):
        copy(t).start()
    tail.start()
    cols[...] = jnp.zeros_like(cols)
    zero = jnp.zeros((N, N), BF16)
    for a in range(T // 2):
        for piece in (high, low):
            piece[a, N : 2 * N, 0:N] = zero
            piece[a, 0:N, T * N : (T + 1) * N] = zero
    head.wait()

    def step(a, carry):
        for half in range(2):
            t = 2 * a + half
            copy(t).wait()
            rows = jnp.zeros((N, N), F32)
            for k in range(T):
                m = buf[t, k] * mask[t, k].astype(F32)
                rows = rows + m
                cols[t + k + 1] += jnp.sum(m.reshape(N // 8, 8, N), axis=0)
                h = m.astype(BF16)
                place = slice((k + half) * N, (k + half + 1) * N)
                high[a, half * N : (half + 1) * N, place] = h
                low[a, half * N : (half + 1) * N, place] = (m - h.astype(F32)).astype(BF16)
            own[pl.ds(t, 1), :] = jnp.sum(rows.T, axis=0, keepdims=True)
        return carry

    lax.fori_loop(0, T // 2, step, 0)
    tail.wait()
    own[...] += jnp.sum(cols[:T], axis=1) + extra[...]


def band_pieces(pattern, weights, reg):
    pattern, weights, reg = in_hbm(pattern), in_hbm(weights), in_hbm(reg)
    return call(
        band_kernel,
        (shape(*BAND, dtype=BF16), shape(*BAND, dtype=BF16), shape(T, N)),
        [HBM, HBM, HBM],
        [
            pltpu.SMEM((T, T), jnp.int32),
            pltpu.VMEM((T, T, N, N), F32),
            pltpu.VMEM((2 * T, 8, N), F32),
            pltpu.VMEM((T, N), F32),
            pltpu.SemaphoreType.DMA((T + 2,)),
        ],
        flops=2048 * T * T * N * N,
        moved=8 * T * T * N * N,
    )(pattern, weights, reg)


def put_pieces(pieces, t, value):
    h = value.astype(BF16)
    pieces[0:R, t * N : (t + 1) * N] = h
    pieces[R : 2 * R, t * N : (t + 1) * N] = (value - h.astype(F32)).astype(BF16)


def product(pieces, cols, high, low, mult):
    both = mult(pieces[:, cols], high)
    return (both[:R] + mult(pieces[0:R, cols], low)) + both[R:]


def to_next(pieces, high, low, out):
    for b in range(T // 2):
        total = None
        for a in range(b, T // 2):
            at = slice((7 + 2 * b - 2 * a) * N, (9 + 2 * b - 2 * a) * N)
            term = product(pieces, slice(a * 2 * N, (a + 1) * 2 * N), high[a, :, at], low[a, :, at], dot)
            total = term if total is None else total + term
        out[2 * b] = total[:, :N]
        out[2 * b + 1] = total[:, N:]


def within(pieces, high, low, out):
    out[0] = jnp.zeros((R, N), F32)
    for p in range(T // 2):
        total = None
        width = 2 * N if p < T // 2 - 1 else N
        for a in range(p + 1):
            at = slice(2 * (p - a) * N, 2 * (p - a) * N + width)
            term = product(pieces, slice(a * 2 * N, (a + 1) * 2 * N), high[a, :, at], low[a, :, at], dot)
            total = term if total is None else total + term
        out[2 * p + 1] = total[:, :N]
        if width > N:
            out[2 * p + 2] = total[:, N:]
    for a in range(T // 2):
        at = slice(0, (7 - 2 * a) * N)
        term = product(pieces, slice((2 * a + 1) * N, T * N), high[a, :, at], low[a, :, at], dot_t)
        out[2 * a] += term[:, :N]
        out[2 * a + 1] += term[:, N:]


def from_next(pieces, high, low, out):
    for a in range(T // 2):
        at = slice((7 - 2 * a) * N, (T + 1) * N)
        term = product(pieces, slice(0, (2 * a + 2) * N), high[a, :, at], low[a, :, at], dot_t)
        out[2 * a] += term[:, :N]
        out[2 * a + 1] += term[:, N:]


def moments(first, second):
    high = low = jnp.zeros((R, N), F32)
    for t in range(T):
        high, err = two_sum(high, first[t] * second[t])
        low = low + err
    return high, low


PIECES = pltpu.VMEM((2 * R, T * N), BF16)
ONE_WAY = 2 * 3 * 40 * R * N * N


def contrib_kernel(vec, high, low, out, pieces):
    for t in range(T):
        put_pieces(pieces, t, vec[t])
    to_next(pieces, high, low, out)


def contrib(vec, high, low):
    return call(contrib_kernel, shape(T, R, N), [VMEM] * 3, [PIECES], flops=ONE_WAY)(vec, high, low)


def local_kernel(count, *refs):
    vecs, (image, high, low, out, found, pieces) = refs[:count], refs[count:]
    for t in range(T):
        put_pieces(pieces, t, vecs[-1][t])
    within(pieces, high, low, out)
    for i, vec in enumerate(vecs):
        h, l = moments(vec, image)
        found[i, 0] = h
        found[i, 1] = l


def local(vecs, image, high, low):
    return call(
        functools.partial(local_kernel, len(vecs)),
        (shape(T, R, N), shape(len(vecs), 2, R, N)),
        [VMEM] * (len(vecs) + 3),
        [PIECES],
        flops=2 * ONE_WAY,
    )(*vecs, image, high, low)


def finish_kernel(vec_next, high, low, partial, out, pieces):
    for t in range(T):
        put_pieces(pieces, t, vec_next[t])
    out[...] = partial[...]
    from_next(pieces, high, low, out)


def finish(vec_next, high, low, partial):
    return call(finish_kernel, shape(T, R, N), [VMEM] * 4, [PIECES], flops=ONE_WAY)(vec_next, high, low, partial)


def fold(found):
    high, low = (jnp.concatenate([f[i] for f in found], axis=0).T for i in range(2))
    value = (high[:N], low[:N])
    size = N
    while size > 8:
        size //= 2
        value = dd_add(tuple(v[:size] for v in value), tuple(v[size:] for v in value))
    for turn in (4, 2, 1):
        value = dd_add(value, tuple(pltpu.roll(v, turn, 0) for v in value))
    return value


def gram_kernel(v0, v1, v2, n0, n1, n2, sent, partial, high, low, m0, m1, m2, image, out, pieces):
    for t in range(T):
        put_pieces(pieces, t, n2[t])
    image[...] = partial[...]
    from_next(pieces, high, low, image)
    last = [
        dd_add(moments(v, image), moments(n, sent)) for v, n in ((v0, n0), (v1, n1), (v2, n2))
    ]
    every = [(m[i, 0], m[i, 1]) for m in (m0, m1, m2) for i in range(m.shape[0])] + last + last[-1:]
    out[...] = jnp.zeros_like(out)
    for q in range(5):
        h, l = fold(every[2 * q : 2 * q + 2])
        out[q : q + 1, :] = h[0:1]
        out[8 + q : 9 + q, :] = l[0:1]


def gram(vecs, ahead, sent, partial, high, low, found):
    return call(gram_kernel, (shape(T, R, N), shape(16, 2 * R)), [VMEM] * 13, [PIECES], flops=ONE_WAY)(
        *vecs, *ahead, sent, partial, high, low, *found
    )


def solve(matrix, right):
    (a00, a01, a02), (a10, a11, a12), (a20, a21, a22) = matrix
    b0, b1, b2 = right
    inv0 = 1.0 / a00
    f1, f2 = a10 * inv0, a20 * inv0
    c11, c12, e1 = a11 - f1 * a01, a12 - f1 * a02, b1 - f1 * b0
    c21, c22, e2 = a21 - f2 * a01, a22 - f2 * a02, b2 - f2 * b0
    inv1 = 1.0 / c11
    g = c21 * inv1
    x2 = (e2 - g * e1) / (c22 - g * c12)
    x1 = (e1 - c12 * x2) * inv1
    x0 = (b0 - a01 * x1 - a02 * x2) * inv0
    return x0, x1, x2


def result_kernel(sums_ref, v0, v1, v2, y0, y1, y2, y3, arrived, sol, res):
    flat = []
    for q in range(5):
        h, l = sums_ref[q : q + 1, :], sums_ref[8 + q : 9 + q, :]
        flat += [(h, l), (pltpu.roll(h, R, 1), pltpu.roll(l, R, 1))]
    g00, g01, g11, g02, g12, g22, g03, g13, g23 = flat[:9]
    full = ((g00, g01, g02, g03), (g01, g11, g12, g13), (g02, g12, g22, g23))
    minus = lambda a, b: dd_add(a, (-b[0], -b[1]))
    matrix = [[minus(row[j], row[j + 1]) for j in range(3)] for row in full]
    right = [row[1] for row in full]
    near = [[m[0] + m[1] for m in row] for row in matrix]
    coef = [jnp.zeros_like(g00[0])] * 3
    for _ in range(3):
        left = []
        for row, value in zip(matrix, right):
            for m, c in zip(row, coef):
                p, e = two_prod(m[0], c)
                value = minus(value, (p, e + m[1] * c))
            left.append(value[0] + value[1])
        coef = [c + s for c, s in zip(coef, solve(near, left))]
    rows = jnp.concatenate([c[:, :N] for c in coef] + [jnp.zeros((N - 3, N), F32)], axis=0).T
    d0, d1, d2 = (jnp.broadcast_to(rows[:R, i : i + 1], (R, N)) for i in range(3))
    for t in range(T):
        sol[t] = v0[t] + (d0 * v0[t] + d1 * v1[t] + d2 * v2[t])
        first, second = y1[t], y2[t]
        res[t] = first - (d0 * (y0[t] - first) + d1 * (first - second) + d2 * (second - (y3[t] + arrived[t])))


def result(total, vecs, images, arrived):
    return call(result_kernel, (shape(T, R, N), shape(T, R, N)), [VMEM] * 9)(total, *vecs, *images, arrived)


def shift(value, steps):
    count = lax.axis_size("tm")
    return lax.ppermute(value, "tm", [(i, (i + steps) % count) for i in range(count)])


def pair_add(values):
    total = (values[0][:8], values[0][8:])
    for value in values[1:]:
        total = dd_add(total, (value[:8], value[8:]))
    return jnp.concatenate(total, axis=0)


def sum_all(value, beside):
    count = lax.axis_size("tm")
    run = 4
    others = [
        lax.ppermute(value, "tm", [(i, i - i % run + (i + s) % run) for i in range(count)]) for s in range(1, run)
    ]
    value, beside = lax.optimization_barrier((pair_add([value] + others), beside))
    groups = [[i for i in range(j, count, run)] for j in range(run)]
    size = count // run
    spread = lax.all_to_all(
        jnp.broadcast_to(value[None], (size,) + value.shape), "tm", 0, 0, axis_index_groups=groups
    )
    return pair_add([spread[i] for i in range(size)]), beside


def shards(weights, pattern, shift_reg, rhs):
    inflow = shift(ahead_sums(pattern, weights), 1)
    high, low, own = band_pieces(pattern, weights, shift_reg)
    diag = own + inflow
    vec = rhs / diag[:, None, :]
    vecs, images, found, ahead = [vec], [rhs], [], []
    for step in range(3):
        ahead.append(shift(vec, -1))
        sent = contrib(vec, high, low)
        arrived = shift(sent, 1)
        partial, part = local(vecs, images[-1], high, low)
        found.append(part)
        if step < 2:
            images.append(finish(ahead[-1], high, low, partial) + arrived)
            vec = images[-1] / diag[:, None, :]
            vecs.append(vec)
    image, total = gram(vecs, ahead, sent, partial, high, low, found)
    total, arrived = sum_all(total, arrived)
    return result(total, vecs, images + [image], arrived)


def solution(mesh):
    return jax.shard_map(
        shards,
        mesh=mesh,
        in_specs=(P("tm", None, None, None), P("tm", None), P("tm", None), P("tm", "scen", None)),
        out_specs=(P("tm", "scen", None), P("tm", "scen", None)),
        check_vma=False,
    )
```

```python
import functools

import jax
import jax.numpy as jnp
from jax import lax
from jax.experimental import pallas as pl
from jax.experimental.pallas import tpu as pltpu
from jax.sharding import PartitionSpec as P

F32 = jnp.float32
BF16 = jnp.bfloat16
MIB = 1024 * 1024
N = 128
T = 8
R = 64
VMEM = pl.BlockSpec(memory_space=pltpu.VMEM)
HBM = pl.BlockSpec(memory_space=pltpu.HBM)

BAND = (T // 2, 2 * N, (T + 1) * N)


def call(body, outs, specs=None, scratch=(), limit=16, flops=0, moved=0):
    return pl.pallas_call(
        body,
        out_shape=outs,
        in_specs=specs,
        out_specs=jax.tree.map(lambda _: VMEM, outs),
        scratch_shapes=list(scratch),
        compiler_params=pltpu.CompilerParams(vmem_limit_bytes=limit * MIB),
        cost_estimate=pl.CostEstimate(flops=flops, bytes_accessed=moved, transcendentals=0),
    )


def in_hbm(value):
    return pltpu.with_memory_space_constraint(value, pltpu.HBM)


def shape(*dims, dtype=F32):
    return jax.ShapeDtypeStruct(dims, dtype)


def dot(a, b):
    return lax.dot_general(a, b, (((1,), (0,)), ((), ())), preferred_element_type=F32)


def dot_t(a, b):
    return lax.dot_general(a, b, (((1,), (1,)), ((), ())), preferred_element_type=F32)


def two_sum(a, b):
    s = a + b
    t = s - a
    return s, (a - (s - t)) + (b - t)


def dd_add(a, b):
    s, e = two_sum(a[0], b[0])
    return s, e + (a[1] + b[1])


def halves(a):
    t = a * 4097.0
    h = t - (t - a)
    return h, a - h


def two_prod(a, b):
    p = a * b
    ah, al = halves(a)
    bh, bl = halves(b)
    return p, ((ah * bh - p) + ah * bl + al * bh) + al * bl


def ahead_kernel(pattern, weights, ahead, mask, buf, cols, sems):
    head = pltpu.make_async_copy(pattern, mask, sems.at[T])
    head.start()
    copies = []
    for t in range(T):
        some = slice(T - 1 - t, T)
        copies.append(pltpu.make_async_copy(weights.at[t, some], buf.at[t, some], sems.at[t]))
    for copy in copies:
        copy.start()
    cols[...] = jnp.zeros_like(cols)
    head.wait()
    for t in range(T):
        copies[t].wait()

        def step(k, carry):
            m = buf[t, k] * mask[t, k].astype(F32)
            cols[t + k + 1 - T] += jnp.sum(m.reshape(N // 8, 8, N), axis=0)
            return carry

        lax.fori_loop(T - 1 - t, T, step, 0)
    ahead[...] = jnp.sum(cols[...], axis=1)


def ahead_sums(pattern, weights):
    pattern, weights = in_hbm(pattern), in_hbm(weights)
    return call(
        ahead_kernel,
        shape(T, N),
        [HBM, HBM],
        [
            pltpu.SMEM((T, T), jnp.int32),
            pltpu.VMEM((T, T, N, N), F32),
            pltpu.VMEM((T, 8, N), F32),
            pltpu.SemaphoreType.DMA((T + 1,)),
        ],
        flops=4 * T * T * N * N,
        moved=4 * T * T * N * N,
    )(pattern, weights)


def band_kernel(pattern, weights, reg, high, low, own, mask, buf, cols, extra, sems):
    def copy(t):
        return pltpu.make_async_copy(weights.at[t], buf.at[t], sems.at[t])

    head = pltpu.make_async_copy(pattern, mask, sems.at[T])
    tail = pltpu.make_async_copy(reg, extra, sems.at[T + 1])
    head.start()
    for t in range(T):
        copy(t).start()
    tail.start()
    cols[...] = jnp.zeros_like(cols)
    zero = jnp.zeros((N, N), BF16)
    for a in range(T // 2):
        for piece in (high, low):
            piece[a, N : 2 * N, 0:N] = zero
            piece[a, 0:N, T * N : (T + 1) * N] = zero
    head.wait()

    def step(a, carry):
        for half in range(2):
            t = 2 * a + half
            copy(t).wait()
            rows = jnp.zeros((N, N), F32)
            for k in range(T):
                m = buf[t, k] * mask[t, k].astype(F32)
                rows = rows + m
                cols[t + k + 1] += jnp.sum(m.reshape(N // 8, 8, N), axis=0)
                h = m.astype(BF16)
                place = slice((k + half) * N, (k + half + 1) * N)
                high[a, half * N : (half + 1) * N, place] = h
                low[a, half * N : (half + 1) * N, place] = (m - h.astype(F32)).astype(BF16)
            own[pl.ds(t, 1), :] = jnp.sum(rows.T, axis=0, keepdims=True)
        return carry

    lax.fori_loop(0, T // 2, step, 0)
    tail.wait()
    own[...] += jnp.sum(cols[:T], axis=1) + extra[...]


def band_pieces(pattern, weights, reg):
    pattern, weights, reg = in_hbm(pattern), in_hbm(weights), in_hbm(reg)
    return call(
        band_kernel,
        (shape(*BAND, dtype=BF16), shape(*BAND, dtype=BF16), shape(T, N)),
        [HBM, HBM, HBM],
        [
            pltpu.SMEM((T, T), jnp.int32),
            pltpu.VMEM((T, T, N, N), F32),
            pltpu.VMEM((2 * T, 8, N), F32),
            pltpu.VMEM((T, N), F32),
            pltpu.SemaphoreType.DMA((T + 2,)),
        ],
        flops=2048 * T * T * N * N,
        moved=8 * T * T * N * N,
    )(pattern, weights, reg)


def put_pieces(pieces, t, value):
    h = value.astype(BF16)
    pieces[0:R, t * N : (t + 1) * N] = h
    pieces[R : 2 * R, t * N : (t + 1) * N] = (value - h.astype(F32)).astype(BF16)


def product(pieces, cols, high, low, mult):
    both = mult(pieces[:, cols], high)
    return (both[:R] + mult(pieces[0:R, cols], low)) + both[R:]


def to_next(pieces, high, low, out):
    for b in range(T // 2):
        total = None
        for a in range(b, T // 2):
            at = slice((7 + 2 * b - 2 * a) * N, (9 + 2 * b - 2 * a) * N)
            term = product(pieces, slice(a * 2 * N, (a + 1) * 2 * N), high[a, :, at], low[a, :, at], dot)
            total = term if total is None else total + term
        out[2 * b] = total[:, :N]
        out[2 * b + 1] = total[:, N:]


def within(pieces, high, low, out):
    out[0] = jnp.zeros((R, N), F32)
    for p in range(T // 2):
        total = None
        width = 2 * N if p < T // 2 - 1 else N
        for a in range(p + 1):
            at = slice(2 * (p - a) * N, 2 * (p - a) * N + width)
            term = product(pieces, slice(a * 2 * N, (a + 1) * 2 * N), high[a, :, at], low[a, :, at], dot)
            total = term if total is None else total + term
        out[2 * p + 1] = total[:, :N]
        if width > N:
            out[2 * p + 2] = total[:, N:]
    for a in range(T // 2):
        at = slice(0, (7 - 2 * a) * N)
        term = product(pieces, slice((2 * a + 1) * N, T * N), high[a, :, at], low[a, :, at], dot_t)
        out[2 * a] += term[:, :N]
        out[2 * a + 1] += term[:, N:]


def from_next(pieces, high, low, out):
    for a in range(T // 2):
        at = slice((7 - 2 * a) * N, (T + 1) * N)
        term = product(pieces, slice(0, (2 * a + 2) * N), high[a, :, at], low[a, :, at], dot_t)
        out[2 * a] += term[:, :N]
        out[2 * a + 1] += term[:, N:]


def moments(first, second):
    high = low = jnp.zeros((R, N), F32)
    for t in range(T):
        high, err = two_sum(high, first[t] * second[t])
        low = low + err
    return high, low


PIECES = pltpu.VMEM((2 * R, T * N), BF16)
ONE_WAY = 2 * 3 * 40 * R * N * N


def contrib_kernel(vec, high, low, out, pieces):
    for t in range(T):
        put_pieces(pieces, t, vec[t])
    to_next(pieces, high, low, out)


def contrib(vec, high, low):
    return call(contrib_kernel, shape(T, R, N), [VMEM] * 3, [PIECES], flops=ONE_WAY)(vec, high, low)


def local_kernel(count, *refs):
    vecs, (image, high, low, out, found, pieces) = refs[:count], refs[count:]
    for t in range(T):
        put_pieces(pieces, t, vecs[-1][t])
    within(pieces, high, low, out)
    for i, vec in enumerate(vecs):
        h, l = moments(vec, image)
        found[i, 0] = h
        found[i, 1] = l


def local(vecs, image, high, low):
    return call(
        functools.partial(local_kernel, len(vecs)),
        (shape(T, R, N), shape(len(vecs), 2, R, N)),
        [VMEM] * (len(vecs) + 3),
        [PIECES],
        flops=2 * ONE_WAY,
    )(*vecs, image, high, low)


def finish_kernel(vec_next, high, low, partial, out, pieces):
    for t in range(T):
        put_pieces(pieces, t, vec_next[t])
    out[...] = partial[...]
    from_next(pieces, high, low, out)


def finish(vec_next, high, low, partial):
    return call(finish_kernel, shape(T, R, N), [VMEM] * 4, [PIECES], flops=ONE_WAY)(vec_next, high, low, partial)


def fold(found):
    high, low = (jnp.concatenate([f[i] for f in found], axis=0).T for i in range(2))
    value = (high[:N], low[:N])
    size = N
    while size > 8:
        size //= 2
        value = dd_add(tuple(v[:size] for v in value), tuple(v[size:] for v in value))
    for turn in (4, 2, 1):
        value = dd_add(value, tuple(pltpu.roll(v, turn, 0) for v in value))
    return value


def gram_kernel(v0, v1, v2, ahead, arrived, partial, high, low, m0, m1, m2, image, out, pieces):
    for t in range(T):
        put_pieces(pieces, t, ahead[t])
        image[t] = partial[t] + arrived[t]
    from_next(pieces, high, low, image)
    last = [moments(v, image) for v in (v0, v1, v2)]
    every = [(m[i, 0], m[i, 1]) for m in (m0, m1, m2) for i in range(m.shape[0])] + last + last[-1:]
    out[...] = jnp.zeros_like(out)
    for q in range(5):
        h, l = fold(every[2 * q : 2 * q + 2])
        out[q : q + 1, :] = h[0:1]
        out[8 + q : 9 + q, :] = l[0:1]


def gram(vecs, ahead, arrived, partial, high, low, found):
    return call(gram_kernel, (shape(T, R, N), shape(16, 2 * R)), [VMEM] * 11, [PIECES], flops=ONE_WAY)(
        *vecs, ahead, arrived, partial, high, low, *found
    )


def solve(matrix, right):
    (a00, a01, a02), (a10, a11, a12), (a20, a21, a22) = matrix
    b0, b1, b2 = right
    inv0 = 1.0 / a00
    f1, f2 = a10 * inv0, a20 * inv0
    c11, c12, e1 = a11 - f1 * a01, a12 - f1 * a02, b1 - f1 * b0
    c21, c22, e2 = a21 - f2 * a01, a22 - f2 * a02, b2 - f2 * b0
    inv1 = 1.0 / c11
    g = c21 * inv1
    x2 = (e2 - g * e1) / (c22 - g * c12)
    x1 = (e1 - c12 * x2) * inv1
    x0 = (b0 - a01 * x1 - a02 * x2) * inv0
    return x0, x1, x2


def result_kernel(sums_ref, v0, v1, v2, y0, y1, y2, y3, sol, res):
    flat = []
    for q in range(5):
        h, l = sums_ref[q : q + 1, :], sums_ref[8 + q : 9 + q, :]
        flat += [(h, l), (pltpu.roll(h, R, 1), pltpu.roll(l, R, 1))]
    g00, g01, g11, g02, g12, g22, g03, g13, g23 = flat[:9]
    full = ((g00, g01, g02, g03), (g01, g11, g12, g13), (g02, g12, g22, g23))
    minus = lambda a, b: dd_add(a, (-b[0], -b[1]))
    matrix = [[minus(row[j], row[j + 1]) for j in range(3)] for row in full]
    right = [row[1] for row in full]
    near = [[m[0] + m[1] for m in row] for row in matrix]
    coef = [jnp.zeros_like(g00[0])] * 3
    for _ in range(3):
        left = []
        for row, value in zip(matrix, right):
            for m, c in zip(row, coef):
                p, e = two_prod(m[0], c)
                value = minus(value, (p, e + m[1] * c))
            left.append(value[0] + value[1])
        coef = [c + s for c, s in zip(coef, solve(near, left))]
    rows = jnp.concatenate([c[:, :N] for c in coef] + [jnp.zeros((N - 3, N), F32)], axis=0).T
    d0, d1, d2 = (jnp.broadcast_to(rows[:R, i : i + 1], (R, N)) for i in range(3))
    for t in range(T):
        sol[t] = v0[t] + (d0 * v0[t] + d1 * v1[t] + d2 * v2[t])
        first, second = y1[t], y2[t]
        res[t] = first - (d0 * (y0[t] - first) + d1 * (first - second) + d2 * (second - y3[t]))


def result(total, vecs, images):
    return call(result_kernel, (shape(T, R, N), shape(T, R, N)), [VMEM] * 8)(total, *vecs, *images)


def shift(value, steps):
    count = lax.axis_size("tm")
    return lax.ppermute(value, "tm", [(i, (i + steps) % count) for i in range(count)])


def pair_add(values):
    total = (values[0][:8], values[0][8:])
    for value in values[1:]:
        total = dd_add(total, (value[:8], value[8:]))
    return jnp.concatenate(total, axis=0)


def sum_all(value):
    count = lax.axis_size("tm")
    run = 4
    others = [
        lax.ppermute(value, "tm", [(i, i - i % run + (i + s) % run) for i in range(count)]) for s in range(1, run)
    ]
    value = pair_add([value] + others)
    groups = [[i for i in range(j, count, run)] for j in range(run)]
    size = count // run
    spread = lax.all_to_all(
        jnp.broadcast_to(value[None], (size,) + value.shape), "tm", 0, 0, axis_index_groups=groups
    )
    return pair_add([spread[i] for i in range(size)])


def exchange(vec, sent):
    count = lax.axis_size("tm")
    even = lax.axis_index("tm") % 2 == 0
    one = lax.ppermute(jnp.where(even, sent, vec), "tm", [(i, i ^ 1) for i in range(count)])
    two = lax.ppermute(
        jnp.where(even, vec, sent), "tm", [(i, (i + (1 if i % 2 else -1)) % count) for i in range(count)]
    )
    return jnp.where(even, one, two), jnp.where(even, two, one)


def shards(weights, pattern, shift_reg, rhs):
    inflow = shift(ahead_sums(pattern, weights), 1)
    high, low, own = band_pieces(pattern, weights, shift_reg)
    diag = own + inflow
    vecs, images, found = [rhs / diag[:, None, :]], [rhs], []
    for step in range(3):
        vec = vecs[-1]
        ahead, arrived = exchange(vec, contrib(vec, high, low))
        partial, part = local(vecs, images[-1], high, low)
        found.append(part)
        if step < 2:
            images.append(finish(ahead, high, low, partial) + arrived)
            vecs.append(images[-1] / diag[:, None, :])
    image, total = gram(vecs, ahead, arrived, partial, high, low, found)
    return result(sum_all(total), vecs, images + [image])


def solution(mesh):
    return jax.shard_map(
        shards,
        mesh=mesh,
        in_specs=(P("tm", None, None, None), P("tm", None), P("tm", None), P("tm", "scen", None)),
        out_specs=(P("tm", "scen", None), P("tm", "scen", None)),
        check_vma=False,
    )
```

```python
import functools

import jax
import jax.numpy as jnp
from jax import lax
from jax.experimental import pallas as pl
from jax.experimental.pallas import tpu as pltpu
from jax.sharding import PartitionSpec as P

F32 = jnp.float32
BF16 = jnp.bfloat16
MIB = 1024 * 1024
N = 128
T = 8
R = 64
VMEM = pl.BlockSpec(memory_space=pltpu.VMEM)
HBM = pl.BlockSpec(memory_space=pltpu.HBM)

BAND = (T // 2, 2 * N, (T + 1) * N)


def call(body, outs, specs=None, scratch=(), limit=16, flops=0, moved=0):
    return pl.pallas_call(
        body,
        out_shape=outs,
        in_specs=specs,
        out_specs=jax.tree.map(lambda _: VMEM, outs),
        scratch_shapes=list(scratch),
        compiler_params=pltpu.CompilerParams(vmem_limit_bytes=limit * MIB),
        cost_estimate=pl.CostEstimate(flops=flops, bytes_accessed=moved, transcendentals=0),
    )


def in_hbm(value):
    return pltpu.with_memory_space_constraint(value, pltpu.HBM)


def shape(*dims, dtype=F32):
    return jax.ShapeDtypeStruct(dims, dtype)


def dot(a, b):
    return lax.dot_general(a, b, (((1,), (0,)), ((), ())), preferred_element_type=F32)


def dot_t(a, b):
    return lax.dot_general(a, b, (((1,), (1,)), ((), ())), preferred_element_type=F32)


def two_sum(a, b):
    s = a + b
    t = s - a
    return s, (a - (s - t)) + (b - t)


def dd_add(a, b):
    s, e = two_sum(a[0], b[0])
    return s, e + (a[1] + b[1])


def halves(a):
    t = a * 4097.0
    h = t - (t - a)
    return h, a - h


def two_prod(a, b):
    p = a * b
    ah, al = halves(a)
    bh, bl = halves(b)
    return p, ((ah * bh - p) + ah * bl + al * bh) + al * bl


def ahead_kernel(pattern, weights, ahead, mask, buf, cols, sems):
    head = pltpu.make_async_copy(pattern, mask, sems.at[T])
    head.start()
    copies = []
    for t in range(T):
        some = slice(T - 1 - t, T)
        copies.append(pltpu.make_async_copy(weights.at[t, some], buf.at[t, some], sems.at[t]))
    for copy in copies:
        copy.start()
    cols[...] = jnp.zeros_like(cols)
    head.wait()
    for t in range(T):
        copies[t].wait()

        def step(k, carry):
            m = buf[t, k] * mask[t, k].astype(F32)
            cols[t + k + 1 - T] += jnp.sum(m.reshape(N // 8, 8, N), axis=0)
            return carry

        lax.fori_loop(T - 1 - t, T, step, 0)
    ahead[...] = jnp.sum(cols[...], axis=1)


def ahead_sums(pattern, weights):
    pattern, weights = in_hbm(pattern), in_hbm(weights)
    return call(
        ahead_kernel,
        shape(T, N),
        [HBM, HBM],
        [
            pltpu.SMEM((T, T), jnp.int32),
            pltpu.VMEM((T, T, N, N), F32),
            pltpu.VMEM((T, 8, N), F32),
            pltpu.SemaphoreType.DMA((T + 1,)),
        ],
        flops=4 * T * T * N * N,
        moved=4 * T * T * N * N,
    )(pattern, weights)


def band_kernel(pattern, weights, reg, high, low, own, mask, buf, cols, extra, sems):
    def copy(t):
        return pltpu.make_async_copy(weights.at[t], buf.at[t], sems.at[t])

    head = pltpu.make_async_copy(pattern, mask, sems.at[T])
    tail = pltpu.make_async_copy(reg, extra, sems.at[T + 1])
    head.start()
    for t in range(T):
        copy(t).start()
    tail.start()
    cols[...] = jnp.zeros_like(cols)
    zero = jnp.zeros((N, N), BF16)
    for a in range(T // 2):
        for piece in (high, low):
            piece[a, N : 2 * N, 0:N] = zero
            piece[a, 0:N, T * N : (T + 1) * N] = zero
    head.wait()

    def step(a, carry):
        for half in range(2):
            t = 2 * a + half
            copy(t).wait()
            rows = jnp.zeros((N, N), F32)
            for k in range(T):
                m = buf[t, k] * mask[t, k].astype(F32)
                rows = rows + m
                cols[t + k + 1] += jnp.sum(m.reshape(N // 8, 8, N), axis=0)
                h = m.astype(BF16)
                place = slice((k + half) * N, (k + half + 1) * N)
                high[a, half * N : (half + 1) * N, place] = h
                low[a, half * N : (half + 1) * N, place] = (m - h.astype(F32)).astype(BF16)
            own[pl.ds(t, 1), :] = jnp.sum(rows.T, axis=0, keepdims=True)
        return carry

    lax.fori_loop(0, T // 2, step, 0)
    tail.wait()
    own[...] += jnp.sum(cols[:T], axis=1) + extra[...]


def band_pieces(pattern, weights, reg):
    pattern, weights, reg = in_hbm(pattern), in_hbm(weights), in_hbm(reg)
    return call(
        band_kernel,
        (shape(*BAND, dtype=BF16), shape(*BAND, dtype=BF16), shape(T, N)),
        [HBM, HBM, HBM],
        [
            pltpu.SMEM((T, T), jnp.int32),
            pltpu.VMEM((T, T, N, N), F32),
            pltpu.VMEM((2 * T, 8, N), F32),
            pltpu.VMEM((T, N), F32),
            pltpu.SemaphoreType.DMA((T + 2,)),
        ],
        flops=2048 * T * T * N * N,
        moved=8 * T * T * N * N,
    )(pattern, weights, reg)


def put_pieces(pieces, t, value):
    h = value.astype(BF16)
    pieces[0:R, t * N : (t + 1) * N] = h
    pieces[R : 2 * R, t * N : (t + 1) * N] = (value - h.astype(F32)).astype(BF16)


def product(pieces, cols, high, low, mult):
    both = mult(pieces[:, cols], high)
    return (both[:R] + mult(pieces[0:R, cols], low)) + both[R:]


def to_next(pieces, high, low, out):
    for b in range(T // 2):
        total = None
        for a in range(b, T // 2):
            at = slice((7 + 2 * b - 2 * a) * N, (9 + 2 * b - 2 * a) * N)
            term = product(pieces, slice(a * 2 * N, (a + 1) * 2 * N), high[a, :, at], low[a, :, at], dot)
            total = term if total is None else total + term
        out[2 * b] = total[:, :N]
        out[2 * b + 1] = total[:, N:]


def within(pieces, high, low, out):
    out[0] = jnp.zeros((R, N), F32)
    for p in range(T // 2):
        total = None
        width = 2 * N if p < T // 2 - 1 else N
        for a in range(p + 1):
            at = slice(2 * (p - a) * N, 2 * (p - a) * N + width)
            term = product(pieces, slice(a * 2 * N, (a + 1) * 2 * N), high[a, :, at], low[a, :, at], dot)
            total = term if total is None else total + term
        out[2 * p + 1] = total[:, :N]
        if width > N:
            out[2 * p + 2] = total[:, N:]
    for a in range(T // 2):
        at = slice(0, (7 - 2 * a) * N)
        term = product(pieces, slice((2 * a + 1) * N, T * N), high[a, :, at], low[a, :, at], dot_t)
        out[2 * a] += term[:, :N]
        out[2 * a + 1] += term[:, N:]


def turned_rows(a):
    return slice(a * (a + 1) * N, (a + 1) * (a + 2) * N)


def turn(high, low, turned_high, turned_low):
    for piece, out in ((high, turned_high), (low, turned_low)):
        for a in range(T // 2):
            out[turned_rows(a), :] = piece[a, :, (7 - 2 * a) * N :].T


def from_next(pieces, high, low, out):
    for a in range(T // 2):
        rows = turned_rows(a)
        term = product(pieces, slice(0, (2 * a + 2) * N), high[rows, :], low[rows, :], dot)
        out[2 * a] += term[:, :N]
        out[2 * a + 1] += term[:, N:]


def moments(first, second):
    high = low = jnp.zeros((R, N), F32)
    for t in range(T):
        high, err = two_sum(high, first[t] * second[t])
        low = low + err
    return high, low


PIECES = pltpu.VMEM((2 * R, T * N), BF16)
ONE_WAY = 2 * 3 * 40 * R * N * N


def choose(flag, first, second):
    return jnp.where(jnp.broadcast_to(flag[0:1, :], (R, N)) > 0, first, second)


def hand_out(flag, vec, high, low, one, two, sent, pieces):
    for t in range(T):
        put_pieces(pieces, t, vec[t])
    to_next(pieces, high, low, sent)
    for t in range(T):
        one[t] = choose(flag, sent[t], vec[t])
        two[t] = choose(flag, vec[t], sent[t])


BLOCKS = shape(T, R, N)
SENT = pltpu.VMEM((T, R, N), F32)
TURNED = shape((T // 2) * (T // 2 + 1) * N, 2 * N, dtype=BF16)


def first_kernel(flag, rhs, own, inflow, high, low, diag, vec, one, two, sent, pieces):
    diag[...] = own[...] + inflow[...]
    for t in range(T):
        vec[t] = rhs[t] / diag[t : t + 1, :]
    hand_out(flag, vec, high, low, one, two, sent, pieces)


def first(flag, rhs, own, inflow, high, low):
    return call(
        first_kernel,
        (shape(T, N), BLOCKS, BLOCKS, BLOCKS),
        [VMEM] * 6,
        [SENT, PIECES],
        flops=ONE_WAY,
    )(flag, rhs, own, inflow, high, low)


def local_kernel(count, *refs):
    vecs, (image, high, low, out, found, *turned, pieces) = refs[:count], refs[count:]
    if turned:
        turn(high, low, *turned)
    for t in range(T):
        put_pieces(pieces, t, vecs[-1][t])
    within(pieces, high, low, out)
    for i, vec in enumerate(vecs):
        h, l = moments(vec, image)
        found[i, 0] = h
        found[i, 1] = l


def local(vecs, image, high, low):
    turned = (TURNED, TURNED) if len(vecs) == 1 else ()
    return call(
        functools.partial(local_kernel, len(vecs)),
        (BLOCKS, shape(len(vecs), 2, R, N)) + turned,
        [VMEM] * (len(vecs) + 3),
        [PIECES],
        flops=2 * ONE_WAY,
    )(*vecs, image, high, low)


def add_received(flag, got_one, got_two, partial, turned_high, turned_low, image, pieces):
    for t in range(T):
        put_pieces(pieces, t, choose(flag, got_one[t], got_two[t]))
        image[t] = partial[t] + choose(flag, got_two[t], got_one[t])
    from_next(pieces, turned_high, turned_low, image)


def step_kernel(flag, got_one, got_two, partial, diag, high, low, turned_high, turned_low, image, vec, one, two, sent, pieces):
    add_received(flag, got_one, got_two, partial, turned_high, turned_low, image, pieces)
    for t in range(T):
        vec[t] = image[t] / diag[t : t + 1, :]
    hand_out(flag, vec, high, low, one, two, sent, pieces)


def next_step(*args):
    return call(step_kernel, (BLOCKS,) * 4, [VMEM] * 9, [SENT, PIECES], flops=2 * ONE_WAY)(*args)


def fold(found):
    high, low = (jnp.concatenate([f[i] for f in found], axis=0).T for i in range(2))
    value = (high[:N], low[:N])
    size = N
    while size > 8:
        size //= 2
        value = dd_add(tuple(v[:size] for v in value), tuple(v[size:] for v in value))
    for turn_by in (4, 2, 1):
        value = dd_add(value, tuple(pltpu.roll(v, turn_by, 0) for v in value))
    return value


def gram_kernel(
    flag, got_one, got_two, partial, turned_high, turned_low, v0, v1, v2, m0, m1, m2, image, out, pieces
):
    add_received(flag, got_one, got_two, partial, turned_high, turned_low, image, pieces)
    last = [moments(v, image) for v in (v0, v1, v2)]
    every = [(m[i, 0], m[i, 1]) for m in (m0, m1, m2) for i in range(m.shape[0])] + last + last[-1:]
    out[...] = jnp.zeros_like(out)
    for q in range(5):
        h, l = fold(every[2 * q : 2 * q + 2])
        out[q : q + 1, :] = h[0:1]
        out[8 + q : 9 + q, :] = l[0:1]


def gram(*args):
    return call(gram_kernel, (BLOCKS, shape(16, 2 * R)), [VMEM] * 12, [PIECES], flops=ONE_WAY)(*args)


def solve(matrix, right):
    (a00, a01, a02), (a10, a11, a12), (a20, a21, a22) = matrix
    b0, b1, b2 = right
    inv0 = 1.0 / a00
    f1, f2 = a10 * inv0, a20 * inv0
    c11, c12, e1 = a11 - f1 * a01, a12 - f1 * a02, b1 - f1 * b0
    c21, c22, e2 = a21 - f2 * a01, a22 - f2 * a02, b2 - f2 * b0
    inv1 = 1.0 / c11
    g = c21 * inv1
    x2 = (e2 - g * e1) / (c22 - g * c12)
    x1 = (e1 - c12 * x2) * inv1
    x0 = (b0 - a01 * x1 - a02 * x2) * inv0
    return x0, x1, x2


def result_kernel(sums_ref, v0, v1, v2, y0, y1, y2, y3, sol, res):
    flat = []
    for q in range(5):
        h, l = sums_ref[q : q + 1, :], sums_ref[8 + q : 9 + q, :]
        flat += [(h, l), (pltpu.roll(h, R, 1), pltpu.roll(l, R, 1))]
    g00, g01, g11, g02, g12, g22, g03, g13, g23 = flat[:9]
    full = ((g00, g01, g02, g03), (g01, g11, g12, g13), (g02, g12, g22, g23))
    minus = lambda a, b: dd_add(a, (-b[0], -b[1]))
    matrix = [[minus(row[j], row[j + 1]) for j in range(3)] for row in full]
    right = [row[1] for row in full]
    near = [[m[0] + m[1] for m in row] for row in matrix]
    coef = [jnp.zeros_like(g00[0])] * 3
    for _ in range(3):
        left = []
        for row, value in zip(matrix, right):
            for m, c in zip(row, coef):
                p, e = two_prod(m[0], c)
                value = minus(value, (p, e + m[1] * c))
            left.append(value[0] + value[1])
        coef = [c + s for c, s in zip(coef, solve(near, left))]
    rows = jnp.concatenate([c[:, :N] for c in coef] + [jnp.zeros((N - 3, N), F32)], axis=0).T
    d0, d1, d2 = (jnp.broadcast_to(rows[:R, i : i + 1], (R, N)) for i in range(3))
    for t in range(T):
        sol[t] = v0[t] + (d0 * v0[t] + d1 * v1[t] + d2 * v2[t])
        first, second = y1[t], y2[t]
        res[t] = first - (d0 * (y0[t] - first) + d1 * (first - second) + d2 * (second - y3[t]))


def result(total, vecs, images):
    return call(result_kernel, (shape(T, R, N), shape(T, R, N)), [VMEM] * 8)(total, *vecs, *images)


def shift(value, steps):
    count = lax.axis_size("tm")
    return lax.ppermute(value, "tm", [(i, (i + steps) % count) for i in range(count)])


def pair_add(values):
    total = (values[0][:8], values[0][8:])
    for value in values[1:]:
        total = dd_add(total, (value[:8], value[8:]))
    return jnp.concatenate(total, axis=0)


def sum_all(value):
    count = lax.axis_size("tm")
    run = 4
    others = [
        lax.ppermute(value, "tm", [(i, i - i % run + (i + s) % run) for i in range(count)]) for s in range(1, run)
    ]
    value = pair_add([value] + others)
    groups = [[i for i in range(j, count, run)] for j in range(run)]
    size = count // run
    spread = lax.all_to_all(
        jnp.broadcast_to(value[None], (size,) + value.shape), "tm", 0, 0, axis_index_groups=groups
    )
    return pair_add([spread[i] for i in range(size)])


def swaps(one, two):
    count = lax.axis_size("tm")
    one = lax.ppermute(one, "tm", [(i, i ^ 1) for i in range(count)])
    return one, lax.ppermute(two, "tm", [(i, (i + (1 if i % 2 else -1)) % count) for i in range(count)])


def shards(weights, pattern, shift_reg, rhs):
    flag = jnp.broadcast_to((1 - lax.axis_index("tm") % 2).astype(F32), (8, N))
    flag, pattern = lax.optimization_barrier((flag, pattern))
    inflow = shift(ahead_sums(pattern, weights), 1)
    high, low, own = band_pieces(pattern, weights, shift_reg)
    diag, vec, *leaving = first(flag, rhs, own, inflow, high, low)
    vecs, images, found = [vec], [rhs], []
    for step in range(3):
        got = swaps(*leaving)
        partial, part, *extra = local(vecs, images[-1], high, low)
        found.append(part)
        turned = extra or turned
        if step < 2:
            image, vec, *leaving = next_step(flag, *got, partial, diag, high, low, *turned)
            images.append(image)
            vecs.append(vec)
    image, total = gram(flag, *got, partial, *turned, *vecs, *found)
    return result(sum_all(total), vecs, images + [image])


def solution(mesh):
    return jax.shard_map(
        shards,
        mesh=mesh,
        in_specs=(P("tm", None, None, None), P("tm", None), P("tm", None), P("tm", "scen", None)),
        out_specs=(P("tm", "scen", None), P("tm", "scen", None)),
        check_vma=False,
    )
```

```python
import functools

import jax
import jax.numpy as jnp
from jax import lax
from jax.experimental import pallas as pl
from jax.experimental.pallas import tpu as pltpu
from jax.sharding import PartitionSpec as P

F32 = jnp.float32
BF16 = jnp.bfloat16
MIB = 1024 * 1024
N = 128
T = 8
R = 64
VMEM = pl.BlockSpec(memory_space=pltpu.VMEM)
HBM = pl.BlockSpec(memory_space=pltpu.HBM)

BAND = (T // 2, 2 * N, (T + 1) * N)


def call(body, outs, specs=None, scratch=(), limit=16, flops=0, moved=0):
    return pl.pallas_call(
        body,
        out_shape=outs,
        in_specs=specs,
        out_specs=jax.tree.map(lambda _: VMEM, outs),
        scratch_shapes=list(scratch),
        compiler_params=pltpu.CompilerParams(vmem_limit_bytes=limit * MIB),
        cost_estimate=pl.CostEstimate(flops=flops, bytes_accessed=moved, transcendentals=0),
    )


def in_hbm(value):
    return pltpu.with_memory_space_constraint(value, pltpu.HBM)


def shape(*dims, dtype=F32):
    return jax.ShapeDtypeStruct(dims, dtype)


def dot(a, b):
    return lax.dot_general(a, b, (((1,), (0,)), ((), ())), preferred_element_type=F32)


def dot_t(a, b):
    return lax.dot_general(a, b, (((1,), (1,)), ((), ())), preferred_element_type=F32)


def two_sum(a, b):
    s = a + b
    t = s - a
    return s, (a - (s - t)) + (b - t)


def dd_add(a, b):
    s, e = two_sum(a[0], b[0])
    return s, e + (a[1] + b[1])


def halves(a):
    t = a * 4097.0
    h = t - (t - a)
    return h, a - h


def two_prod(a, b):
    p = a * b
    ah, al = halves(a)
    bh, bl = halves(b)
    return p, ((ah * bh - p) + ah * bl + al * bh) + al * bl


def ahead_kernel(pattern, weights, ahead, mask, buf, cols, sems):
    head = pltpu.make_async_copy(pattern, mask, sems.at[T])
    head.start()
    copies = []
    for t in range(T):
        some = slice(T - 1 - t, T)
        copies.append(pltpu.make_async_copy(weights.at[t, some], buf.at[t, some], sems.at[t]))
    for copy in copies:
        copy.start()
    cols[...] = jnp.zeros_like(cols)
    head.wait()
    for t in range(T):
        copies[t].wait()

        def step(k, carry):
            m = buf[t, k] * mask[t, k].astype(F32)
            cols[t + k + 1 - T] += jnp.sum(m.reshape(N // 8, 8, N), axis=0)
            return carry

        lax.fori_loop(T - 1 - t, T, step, 0)
    ahead[...] = jnp.sum(cols[...], axis=1)


def ahead_sums(pattern, weights):
    pattern, weights = in_hbm(pattern), in_hbm(weights)
    return call(
        ahead_kernel,
        shape(T, N),
        [HBM, HBM],
        [
            pltpu.SMEM((T, T), jnp.int32),
            pltpu.VMEM((T, T, N, N), F32),
            pltpu.VMEM((T, 8, N), F32),
            pltpu.SemaphoreType.DMA((T + 1,)),
        ],
        flops=4 * T * T * N * N,
        moved=4 * T * T * N * N,
    )(pattern, weights)


def band_kernel(pattern, weights, reg, high, low, own, mask, buf, cols, extra, sems):
    def copy(t):
        return pltpu.make_async_copy(weights.at[t], buf.at[t], sems.at[t])

    head = pltpu.make_async_copy(pattern, mask, sems.at[T])
    tail = pltpu.make_async_copy(reg, extra, sems.at[T + 1])
    head.start()
    for t in range(T):
        copy(t).start()
    tail.start()
    cols[...] = jnp.zeros_like(cols)
    zero = jnp.zeros((N, N), BF16)
    for a in range(T // 2):
        for piece in (high, low):
            piece[a, N : 2 * N, 0:N] = zero
            piece[a, 0:N, T * N : (T + 1) * N] = zero
    head.wait()

    def step(a, carry):
        for half in range(2):
            t = 2 * a + half
            copy(t).wait()
            rows = jnp.zeros((N, N), F32)
            for k in range(T):
                m = buf[t, k] * mask[t, k].astype(F32)
                rows = rows + m
                cols[t + k + 1] += jnp.sum(m.reshape(N // 8, 8, N), axis=0)
                h = m.astype(BF16)
                place = slice((k + half) * N, (k + half + 1) * N)
                high[a, half * N : (half + 1) * N, place] = h
                low[a, half * N : (half + 1) * N, place] = (m - h.astype(F32)).astype(BF16)
            own[pl.ds(t, 1), :] = jnp.sum(rows.T, axis=0, keepdims=True)
        return carry

    lax.fori_loop(0, T // 2, step, 0)
    tail.wait()
    own[...] += jnp.sum(cols[:T], axis=1) + extra[...]


def band_pieces(pattern, weights, reg):
    pattern, weights, reg = in_hbm(pattern), in_hbm(weights), in_hbm(reg)
    return call(
        band_kernel,
        (shape(*BAND, dtype=BF16), shape(*BAND, dtype=BF16), shape(T, N)),
        [HBM, HBM, HBM],
        [
            pltpu.SMEM((T, T), jnp.int32),
            pltpu.VMEM((T, T, N, N), F32),
            pltpu.VMEM((2 * T, 8, N), F32),
            pltpu.VMEM((T, N), F32),
            pltpu.SemaphoreType.DMA((T + 2,)),
        ],
        flops=2048 * T * T * N * N,
        moved=8 * T * T * N * N,
    )(pattern, weights, reg)


def put_pieces(pieces, t, value):
    h = value.astype(BF16)
    pieces[0:R, t * N : (t + 1) * N] = h
    pieces[R : 2 * R, t * N : (t + 1) * N] = (value - h.astype(F32)).astype(BF16)


def product(pieces, cols, high, low, mult):
    both = mult(pieces[:, cols], high)
    return (both[:R] + mult(pieces[0:R, cols], low)) + both[R:]


def to_next(pieces, high, low, out):
    for b in range(T // 2):
        total = None
        for a in range(b, T // 2):
            at = slice((7 + 2 * b - 2 * a) * N, (9 + 2 * b - 2 * a) * N)
            term = product(pieces, slice(a * 2 * N, (a + 1) * 2 * N), high[a, :, at], low[a, :, at], dot)
            total = term if total is None else total + term
        out[2 * b] = total[:, :N]
        out[2 * b + 1] = total[:, N:]


def within(pieces, high, low, out):
    out[0] = jnp.zeros((R, N), F32)
    for p in range(T // 2):
        total = None
        width = 2 * N if p < T // 2 - 1 else N
        for a in range(p + 1):
            at = slice(2 * (p - a) * N, 2 * (p - a) * N + width)
            term = product(pieces, slice(a * 2 * N, (a + 1) * 2 * N), high[a, :, at], low[a, :, at], dot)
            total = term if total is None else total + term
        out[2 * p + 1] = total[:, :N]
        if width > N:
            out[2 * p + 2] = total[:, N:]
    for a in range(T // 2):
        at = slice(0, (7 - 2 * a) * N)
        term = product(pieces, slice((2 * a + 1) * N, T * N), high[a, :, at], low[a, :, at], dot_t)
        out[2 * a] += term[:, :N]
        out[2 * a + 1] += term[:, N:]


def turned_rows(a):
    return slice(a * (a + 1) * N, (a + 1) * (a + 2) * N)


def turn(high, low, turned_high, turned_low):
    for piece, out in ((high, turned_high), (low, turned_low)):
        for a in range(T // 2):
            out[turned_rows(a), :] = piece[a, :, (7 - 2 * a) * N :].T


def from_next(pieces, high, low, out):
    for a in range(T // 2):
        rows = turned_rows(a)
        term = product(pieces, slice(0, (2 * a + 2) * N), high[rows, :], low[rows, :], dot)
        out[2 * a] += term[:, :N]
        out[2 * a + 1] += term[:, N:]


def moments(first, second):
    high = low = jnp.zeros((R, N), F32)
    for t in range(T):
        high, err = two_sum(high, first[t] * second[t])
        low = low + err
    return high, low


PIECES = pltpu.VMEM((2 * R, T * N), BF16)
ONE_WAY = 2 * 3 * 40 * R * N * N


def choose(flag, first, second):
    return jnp.where(jnp.broadcast_to(flag[0:1, :], (R, N)) > 0, first, second)


def hand_out(flag, vec, high, low, one, two, sent, pieces):
    for t in range(T):
        put_pieces(pieces, t, vec[t])
    to_next(pieces, high, low, sent)
    for t in range(T):
        one[t] = choose(flag, sent[t], vec[t])
        two[t] = choose(flag, vec[t], sent[t])


BLOCKS = shape(T, R, N)
SENT = pltpu.VMEM((T, R, N), F32)
TURNED = shape((T // 2) * (T // 2 + 1) * N, 2 * N, dtype=BF16)


def first_kernel(flag, rhs, own, inflow, high, low, diag, vec, one, two, sent, pieces):
    diag[...] = own[...] + inflow[...]
    for t in range(T):
        vec[t] = rhs[t] / diag[t : t + 1, :]
    hand_out(flag, vec, high, low, one, two, sent, pieces)


def first(flag, rhs, own, inflow, high, low):
    return call(
        first_kernel,
        (shape(T, N), BLOCKS, BLOCKS, BLOCKS),
        [VMEM] * 6,
        [SENT, PIECES],
        flops=ONE_WAY,
    )(flag, rhs, own, inflow, high, low)


def local_kernel(count, *refs):
    vecs, (image, high, low, out, found, *turned, pieces) = refs[:count], refs[count:]
    if turned:
        turn(high, low, *turned)
    for t in range(T):
        put_pieces(pieces, t, vecs[-1][t])
    within(pieces, high, low, out)
    for i, vec in enumerate(vecs):
        h, l = moments(vec, image)
        found[i, 0] = h
        found[i, 1] = l


def local(vecs, image, high, low):
    turned = (TURNED, TURNED) if len(vecs) == 1 else ()
    return call(
        functools.partial(local_kernel, len(vecs)),
        (BLOCKS, shape(len(vecs), 2, R, N)) + turned,
        [VMEM] * (len(vecs) + 3),
        [PIECES],
        flops=2 * ONE_WAY,
    )(*vecs, image, high, low)


def add_received(flag, got_one, got_two, partial, turned_high, turned_low, image, pieces):
    for t in range(T):
        put_pieces(pieces, t, choose(flag, got_one[t], got_two[t]))
        image[t] = partial[t] + choose(flag, got_two[t], got_one[t])
    from_next(pieces, turned_high, turned_low, image)


def step_kernel(flag, got_one, got_two, partial, diag, high, low, turned_high, turned_low, image, vec, one, two, sent, pieces):
    add_received(flag, got_one, got_two, partial, turned_high, turned_low, image, pieces)
    for t in range(T):
        vec[t] = image[t] / diag[t : t + 1, :]
    hand_out(flag, vec, high, low, one, two, sent, pieces)


def next_step(*args):
    return call(step_kernel, (BLOCKS,) * 4, [VMEM] * 9, [SENT, PIECES], flops=2 * ONE_WAY)(*args)


PAIRS = 5


def fold(high, low):
    value = (high, low)
    size = high.shape[0]
    while size > 8:
        size //= 2
        value = dd_add(tuple(v[:size] for v in value), tuple(v[size:] for v in value))
    for turn_by in (4, 2, 1):
        value = dd_add(value, tuple(pltpu.roll(v, turn_by, 0) for v in value))
    return value


def gram_kernel(
    flag, got_one, got_two, partial, turned_high, turned_low, v0, v1, v2, m0, m1, m2, image, out, pieces
):
    add_received(flag, got_one, got_two, partial, turned_high, turned_low, image, pieces)
    last = [moments(v, image) for v in (v0, v1, v2)]
    every = [(m[i, 0], m[i, 1]) for m in (m0, m1, m2) for i in range(m.shape[0])] + last + last[-1:]
    for q in range(PAIRS):
        pair = every[2 * q : 2 * q + 2]
        h, l = fold(*(jnp.concatenate([f[i] for f in pair], axis=0).T for i in range(2)))
        out[:, q * N : (q + 1) * N] = (h + l)[0:1]


def gram(*args):
    return call(gram_kernel, (BLOCKS, shape(1, PAIRS * N)), [VMEM] * 12, [PIECES], flops=ONE_WAY)(*args)


def solve(matrix, right):
    (a00, a01, a02), (a10, a11, a12), (a20, a21, a22) = matrix
    b0, b1, b2 = right
    inv0 = 1.0 / a00
    f1, f2 = a10 * inv0, a20 * inv0
    c11, c12, e1 = a11 - f1 * a01, a12 - f1 * a02, b1 - f1 * b0
    c21, c22, e2 = a21 - f2 * a01, a22 - f2 * a02, b2 - f2 * b0
    inv1 = 1.0 / c11
    g = c21 * inv1
    x2 = (e2 - g * e1) / (c22 - g * c12)
    x1 = (e1 - c12 * x2) * inv1
    x0 = (b0 - a01 * x1 - a02 * x2) * inv0
    return x0, x1, x2


def result_kernel(parts, v0, v1, v2, y0, y1, y2, y3, sol, res):
    flat = []
    for q in range(PAIRS):
        part = parts[:, q * N : (q + 1) * N]
        h, l = (v[0:1] for v in fold(part, jnp.zeros_like(part)))
        flat += [(h, l), (pltpu.roll(h, R, 1), pltpu.roll(l, R, 1))]
    g00, g01, g11, g02, g12, g22, g03, g13, g23 = flat[:9]
    full = ((g00, g01, g02, g03), (g01, g11, g12, g13), (g02, g12, g22, g23))
    minus = lambda a, b: dd_add(a, (-b[0], -b[1]))
    matrix = [[minus(row[j], row[j + 1]) for j in range(3)] for row in full]
    right = [row[1] for row in full]
    near = [[m[0] + m[1] for m in row] for row in matrix]
    coef = [jnp.zeros_like(g00[0])] * 3
    for _ in range(3):
        left = []
        for row, value in zip(matrix, right):
            for m, c in zip(row, coef):
                p, e = two_prod(m[0], c)
                value = minus(value, (p, e + m[1] * c))
            left.append(value[0] + value[1])
        coef = [c + s for c, s in zip(coef, solve(near, left))]
    rows = jnp.concatenate([c[:, :N] for c in coef] + [jnp.zeros((N - 3, N), F32)], axis=0).T
    d0, d1, d2 = (jnp.broadcast_to(rows[:R, i : i + 1], (R, N)) for i in range(3))
    for t in range(T):
        sol[t] = v0[t] + (d0 * v0[t] + d1 * v1[t] + d2 * v2[t])
        first, second = y1[t], y2[t]
        res[t] = first - (d0 * (y0[t] - first) + d1 * (first - second) + d2 * (second - y3[t]))


def result(parts, vecs, images):
    return call(result_kernel, (shape(T, R, N), shape(T, R, N)), [VMEM] * 8)(parts, *vecs, *images)


def shift(value, steps):
    count = lax.axis_size("tm")
    return lax.ppermute(value, "tm", [(i, (i + steps) % count) for i in range(count)])


def all_parts(value):
    count = lax.axis_size("tm")
    spread = lax.all_to_all(jnp.broadcast_to(value[None], (count,) + value.shape), "tm", 0, 0)
    return spread.reshape(count, value.shape[1])


def swaps(one, two):
    count = lax.axis_size("tm")
    one = lax.ppermute(one, "tm", [(i, i ^ 1) for i in range(count)])
    return one, lax.ppermute(two, "tm", [(i, (i + (1 if i % 2 else -1)) % count) for i in range(count)])


def shards(weights, pattern, shift_reg, rhs):
    flag = jnp.broadcast_to((1 - lax.axis_index("tm") % 2).astype(F32), (8, N))
    flag, pattern = lax.optimization_barrier((flag, pattern))
    inflow = shift(ahead_sums(pattern, weights), 1)
    high, low, own = band_pieces(pattern, weights, shift_reg)
    diag, vec, *leaving = first(flag, rhs, own, inflow, high, low)
    vecs, images, found = [vec], [rhs], []
    for step in range(3):
        got = swaps(*leaving)
        partial, part, *extra = local(vecs, images[-1], high, low)
        found.append(part)
        turned = extra or turned
        if step < 2:
            image, vec, *leaving = next_step(flag, *got, partial, diag, high, low, *turned)
            images.append(image)
            vecs.append(vec)
    image, part = gram(flag, *got, partial, *turned, *vecs, *found)
    return result(all_parts(part), vecs, images + [image])


def solution(mesh):
    return jax.shard_map(
        shards,
        mesh=mesh,
        in_specs=(P("tm", None, None, None), P("tm", None), P("tm", None), P("tm", "scen", None)),
        out_specs=(P("tm", "scen", None), P("tm", "scen", None)),
        check_vma=False,
    )
```

```python
import functools

import jax
import jax.numpy as jnp
from jax import lax
from jax.experimental import pallas as pl
from jax.experimental.pallas import tpu as pltpu
from jax.sharding import PartitionSpec as P

F32 = jnp.float32
BF16 = jnp.bfloat16
MIB = 1024 * 1024
N = 128
T = 8
R = 64
VMEM = pl.BlockSpec(memory_space=pltpu.VMEM)
HBM = pl.BlockSpec(memory_space=pltpu.HBM)

BAND = (T // 2, 2 * N, (T + 1) * N)


def call(body, outs, specs=None, scratch=(), limit=16, flops=0, moved=0):
    return pl.pallas_call(
        body,
        out_shape=outs,
        in_specs=specs,
        out_specs=jax.tree.map(lambda _: VMEM, outs),
        scratch_shapes=list(scratch),
        compiler_params=pltpu.CompilerParams(vmem_limit_bytes=limit * MIB),
        cost_estimate=pl.CostEstimate(flops=flops, bytes_accessed=moved, transcendentals=0),
    )


def in_hbm(value):
    return pltpu.with_memory_space_constraint(value, pltpu.HBM)


def shape(*dims, dtype=F32):
    return jax.ShapeDtypeStruct(dims, dtype)


def dot(a, b):
    return lax.dot_general(a, b, (((1,), (0,)), ((), ())), preferred_element_type=F32)


def dot_t(a, b):
    return lax.dot_general(a, b, (((1,), (1,)), ((), ())), preferred_element_type=F32)


def two_sum(a, b):
    s = a + b
    t = s - a
    return s, (a - (s - t)) + (b - t)


def dd_add(a, b):
    s, e = two_sum(a[0], b[0])
    return s, e + (a[1] + b[1])


def halves(a):
    t = a * 4097.0
    h = t - (t - a)
    return h, a - h


def two_prod(a, b):
    p = a * b
    ah, al = halves(a)
    bh, bl = halves(b)
    return p, ((ah * bh - p) + ah * bl + al * bh) + al * bl


def ahead_kernel(pattern, weights, ahead, mask, buf, cols, sems):
    head = pltpu.make_async_copy(pattern, mask, sems.at[T])
    head.start()
    copies = []
    for t in range(T):
        some = slice(T - 1 - t, T)
        copies.append(pltpu.make_async_copy(weights.at[t, some], buf.at[t, some], sems.at[t]))
    for copy in copies:
        copy.start()
    cols[...] = jnp.zeros_like(cols)
    head.wait()
    for t in range(T):
        copies[t].wait()

        def step(k, carry):
            m = buf[t, k] * mask[t, k].astype(F32)
            cols[t + k + 1 - T] += jnp.sum(m.reshape(N // 8, 8, N), axis=0)
            return carry

        lax.fori_loop(T - 1 - t, T, step, 0)
    ahead[...] = jnp.sum(cols[...], axis=1)


def ahead_sums(pattern, weights):
    pattern, weights = in_hbm(pattern), in_hbm(weights)
    return call(
        ahead_kernel,
        shape(T, N),
        [HBM, HBM],
        [
            pltpu.SMEM((T, T), jnp.int32),
            pltpu.VMEM((T, T, N, N), F32),
            pltpu.VMEM((T, 8, N), F32),
            pltpu.SemaphoreType.DMA((T + 1,)),
        ],
        flops=4 * T * T * N * N,
        moved=4 * T * T * N * N,
    )(pattern, weights)


def band_kernel(pattern, weights, reg, high, low, own, mask, buf, cols, extra, sems):
    def copy(t):
        return pltpu.make_async_copy(weights.at[t], buf.at[t], sems.at[t])

    head = pltpu.make_async_copy(pattern, mask, sems.at[T])
    tail = pltpu.make_async_copy(reg, extra, sems.at[T + 1])
    head.start()
    for t in range(T):
        copy(t).start()
    tail.start()
    cols[...] = jnp.zeros_like(cols)
    zero = jnp.zeros((N, N), BF16)
    for a in range(T // 2):
        for piece in (high, low):
            piece[a, N : 2 * N, 0:N] = zero
            piece[a, 0:N, T * N : (T + 1) * N] = zero
    head.wait()

    def step(a, carry):
        for half in range(2):
            t = 2 * a + half
            copy(t).wait()
            rows = jnp.zeros((N, N), F32)
            for k in range(T):
                m = buf[t, k] * mask[t, k].astype(F32)
                rows = rows + m
                cols[t + k + 1] += jnp.sum(m.reshape(N // 8, 8, N), axis=0)
                h = m.astype(BF16)
                place = slice((k + half) * N, (k + half + 1) * N)
                high[a, half * N : (half + 1) * N, place] = h
                low[a, half * N : (half + 1) * N, place] = (m - h.astype(F32)).astype(BF16)
            own[pl.ds(t, 1), :] = jnp.sum(rows.T, axis=0, keepdims=True)
        return carry

    lax.fori_loop(0, T // 2, step, 0)
    tail.wait()
    own[...] += jnp.sum(cols[:T], axis=1) + extra[...]


def band_pieces(pattern, weights, reg):
    pattern, weights, reg = in_hbm(pattern), in_hbm(weights), in_hbm(reg)
    return call(
        band_kernel,
        (shape(*BAND, dtype=BF16), shape(*BAND, dtype=BF16), shape(T, N)),
        [HBM, HBM, HBM],
        [
            pltpu.SMEM((T, T), jnp.int32),
            pltpu.VMEM((T, T, N, N), F32),
            pltpu.VMEM((2 * T, 8, N), F32),
            pltpu.VMEM((T, N), F32),
            pltpu.SemaphoreType.DMA((T + 2,)),
        ],
        flops=2048 * T * T * N * N,
        moved=8 * T * T * N * N,
    )(pattern, weights, reg)


def put_pieces(pieces, t, value):
    h = value.astype(BF16)
    pieces[0:R, t * N : (t + 1) * N] = h
    pieces[R : 2 * R, t * N : (t + 1) * N] = (value - h.astype(F32)).astype(BF16)


def product(pieces, cols, high, low, mult):
    both = mult(pieces[:, cols], high)
    return (both[:R] + mult(pieces[0:R, cols], low)) + both[R:]


def to_next(pieces, high, low, out):
    for b in range(T // 2):
        total = None
        for a in range(b, T // 2):
            at = slice((7 + 2 * b - 2 * a) * N, (9 + 2 * b - 2 * a) * N)
            term = product(pieces, slice(a * 2 * N, (a + 1) * 2 * N), high[a, :, at], low[a, :, at], dot)
            total = term if total is None else total + term
        out[2 * b] = total[:, :N]
        out[2 * b + 1] = total[:, N:]


def within(pieces, high, low, out):
    out[0] = jnp.zeros((R, N), F32)
    for p in range(T // 2):
        total = None
        width = 2 * N if p < T // 2 - 1 else N
        for a in range(p + 1):
            at = slice(2 * (p - a) * N, 2 * (p - a) * N + width)
            term = product(pieces, slice(a * 2 * N, (a + 1) * 2 * N), high[a, :, at], low[a, :, at], dot)
            total = term if total is None else total + term
        out[2 * p + 1] = total[:, :N]
        if width > N:
            out[2 * p + 2] = total[:, N:]
    for a in range(T // 2):
        at = slice(0, (7 - 2 * a) * N)
        term = product(pieces, slice((2 * a + 1) * N, T * N), high[a, :, at], low[a, :, at], dot_t)
        out[2 * a] += term[:, :N]
        out[2 * a + 1] += term[:, N:]


def turned_rows(a):
    return slice(a * (a + 1) * N, (a + 1) * (a + 2) * N)


def turn(high, low, turned_high, turned_low):
    for piece, out in ((high, turned_high), (low, turned_low)):
        for a in range(T // 2):
            out[turned_rows(a), :] = piece[a, :, (7 - 2 * a) * N :].T


def from_next(pieces, high, low, out):
    for a in range(T // 2):
        rows = turned_rows(a)
        term = product(pieces, slice(0, (2 * a + 2) * N), high[rows, :], low[rows, :], dot)
        out[2 * a] += term[:, :N]
        out[2 * a + 1] += term[:, N:]


def moments(first, second):
    high = low = jnp.zeros((R, N), F32)
    for t in range(T):
        high, err = two_sum(high, first[t] * second[t])
        low = low + err
    return high, low


PIECES = pltpu.VMEM((2 * R, T * N), BF16)
ONE_WAY = 2 * 3 * 40 * R * N * N


def choose(flag, first, second):
    return jnp.where(jnp.broadcast_to(flag[0:1, :], (R, N)) > 0, first, second)


def hand_out(flag, vec, high, low, two, sent, pieces):
    for t in range(T):
        put_pieces(pieces, t, vec[t])
    to_next(pieces, high, low, sent)
    for t in range(T):
        two[t] = choose(flag, vec[t], sent[t])


BLOCKS = shape(T, R, N)
TURNED = shape((T // 2) * (T // 2 + 1) * N, 2 * N, dtype=BF16)


def first_kernel(flag, rhs, own, inflow, high, low, diag, vec, two, sent, pieces):
    diag[...] = own[...] + inflow[...]
    for t in range(T):
        vec[t] = rhs[t] / diag[t : t + 1, :]
    hand_out(flag, vec, high, low, two, sent, pieces)


def first(flag, rhs, own, inflow, high, low):
    return call(
        first_kernel,
        (shape(T, N), BLOCKS, BLOCKS, BLOCKS),
        [VMEM] * 6,
        [PIECES],
        flops=ONE_WAY,
    )(flag, rhs, own, inflow, high, low)


def local_kernel(count, *refs):
    vecs, (image, high, low, flag, sent, out, found, one, *turned, pieces) = refs[:count], refs[count:]
    for t in range(T):
        one[t] = choose(flag, sent[t], vecs[-1][t])
    if turned:
        turn(high, low, *turned)
    for t in range(T):
        put_pieces(pieces, t, vecs[-1][t])
    within(pieces, high, low, out)
    for i, vec in enumerate(vecs):
        h, l = moments(vec, image)
        found[i, 0] = h
        found[i, 1] = l


def local(vecs, *args):
    turned = (TURNED, TURNED) if len(vecs) == 1 else ()
    return call(
        functools.partial(local_kernel, len(vecs)),
        (BLOCKS, shape(len(vecs), 2, R, N), BLOCKS) + turned,
        [VMEM] * (len(vecs) + 5),
        [PIECES],
        flops=2 * ONE_WAY,
    )(*vecs, *args)


def add_received(flag, got_one, got_two, partial, turned_high, turned_low, image, pieces):
    for t in range(T):
        put_pieces(pieces, t, choose(flag, got_one[t], got_two[t]))
        image[t] = partial[t] + choose(flag, got_two[t], got_one[t])
    from_next(pieces, turned_high, turned_low, image)


def step_kernel(flag, got_one, got_two, partial, diag, high, low, turned_high, turned_low, image, vec, two, sent, pieces):
    add_received(flag, got_one, got_two, partial, turned_high, turned_low, image, pieces)
    for t in range(T):
        vec[t] = image[t] / diag[t : t + 1, :]
    hand_out(flag, vec, high, low, two, sent, pieces)


def next_step(*args):
    return call(step_kernel, (BLOCKS,) * 4, [VMEM] * 9, [PIECES], flops=2 * ONE_WAY)(*args)


PAIRS = 5


def fold(high, low):
    value = (high, low)
    size = high.shape[0]
    while size > 8:
        size //= 2
        value = dd_add(tuple(v[:size] for v in value), tuple(v[size:] for v in value))
    for turn_by in (4, 2, 1):
        value = dd_add(value, tuple(pltpu.roll(v, turn_by, 0) for v in value))
    return value


def gram_kernel(
    flag, got_one, got_two, partial, turned_high, turned_low, v0, v1, v2, m0, m1, m2, image, out, pieces
):
    add_received(flag, got_one, got_two, partial, turned_high, turned_low, image, pieces)
    last = [moments(v, image) for v in (v0, v1, v2)]
    every = [(m[i, 0], m[i, 1]) for m in (m0, m1, m2) for i in range(m.shape[0])] + last + last[-1:]
    for q in range(PAIRS):
        pair = every[2 * q : 2 * q + 2]
        h, l = fold(*(jnp.concatenate([f[i] for f in pair], axis=0).T for i in range(2)))
        out[:, q * N : (q + 1) * N] = (h + l)[0:1]


def gram(*args):
    return call(gram_kernel, (BLOCKS, shape(1, PAIRS * N)), [VMEM] * 12, [PIECES], flops=ONE_WAY)(*args)


def solve(matrix, right):
    (a00, a01, a02), (a10, a11, a12), (a20, a21, a22) = matrix
    b0, b1, b2 = right
    inv0 = 1.0 / a00
    f1, f2 = a10 * inv0, a20 * inv0
    c11, c12, e1 = a11 - f1 * a01, a12 - f1 * a02, b1 - f1 * b0
    c21, c22, e2 = a21 - f2 * a01, a22 - f2 * a02, b2 - f2 * b0
    inv1 = 1.0 / c11
    g = c21 * inv1
    x2 = (e2 - g * e1) / (c22 - g * c12)
    x1 = (e1 - c12 * x2) * inv1
    x0 = (b0 - a01 * x1 - a02 * x2) * inv0
    return x0, x1, x2


def result_kernel(parts, v0, v1, v2, y0, y1, y2, y3, sol, res):
    flat = []
    for q in range(PAIRS):
        part = parts[:, q * N : (q + 1) * N]
        h, l = (v[0:1] for v in fold(part, jnp.zeros_like(part)))
        flat += [(h, l), (pltpu.roll(h, R, 1), pltpu.roll(l, R, 1))]
    g00, g01, g11, g02, g12, g22, g03, g13, g23 = flat[:9]
    full = ((g00, g01, g02, g03), (g01, g11, g12, g13), (g02, g12, g22, g23))
    minus = lambda a, b: dd_add(a, (-b[0], -b[1]))
    matrix = [[minus(row[j], row[j + 1]) for j in range(3)] for row in full]
    right = [row[1] for row in full]
    near = [[m[0] + m[1] for m in row] for row in matrix]
    coef = [jnp.zeros_like(g00[0])] * 3
    for _ in range(3):
        left = []
        for row, value in zip(matrix, right):
            for m, c in zip(row, coef):
                p, e = two_prod(m[0], c)
                value = minus(value, (p, e + m[1] * c))
            left.append(value[0] + value[1])
        coef = [c + s for c, s in zip(coef, solve(near, left))]
    rows = jnp.concatenate([c[:, :N] for c in coef] + [jnp.zeros((N - 3, N), F32)], axis=0).T
    d0, d1, d2 = (jnp.broadcast_to(rows[:R, i : i + 1], (R, N)) for i in range(3))
    for t in range(T):
        sol[t] = v0[t] + (d0 * v0[t] + d1 * v1[t] + d2 * v2[t])
        first, second = y1[t], y2[t]
        res[t] = first - (d0 * (y0[t] - first) + d1 * (first - second) + d2 * (second - y3[t]))


def result(parts, vecs, images):
    return call(result_kernel, (shape(T, R, N), shape(T, R, N)), [VMEM] * 8)(parts, *vecs, *images)


def shift(value, steps):
    count = lax.axis_size("tm")
    return lax.ppermute(value, "tm", [(i, (i + steps) % count) for i in range(count)])


def all_parts(value):
    count = lax.axis_size("tm")
    spread = lax.all_to_all(jnp.broadcast_to(value[None], (count,) + value.shape), "tm", 0, 0)
    return spread.reshape(count, value.shape[1])


def swap_within(value):
    return lax.ppermute(value, "tm", [(i, i ^ 1) for i in range(lax.axis_size("tm"))])


def swap_across(value):
    count = lax.axis_size("tm")
    return lax.ppermute(value, "tm", [(i, (i + (1 if i % 2 else -1)) % count) for i in range(count)])


def shards(weights, pattern, shift_reg, rhs):
    flag = jnp.broadcast_to((1 - lax.axis_index("tm") % 2).astype(F32), (8, N))
    flag, pattern = lax.optimization_barrier((flag, pattern))
    inflow = shift(ahead_sums(pattern, weights), 1)
    high, low, own = band_pieces(pattern, weights, shift_reg)
    diag, vec, two, sent = first(flag, rhs, own, inflow, high, low)
    vecs, images, found = [vec], [rhs], []
    for step in range(3):
        got_two = swap_across(two)
        partial, part, one, *extra = local(vecs, images[-1], high, low, flag, sent)
        got = swap_within(one), got_two
        found.append(part)
        turned = extra or turned
        if step < 2:
            image, vec, two, sent = next_step(flag, *got, partial, diag, high, low, *turned)
            images.append(image)
            vecs.append(vec)
    image, part = gram(flag, *got, partial, *turned, *vecs, *found)
    return result(all_parts(part), vecs, images + [image])


def solution(mesh):
    return jax.shard_map(
        shards,
        mesh=mesh,
        in_specs=(P("tm", None, None, None), P("tm", None), P("tm", None), P("tm", "scen", None)),
        out_specs=(P("tm", "scen", None), P("tm", "scen", None)),
        check_vma=False,
    )
```

```python
import functools

import jax
import jax.numpy as jnp
from jax import lax
from jax.experimental import pallas as pl
from jax.experimental.pallas import tpu as pltpu
from jax.sharding import PartitionSpec as P

F32 = jnp.float32
BF16 = jnp.bfloat16
MIB = 1024 * 1024
N = 128
T = 8
R = 64
VMEM = pl.BlockSpec(memory_space=pltpu.VMEM)
HBM = pl.BlockSpec(memory_space=pltpu.HBM)

BAND = (T // 2, 2 * N, (T + 1) * N)


def call(body, outs, specs=None, scratch=(), limit=16, flops=0, moved=0):
    return pl.pallas_call(
        body,
        out_shape=outs,
        in_specs=specs,
        out_specs=jax.tree.map(lambda _: VMEM, outs),
        scratch_shapes=list(scratch),
        compiler_params=pltpu.CompilerParams(vmem_limit_bytes=limit * MIB),
        cost_estimate=pl.CostEstimate(flops=flops, bytes_accessed=moved, transcendentals=0),
    )


def in_hbm(value):
    return pltpu.with_memory_space_constraint(value, pltpu.HBM)


def shape(*dims, dtype=F32):
    return jax.ShapeDtypeStruct(dims, dtype)


def dot(a, b):
    return lax.dot_general(a, b, (((1,), (0,)), ((), ())), preferred_element_type=F32)


def dot_t(a, b):
    return lax.dot_general(a, b, (((1,), (1,)), ((), ())), preferred_element_type=F32)


def two_sum(a, b):
    s = a + b
    t = s - a
    return s, (a - (s - t)) + (b - t)


def dd_add(a, b):
    s, e = two_sum(a[0], b[0])
    return s, e + (a[1] + b[1])


def halves(a):
    t = a * 4097.0
    h = t - (t - a)
    return h, a - h


def two_prod(a, b):
    p = a * b
    ah, al = halves(a)
    bh, bl = halves(b)
    return p, ((ah * bh - p) + ah * bl + al * bh) + al * bl


def on_parity(parity):
    return pl.when(lax.axis_index("tm") % 2 == parity)


def ahead_kernel(parity, pattern, weights, ahead, mask, buf, cols, sems):
    @on_parity(parity)
    def _():
        head = pltpu.make_async_copy(pattern, mask, sems.at[T])
        head.start()
        copies = []
        for t in range(T):
            some = slice(T - 1 - t, T)
            copies.append(pltpu.make_async_copy(weights.at[t, some], buf.at[t, some], sems.at[t]))
        for copy in copies:
            copy.start()
        for t in range(T):
            copies[t].wait()
            for k in range(T - 1 - t, T):
                cols[t, k] = jnp.sum(buf[t, k].reshape(N // 8, 8, N), axis=0)
        head.wait()
        for b in range(T):
            total = jnp.zeros((8, N), F32)
            for t in range(b, T):
                k = T - 1 - t + b
                total = total + cols[t, k] * mask[t, k].astype(F32)
            ahead[b : b + 1, :] = jnp.sum(total, axis=0, keepdims=True)


def ahead_sums(parity, pattern, weights):
    pattern, weights = in_hbm(pattern), in_hbm(weights)
    return call(
        functools.partial(ahead_kernel, parity),
        shape(T, N),
        [HBM, HBM],
        [
            pltpu.SMEM((T, T), jnp.int32),
            pltpu.VMEM((T, T, N, N), F32),
            pltpu.VMEM((T, T, 8, N), F32),
            pltpu.SemaphoreType.DMA((T + 1,)),
        ],
        flops=4 * T * T * N * N,
        moved=4 * T * T * N * N,
    )(pattern, weights)


def band_kernel(pattern, weights, reg, high, low, own, mask, buf, cols, extra, sems):
    def copy(t):
        return pltpu.make_async_copy(weights.at[t], buf.at[t], sems.at[t])

    head = pltpu.make_async_copy(pattern, mask, sems.at[T])
    tail = pltpu.make_async_copy(reg, extra, sems.at[T + 1])
    head.start()
    for t in range(T):
        copy(t).start()
    tail.start()
    cols[...] = jnp.zeros_like(cols)
    zero = jnp.zeros((N, N), BF16)
    for a in range(T // 2):
        for piece in (high, low):
            piece[a, N : 2 * N, 0:N] = zero
            piece[a, 0:N, T * N : (T + 1) * N] = zero
    head.wait()

    def step(a, carry):
        for half in range(2):
            t = 2 * a + half
            copy(t).wait()
            rows = jnp.zeros((N, N), F32)
            for k in range(T):
                m = buf[t, k] * mask[t, k].astype(F32)
                rows = rows + m
                cols[t + k + 1] += jnp.sum(m.reshape(N // 8, 8, N), axis=0)
                h = m.astype(BF16)
                place = slice((k + half) * N, (k + half + 1) * N)
                high[a, half * N : (half + 1) * N, place] = h
                low[a, half * N : (half + 1) * N, place] = (m - h.astype(F32)).astype(BF16)
            own[pl.ds(t, 1), :] = jnp.sum(rows.T, axis=0, keepdims=True)
        return carry

    lax.fori_loop(0, T // 2, step, 0)
    tail.wait()
    own[...] += jnp.sum(cols[:T], axis=1) + extra[...]


def band_pieces(pattern, weights, reg):
    pattern, weights, reg = in_hbm(pattern), in_hbm(weights), in_hbm(reg)
    return call(
        band_kernel,
        (shape(*BAND, dtype=BF16), shape(*BAND, dtype=BF16), shape(T, N)),
        [HBM, HBM, HBM],
        [
            pltpu.SMEM((T, T), jnp.int32),
            pltpu.VMEM((T, T, N, N), F32),
            pltpu.VMEM((2 * T, 8, N), F32),
            pltpu.VMEM((T, N), F32),
            pltpu.SemaphoreType.DMA((T + 2,)),
        ],
        flops=2048 * T * T * N * N,
        moved=8 * T * T * N * N,
    )(pattern, weights, reg)


def put_pieces(pieces, t, value):
    h = value.astype(BF16)
    pieces[0:R, t * N : (t + 1) * N] = h
    pieces[R : 2 * R, t * N : (t + 1) * N] = (value - h.astype(F32)).astype(BF16)


def product(pieces, cols, high, low, mult):
    both = mult(pieces[:, cols], high)
    return (both[:R] + mult(pieces[0:R, cols], low)) + both[R:]


def to_next(pieces, high, low, out):
    for b in range(T // 2):
        total = None
        for a in range(b, T // 2):
            at = slice((7 + 2 * b - 2 * a) * N, (9 + 2 * b - 2 * a) * N)
            term = product(pieces, slice(a * 2 * N, (a + 1) * 2 * N), high[a, :, at], low[a, :, at], dot)
            total = term if total is None else total + term
        out[2 * b] = total[:, :N]
        out[2 * b + 1] = total[:, N:]


def within(pieces, high, low, out):
    out[0] = jnp.zeros((R, N), F32)
    for p in range(T // 2):
        total = None
        width = 2 * N if p < T // 2 - 1 else N
        for a in range(p + 1):
            at = slice(2 * (p - a) * N, 2 * (p - a) * N + width)
            term = product(pieces, slice(a * 2 * N, (a + 1) * 2 * N), high[a, :, at], low[a, :, at], dot)
            total = term if total is None else total + term
        out[2 * p + 1] = total[:, :N]
        if width > N:
            out[2 * p + 2] = total[:, N:]
    for a in range(T // 2):
        at = slice(0, (7 - 2 * a) * N)
        term = product(pieces, slice((2 * a + 1) * N, T * N), high[a, :, at], low[a, :, at], dot_t)
        out[2 * a] += term[:, :N]
        out[2 * a + 1] += term[:, N:]


def turned_rows(a):
    return slice(a * (a + 1) * N, (a + 1) * (a + 2) * N)


def turn(high, low, turned_high, turned_low):
    for piece, out in ((high, turned_high), (low, turned_low)):
        for a in range(T // 2):
            out[turned_rows(a), :] = piece[a, :, (7 - 2 * a) * N :].T


def from_next(pieces, high, low, out):
    for a in range(T // 2):
        rows = turned_rows(a)
        term = product(pieces, slice(0, (2 * a + 2) * N), high[rows, :], low[rows, :], dot)
        out[2 * a] += term[:, :N]
        out[2 * a + 1] += term[:, N:]


def moments(first, second):
    high = low = jnp.zeros((R, N), F32)
    for t in range(T):
        high, err = two_sum(high, first[t] * second[t])
        low = low + err
    return high, low


PIECES = pltpu.VMEM((2 * R, T * N), BF16)
ONE_WAY = 2 * 3 * 40 * R * N * N


def choose(flag, first, second):
    return jnp.where(jnp.broadcast_to(flag[0:1, :], (R, N)) > 0, first, second)


def hand_out(flag, vec, high, low, one, two, sent, pieces):
    for t in range(T):
        put_pieces(pieces, t, vec[t])
    to_next(pieces, high, low, sent)
    for t in range(T):
        one[t] = choose(flag, sent[t], vec[t])
        two[t] = choose(flag, vec[t], sent[t])


BLOCKS = shape(T, R, N)
SENT = pltpu.VMEM((T, R, N), F32)
TURNED = shape((T // 2) * (T // 2 + 1) * N, 2 * N, dtype=BF16)


def first_odd_kernel(rhs, own, inflow, high, low, sent, pieces):
    @on_parity(1)
    def _():
        diag = own[...] + inflow[...]
        for t in range(T):
            put_pieces(pieces, t, rhs[t] / diag[t : t + 1, :])
        to_next(pieces, high, low, sent)


def first_odd(*args):
    return call(first_odd_kernel, BLOCKS, [VMEM] * 5, [PIECES], flops=ONE_WAY)(*args)


def first_even_kernel(rhs, own, inflow_odd, inflow_even, high, low, diag, vec, one, pieces):
    diag[...] = own[...] + (inflow_odd[...] + inflow_even[...])
    for t in range(T):
        vec[t] = rhs[t] / diag[t : t + 1, :]

    @on_parity(0)
    def _():
        for t in range(T):
            put_pieces(pieces, t, vec[t])
        to_next(pieces, high, low, one)

    @on_parity(1)
    def _():
        one[...] = vec[...]


def first_even(*args):
    return call(first_even_kernel, (shape(T, N), BLOCKS, BLOCKS), [VMEM] * 6, [PIECES], flops=ONE_WAY)(*args)


def local_kernel(count, *refs):
    vecs, (image, high, low, out, found, *turned, pieces) = refs[:count], refs[count:]
    if turned:
        turn(high, low, *turned)
    for t in range(T):
        put_pieces(pieces, t, vecs[-1][t])
    within(pieces, high, low, out)
    for i, vec in enumerate(vecs):
        h, l = moments(vec, image)
        found[i, 0] = h
        found[i, 1] = l


def local(vecs, image, high, low):
    turned = (TURNED, TURNED) if len(vecs) == 1 else ()
    return call(
        functools.partial(local_kernel, len(vecs)),
        (BLOCKS, shape(len(vecs), 2, R, N)) + turned,
        [VMEM] * (len(vecs) + 3),
        [PIECES],
        flops=2 * ONE_WAY,
    )(*vecs, image, high, low)


def add_received(flag, got_one, got_even, got_odd, partial, turned_high, turned_low, image, pieces):
    for t in range(T):
        put_pieces(pieces, t, choose(flag, got_one[t], got_odd[t]))
        image[t] = partial[t] + choose(flag, got_even[t], got_one[t])
    from_next(pieces, turned_high, turned_low, image)


def step_kernel(
    flag,
    got_one,
    got_even,
    got_odd,
    partial,
    diag,
    high,
    low,
    turned_high,
    turned_low,
    image,
    vec,
    one,
    two,
    sent,
    pieces,
):
    add_received(flag, got_one, got_even, got_odd, partial, turned_high, turned_low, image, pieces)
    for t in range(T):
        vec[t] = image[t] / diag[t : t + 1, :]
    hand_out(flag, vec, high, low, one, two, sent, pieces)


def next_step(*args):
    return call(step_kernel, (BLOCKS,) * 4, [VMEM] * 10, [SENT, PIECES], flops=2 * ONE_WAY)(*args)


PAIRS = 5


def fold(high, low):
    value = (high, low)
    size = high.shape[0]
    while size > 8:
        size //= 2
        value = dd_add(tuple(v[:size] for v in value), tuple(v[size:] for v in value))
    for turn_by in (4, 2, 1):
        value = dd_add(value, tuple(pltpu.roll(v, turn_by, 0) for v in value))
    return value


def gram_kernel(
    flag, got_one, got_even, got_odd, partial, turned_high, turned_low, v0, v1, v2, m0, m1, m2, image, out, pieces
):
    add_received(flag, got_one, got_even, got_odd, partial, turned_high, turned_low, image, pieces)
    last = [moments(v, image) for v in (v0, v1, v2)]
    every = [(m[i, 0], m[i, 1]) for m in (m0, m1, m2) for i in range(m.shape[0])] + last + last[-1:]
    for q in range(PAIRS):
        pair = every[2 * q : 2 * q + 2]
        h, l = fold(*(jnp.concatenate([f[i] for f in pair], axis=0).T for i in range(2)))
        out[:, q * N : (q + 1) * N] = (h + l)[0:1]


def gram(*args):
    return call(gram_kernel, (BLOCKS, shape(1, PAIRS * N)), [VMEM] * 13, [PIECES], flops=ONE_WAY)(*args)


def solve(matrix, right):
    (a00, a01, a02), (a10, a11, a12), (a20, a21, a22) = matrix
    b0, b1, b2 = right
    inv0 = 1.0 / a00
    f1, f2 = a10 * inv0, a20 * inv0
    c11, c12, e1 = a11 - f1 * a01, a12 - f1 * a02, b1 - f1 * b0
    c21, c22, e2 = a21 - f2 * a01, a22 - f2 * a02, b2 - f2 * b0
    inv1 = 1.0 / c11
    g = c21 * inv1
    x2 = (e2 - g * e1) / (c22 - g * c12)
    x1 = (e1 - c12 * x2) * inv1
    x0 = (b0 - a01 * x1 - a02 * x2) * inv0
    return x0, x1, x2


def result_kernel(parts, v0, v1, v2, y0, y1, y2, y3, sol, res):
    flat = []
    for q in range(PAIRS):
        part = parts[:, q * N : (q + 1) * N]
        h, l = (v[0:1] for v in fold(part, jnp.zeros_like(part)))
        flat += [(h, l), (pltpu.roll(h, R, 1), pltpu.roll(l, R, 1))]
    g00, g01, g11, g02, g12, g22, g03, g13, g23 = flat[:9]
    full = ((g00, g01, g02, g03), (g01, g11, g12, g13), (g02, g12, g22, g23))
    minus = lambda a, b: dd_add(a, (-b[0], -b[1]))
    matrix = [[minus(row[j], row[j + 1]) for j in range(3)] for row in full]
    right = [row[1] for row in full]
    near = [[m[0] + m[1] for m in row] for row in matrix]
    coef = [jnp.zeros_like(g00[0])] * 3
    for _ in range(3):
        left = []
        for row, value in zip(matrix, right):
            for m, c in zip(row, coef):
                p, e = two_prod(m[0], c)
                value = minus(value, (p, e + m[1] * c))
            left.append(value[0] + value[1])
        coef = [c + s for c, s in zip(coef, solve(near, left))]
    rows = jnp.concatenate([c[:, :N] for c in coef] + [jnp.zeros((N - 3, N), F32)], axis=0).T
    d0, d1, d2 = (jnp.broadcast_to(rows[:R, i : i + 1], (R, N)) for i in range(3))
    for t in range(T):
        sol[t] = v0[t] + (d0 * v0[t] + d1 * v1[t] + d2 * v2[t])
        first, second = y1[t], y2[t]
        res[t] = first - (d0 * (y0[t] - first) + d1 * (first - second) + d2 * (second - y3[t]))


def result(parts, vecs, images):
    return call(result_kernel, (shape(T, R, N), shape(T, R, N)), [VMEM] * 8)(parts, *vecs, *images)


def shift(value, steps, parity):
    count = lax.axis_size("tm")
    return lax.ppermute(value, "tm", [(i, (i + steps) % count) for i in range(parity, count, 2)])


def all_parts(value):
    count = lax.axis_size("tm")
    spread = lax.all_to_all(jnp.broadcast_to(value[None], (count,) + value.shape), "tm", 0, 0)
    return spread.reshape(count, value.shape[1])


def swap_within(value):
    return lax.ppermute(value, "tm", [(i, i ^ 1) for i in range(lax.axis_size("tm"))])


def swap_across(value):
    count = lax.axis_size("tm")
    return lax.ppermute(value, "tm", [(i, (i + (1 if i % 2 else -1)) % count) for i in range(count)])


def shards(weights, pattern, shift_reg, rhs):
    flag = jnp.broadcast_to((1 - lax.axis_index("tm") % 2).astype(F32), (8, N))
    flag, pattern = lax.optimization_barrier((flag, pattern))
    inflow_even = shift(ahead_sums(1, pattern, weights), 1, 1)
    inflow_odd = shift(ahead_sums(0, pattern, weights), 1, 0)
    high, low, own = band_pieces(pattern, weights, shift_reg)
    got_even = shift(first_odd(rhs, own, inflow_odd, high, low), 1, 1)
    diag, vec, one = first_even(rhs, own, inflow_odd, inflow_even, high, low)
    got_odd = shift(vec, -1, 0)
    got = swap_within(one), got_even, got_odd
    vecs, images, found = [vec], [rhs], []
    for step in range(3):
        partial, part, *extra = local(vecs, images[-1], high, low)
        found.append(part)
        turned = extra or turned
        if step < 2:
            image, vec, one, two = next_step(flag, *got, partial, diag, high, low, *turned)
            got_two = swap_across(two)
            got = swap_within(one), got_two, got_two
            images.append(image)
            vecs.append(vec)
    image, part = gram(flag, *got, partial, *turned, *vecs, *found)
    return result(all_parts(part), vecs, images + [image])


def solution(mesh):
    return jax.shard_map(
        shards,
        mesh=mesh,
        in_specs=(P("tm", None, None, None), P("tm", None), P("tm", None), P("tm", "scen", None)),
        out_specs=(P("tm", "scen", None), P("tm", "scen", None)),
        check_vma=False,
    )
```

```python
import functools

import jax
import jax.numpy as jnp
from jax import lax
from jax.experimental import pallas as pl
from jax.experimental.pallas import tpu as pltpu
from jax.sharding import PartitionSpec as P

F32 = jnp.float32
BF16 = jnp.bfloat16
MIB = 1024 * 1024
N = 128
T = 8
R = 64
VMEM = pl.BlockSpec(memory_space=pltpu.VMEM)
HBM = pl.BlockSpec(memory_space=pltpu.HBM)

BAND = (T // 2, 2 * N, (T + 1) * N)


def call(body, outs, specs=None, scratch=(), limit=16, flops=0, moved=0):
    return pl.pallas_call(
        body,
        out_shape=outs,
        in_specs=specs,
        out_specs=jax.tree.map(lambda _: VMEM, outs),
        scratch_shapes=list(scratch),
        compiler_params=pltpu.CompilerParams(vmem_limit_bytes=limit * MIB),
        cost_estimate=pl.CostEstimate(flops=flops, bytes_accessed=moved, transcendentals=0),
    )


def in_hbm(value):
    return pltpu.with_memory_space_constraint(value, pltpu.HBM)


def shape(*dims, dtype=F32):
    return jax.ShapeDtypeStruct(dims, dtype)


def dot(a, b):
    return lax.dot_general(a, b, (((1,), (0,)), ((), ())), preferred_element_type=F32)


def dot_t(a, b):
    return lax.dot_general(a, b, (((1,), (1,)), ((), ())), preferred_element_type=F32)


def two_sum(a, b):
    s = a + b
    t = s - a
    return s, (a - (s - t)) + (b - t)


def dd_add(a, b):
    s, e = two_sum(a[0], b[0])
    return s, e + (a[1] + b[1])


def halves(a):
    t = a * 4097.0
    h = t - (t - a)
    return h, a - h


def two_prod(a, b):
    p = a * b
    ah, al = halves(a)
    bh, bl = halves(b)
    return p, ((ah * bh - p) + ah * bl + al * bh) + al * bl


def ahead_kernel(pattern, weights, ahead, mask, buf, cols, sems):
    head = pltpu.make_async_copy(pattern, mask, sems.at[T])
    head.start()
    copies = []
    for t in range(T):
        some = slice(T - 1 - t, T)
        copies.append(pltpu.make_async_copy(weights.at[t, some], buf.at[t, some], sems.at[t]))
    for copy in copies:
        copy.start()
    for t in range(T):
        copies[t].wait()
        for k in range(T - 1 - t, T):
            cols[t, k] = jnp.sum(buf[t, k].reshape(N // 8, 8, N), axis=0)
    head.wait()
    for b in range(T):
        total = jnp.zeros((8, N), F32)
        for t in range(b, T):
            k = T - 1 - t + b
            total = total + cols[t, k] * mask[t, k].astype(F32)
        ahead[b : b + 1, :] = jnp.sum(total, axis=0, keepdims=True)


def ahead_sums(pattern, weights):
    pattern, weights = in_hbm(pattern), in_hbm(weights)
    return call(
        ahead_kernel,
        shape(T, N),
        [HBM, HBM],
        [
            pltpu.SMEM((T, T), jnp.int32),
            pltpu.VMEM((T, T, N, N), F32),
            pltpu.VMEM((T, T, 8, N), F32),
            pltpu.SemaphoreType.DMA((T + 1,)),
        ],
        flops=4 * T * T * N * N,
        moved=4 * T * T * N * N,
    )(pattern, weights)


def band_kernel(pattern, weights, reg, high, low, own, mask, buf, cols, extra, sems):
    def copy(t):
        return pltpu.make_async_copy(weights.at[t], buf.at[t], sems.at[t])

    head = pltpu.make_async_copy(pattern, mask, sems.at[T])
    tail = pltpu.make_async_copy(reg, extra, sems.at[T + 1])
    head.start()
    for t in range(T):
        copy(t).start()
    tail.start()
    cols[...] = jnp.zeros_like(cols)
    zero = jnp.zeros((N, N), BF16)
    for a in range(T // 2):
        for piece in (high, low):
            piece[a, N : 2 * N, 0:N] = zero
            piece[a, 0:N, T * N : (T + 1) * N] = zero
    head.wait()

    def step(a, carry):
        for half in range(2):
            t = 2 * a + half
            copy(t).wait()
            rows = jnp.zeros((N, N), F32)
            for k in range(T):
                m = buf[t, k] * mask[t, k].astype(F32)
                rows = rows + m
                cols[t + k + 1] += jnp.sum(m.reshape(N // 8, 8, N), axis=0)
                h = m.astype(BF16)
                place = slice((k + half) * N, (k + half + 1) * N)
                high[a, half * N : (half + 1) * N, place] = h
                low[a, half * N : (half + 1) * N, place] = (m - h.astype(F32)).astype(BF16)
            own[pl.ds(t, 1), :] = jnp.sum(rows.T, axis=0, keepdims=True)
        return carry

    lax.fori_loop(0, T // 2, step, 0)
    tail.wait()
    own[...] += jnp.sum(cols[:T], axis=1) + extra[...]


def band_pieces(pattern, weights, reg):
    pattern, weights, reg = in_hbm(pattern), in_hbm(weights), in_hbm(reg)
    return call(
        band_kernel,
        (shape(*BAND, dtype=BF16), shape(*BAND, dtype=BF16), shape(T, N)),
        [HBM, HBM, HBM],
        [
            pltpu.SMEM((T, T), jnp.int32),
            pltpu.VMEM((T, T, N, N), F32),
            pltpu.VMEM((2 * T, 8, N), F32),
            pltpu.VMEM((T, N), F32),
            pltpu.SemaphoreType.DMA((T + 2,)),
        ],
        flops=2048 * T * T * N * N,
        moved=8 * T * T * N * N,
    )(pattern, weights, reg)


def put_pieces(pieces, t, value):
    h = value.astype(BF16)
    pieces[0:R, t * N : (t + 1) * N] = h
    pieces[R : 2 * R, t * N : (t + 1) * N] = (value - h.astype(F32)).astype(BF16)


def product(pieces, cols, high, low, mult):
    both = mult(pieces[:, cols], high)
    return (both[:R] + mult(pieces[0:R, cols], low)) + both[R:]


def to_next(pieces, high, low, out):
    for b in range(T // 2):
        total = None
        for a in range(b, T // 2):
            at = slice((7 + 2 * b - 2 * a) * N, (9 + 2 * b - 2 * a) * N)
            term = product(pieces, slice(a * 2 * N, (a + 1) * 2 * N), high[a, :, at], low[a, :, at], dot)
            total = term if total is None else total + term
        out[2 * b] = total[:, :N]
        out[2 * b + 1] = total[:, N:]


def within(pieces, high, low, out):
    out[0] = jnp.zeros((R, N), F32)
    for p in range(T // 2):
        total = None
        width = 2 * N if p < T // 2 - 1 else N
        for a in range(p + 1):
            at = slice(2 * (p - a) * N, 2 * (p - a) * N + width)
            term = product(pieces, slice(a * 2 * N, (a + 1) * 2 * N), high[a, :, at], low[a, :, at], dot)
            total = term if total is None else total + term
        out[2 * p + 1] = total[:, :N]
        if width > N:
            out[2 * p + 2] = total[:, N:]
    for a in range(T // 2):
        at = slice(0, (7 - 2 * a) * N)
        term = product(pieces, slice((2 * a + 1) * N, T * N), high[a, :, at], low[a, :, at], dot_t)
        out[2 * a] += term[:, :N]
        out[2 * a + 1] += term[:, N:]


def turned_rows(a):
    return slice(a * (a + 1) * N, (a + 1) * (a + 2) * N)


def turn(high, low, turned_high, turned_low):
    for piece, out in ((high, turned_high), (low, turned_low)):
        for a in range(T // 2):
            out[turned_rows(a), :] = piece[a, :, (7 - 2 * a) * N :].T


def from_next(pieces, high, low, out):
    for a in range(T // 2):
        rows = turned_rows(a)
        term = product(pieces, slice(0, (2 * a + 2) * N), high[rows, :], low[rows, :], dot)
        out[2 * a] += term[:, :N]
        out[2 * a + 1] += term[:, N:]


def moments(first, second):
    high = low = jnp.zeros((R, N), F32)
    for t in range(T):
        high, err = two_sum(high, first[t] * second[t])
        low = low + err
    return high, low


PIECES = pltpu.VMEM((2 * R, T * N), BF16)
ONE_WAY = 2 * 3 * 40 * R * N * N


def choose(flag, first, second):
    return jnp.where(jnp.broadcast_to(flag[0:1, :], (R, N)) > 0, first, second)


def hand_out(flag, vec, high, low, one, two, sent, pieces):
    for t in range(T):
        put_pieces(pieces, t, vec[t])
    to_next(pieces, high, low, sent)
    for t in range(T):
        one[t] = choose(flag, sent[t], vec[t])
        two[t] = choose(flag, vec[t], sent[t])


BLOCKS = shape(T, R, N)
SENT = pltpu.VMEM((T, R, N), F32)
TURNED = shape((T // 2) * (T // 2 + 1) * N, 2 * N, dtype=BF16)


def on_parity(parity):
    return pl.when(lax.axis_index("tm") % 2 == parity)


def first_kernel(rhs, own, inflow, high, low, diag, vec, two, pieces):
    diag[...] = own[...] + inflow[...]

    @on_parity(0)
    def _():
        for t in range(T):
            value = rhs[t] / diag[t : t + 1, :]
            vec[t] = value
            two[t] = value

    @on_parity(1)
    def _():
        for t in range(T):
            value = rhs[t] / diag[t : t + 1, :]
            vec[t] = value
            put_pieces(pieces, t, value)
        to_next(pieces, high, low, two)


def first(*args):
    return call(first_kernel, (shape(T, N), BLOCKS, BLOCKS), [VMEM] * 5, [PIECES], flops=ONE_WAY)(*args)


def local_kernel(count, *refs):
    vecs, (image, high, low, out, found, *more, pieces) = refs[:count], refs[count:]
    for t in range(T):
        put_pieces(pieces, t, vecs[-1][t])
    if more:
        one, *turned = more

        @on_parity(0)
        def _():
            to_next(pieces, high, low, one)

        @on_parity(1)
        def _():
            one[...] = vecs[0][...]

        turn(high, low, *turned)
    within(pieces, high, low, out)
    for i, vec in enumerate(vecs):
        h, l = moments(vec, image)
        found[i, 0] = h
        found[i, 1] = l


def local(vecs, image, high, low):
    more = (BLOCKS, TURNED, TURNED) if len(vecs) == 1 else ()
    return call(
        functools.partial(local_kernel, len(vecs)),
        (BLOCKS, shape(len(vecs), 2, R, N)) + more,
        [VMEM] * (len(vecs) + 3),
        [PIECES],
        flops=2 * ONE_WAY,
    )(*vecs, image, high, low)


def add_received(flag, got_one, got_two, partial, turned_high, turned_low, image, pieces):
    for t in range(T):
        put_pieces(pieces, t, choose(flag, got_one[t], got_two[t]))
        image[t] = partial[t] + choose(flag, got_two[t], got_one[t])
    from_next(pieces, turned_high, turned_low, image)


def step_kernel(flag, got_one, got_two, partial, diag, high, low, turned_high, turned_low, image, vec, one, two, sent, pieces):
    add_received(flag, got_one, got_two, partial, turned_high, turned_low, image, pieces)
    for t in range(T):
        vec[t] = image[t] / diag[t : t + 1, :]
    hand_out(flag, vec, high, low, one, two, sent, pieces)


def next_step(*args):
    return call(step_kernel, (BLOCKS,) * 4, [VMEM] * 9, [SENT, PIECES], flops=2 * ONE_WAY)(*args)


PAIRS = 5


def fold(high, low):
    value = (high, low)
    size = high.shape[0]
    while size > 8:
        size //= 2
        value = dd_add(tuple(v[:size] for v in value), tuple(v[size:] for v in value))
    for turn_by in (4, 2, 1):
        value = dd_add(value, tuple(pltpu.roll(v, turn_by, 0) for v in value))
    return value


def gram_kernel(
    flag, got_one, got_two, partial, turned_high, turned_low, v0, v1, v2, m0, m1, m2, image, out, pieces
):
    add_received(flag, got_one, got_two, partial, turned_high, turned_low, image, pieces)
    last = [moments(v, image) for v in (v0, v1, v2)]
    every = [(m[i, 0], m[i, 1]) for m in (m0, m1, m2) for i in range(m.shape[0])] + last + last[-1:]
    for q in range(PAIRS):
        pair = every[2 * q : 2 * q + 2]
        h, l = fold(*(jnp.concatenate([f[i] for f in pair], axis=0).T for i in range(2)))
        out[:, q * N : (q + 1) * N] = (h + l)[0:1]


def gram(*args):
    return call(gram_kernel, (BLOCKS, shape(1, PAIRS * N)), [VMEM] * 12, [PIECES], flops=ONE_WAY)(*args)


def solve(matrix, right):
    (a00, a01, a02), (a10, a11, a12), (a20, a21, a22) = matrix
    b0, b1, b2 = right
    inv0 = 1.0 / a00
    f1, f2 = a10 * inv0, a20 * inv0
    c11, c12, e1 = a11 - f1 * a01, a12 - f1 * a02, b1 - f1 * b0
    c21, c22, e2 = a21 - f2 * a01, a22 - f2 * a02, b2 - f2 * b0
    inv1 = 1.0 / c11
    g = c21 * inv1
    x2 = (e2 - g * e1) / (c22 - g * c12)
    x1 = (e1 - c12 * x2) * inv1
    x0 = (b0 - a01 * x1 - a02 * x2) * inv0
    return x0, x1, x2


def result_kernel(parts, v0, v1, v2, y0, y1, y2, y3, sol, res):
    flat = []
    for q in range(PAIRS):
        part = parts[:, q * N : (q + 1) * N]
        h, l = (v[0:1] for v in fold(part, jnp.zeros_like(part)))
        flat += [(h, l), (pltpu.roll(h, R, 1), pltpu.roll(l, R, 1))]
    g00, g01, g11, g02, g12, g22, g03, g13, g23 = flat[:9]
    full = ((g00, g01, g02, g03), (g01, g11, g12, g13), (g02, g12, g22, g23))
    minus = lambda a, b: dd_add(a, (-b[0], -b[1]))
    matrix = [[minus(row[j], row[j + 1]) for j in range(3)] for row in full]
    right = [row[1] for row in full]
    near = [[m[0] + m[1] for m in row] for row in matrix]
    coef = [jnp.zeros_like(g00[0])] * 3
    for _ in range(3):
        left = []
        for row, value in zip(matrix, right):
            for m, c in zip(row, coef):
                p, e = two_prod(m[0], c)
                value = minus(value, (p, e + m[1] * c))
            left.append(value[0] + value[1])
        coef = [c + s for c, s in zip(coef, solve(near, left))]
    rows = jnp.concatenate([c[:, :N] for c in coef] + [jnp.zeros((N - 3, N), F32)], axis=0).T
    d0, d1, d2 = (jnp.broadcast_to(rows[:R, i : i + 1], (R, N)) for i in range(3))
    for t in range(T):
        sol[t] = v0[t] + (d0 * v0[t] + d1 * v1[t] + d2 * v2[t])
        first, second = y1[t], y2[t]
        res[t] = first - (d0 * (y0[t] - first) + d1 * (first - second) + d2 * (second - y3[t]))


def result(parts, vecs, images):
    return call(result_kernel, (shape(T, R, N), shape(T, R, N)), [VMEM] * 8)(parts, *vecs, *images)


def shift(value, steps):
    count = lax.axis_size("tm")
    return lax.ppermute(value, "tm", [(i, (i + steps) % count) for i in range(count)])


def all_parts(value):
    count = lax.axis_size("tm")
    spread = lax.all_to_all(jnp.broadcast_to(value[None], (count,) + value.shape), "tm", 0, 0)
    return spread.reshape(count, value.shape[1])


def swap_within(value):
    return lax.ppermute(value, "tm", [(i, i ^ 1) for i in range(lax.axis_size("tm"))])


def swap_across(value):
    count = lax.axis_size("tm")
    return lax.ppermute(value, "tm", [(i, (i + (1 if i % 2 else -1)) % count) for i in range(count)])


def shards(weights, pattern, shift_reg, rhs):
    flag = jnp.broadcast_to((1 - lax.axis_index("tm") % 2).astype(F32), (8, N))
    flag, pattern = lax.optimization_barrier((flag, pattern))
    inflow = shift(ahead_sums(pattern, weights), 1)
    high, low, own = band_pieces(pattern, weights, shift_reg)
    diag, vec, two = first(rhs, own, inflow, high, low)
    got_two = swap_across(two)
    partial, part, one, *turned = local([vec], rhs, high, low)
    got = swap_within(one), got_two
    vecs, images, found = [vec], [rhs], [part]
    for step in range(2):
        image, vec, one, two = next_step(flag, *got, partial, diag, high, low, *turned)
        got = swap_within(one), swap_across(two)
        images.append(image)
        vecs.append(vec)
        partial, part = local(vecs, image, high, low)
        found.append(part)
    image, part = gram(flag, *got, partial, *turned, *vecs, *found)
    return result(all_parts(part), vecs, images + [image])


def solution(mesh):
    return jax.shard_map(
        shards,
        mesh=mesh,
        in_specs=(P("tm", None, None, None), P("tm", None), P("tm", None), P("tm", "scen", None)),
        out_specs=(P("tm", "scen", None), P("tm", "scen", None)),
        check_vma=False,
    )
```

```python
import functools

import jax
import jax.numpy as jnp
from jax import lax
from jax.experimental import pallas as pl
from jax.experimental.pallas import tpu as pltpu
from jax.sharding import PartitionSpec as P

F32 = jnp.float32
BF16 = jnp.bfloat16
MIB = 1024 * 1024
N = 128
T = 8
R = 64
VMEM = pl.BlockSpec(memory_space=pltpu.VMEM)
HBM = pl.BlockSpec(memory_space=pltpu.HBM)

BAND = (T // 2, 2 * N, (T + 1) * N)


def call(body, outs, specs=None, scratch=(), limit=16, flops=0, moved=0):
    return pl.pallas_call(
        body,
        out_shape=outs,
        in_specs=specs,
        out_specs=jax.tree.map(lambda _: VMEM, outs),
        scratch_shapes=list(scratch),
        compiler_params=pltpu.CompilerParams(vmem_limit_bytes=limit * MIB),
        cost_estimate=pl.CostEstimate(flops=flops, bytes_accessed=moved, transcendentals=0),
    )


def in_hbm(value):
    return pltpu.with_memory_space_constraint(value, pltpu.HBM)


def shape(*dims, dtype=F32):
    return jax.ShapeDtypeStruct(dims, dtype)


def dot(a, b):
    return lax.dot_general(a, b, (((1,), (0,)), ((), ())), preferred_element_type=F32)


def dot_t(a, b):
    return lax.dot_general(a, b, (((1,), (1,)), ((), ())), preferred_element_type=F32)


def two_sum(a, b):
    s = a + b
    t = s - a
    return s, (a - (s - t)) + (b - t)


def dd_add(a, b):
    s, e = two_sum(a[0], b[0])
    return s, e + (a[1] + b[1])


def halves(a):
    t = a * 4097.0
    h = t - (t - a)
    return h, a - h


def two_prod(a, b):
    p = a * b
    ah, al = halves(a)
    bh, bl = halves(b)
    return p, ((ah * bh - p) + ah * bl + al * bh) + al * bl


def ahead_kernel(pattern, weights, ahead, mask, buf, cols, sems):
    head = pltpu.make_async_copy(pattern, mask, sems.at[T])
    head.start()
    copies = []
    for t in range(T):
        some = slice(T - 1 - t, T)
        copies.append(pltpu.make_async_copy(weights.at[t, some], buf.at[t, some], sems.at[t]))
    for copy in copies:
        copy.start()
    for t in range(T):
        copies[t].wait()
        for k in range(T - 1 - t, T):
            cols[t, k] = jnp.sum(buf[t, k].reshape(N // 8, 8, N), axis=0)
    head.wait()
    for b in range(T):
        total = jnp.zeros((8, N), F32)
        for t in range(b, T):
            k = T - 1 - t + b
            total = total + cols[t, k] * mask[t, k].astype(F32)
        ahead[b : b + 1, :] = jnp.sum(total, axis=0, keepdims=True)


def ahead_sums(pattern, weights):
    pattern, weights = in_hbm(pattern), in_hbm(weights)
    return call(
        ahead_kernel,
        shape(T, N),
        [HBM, HBM],
        [
            pltpu.SMEM((T, T), jnp.int32),
            pltpu.VMEM((T, T, N, N), F32),
            pltpu.VMEM((T, T, 8, N), F32),
            pltpu.SemaphoreType.DMA((T + 1,)),
        ],
        flops=4 * T * T * N * N,
        moved=4 * T * T * N * N,
    )(pattern, weights)


def band_kernel(pattern, weights, reg, high, low, own, mask, buf, cols, extra, sems):
    def copy(t):
        return pltpu.make_async_copy(weights.at[t], buf.at[t], sems.at[t])

    head = pltpu.make_async_copy(pattern, mask, sems.at[T])
    tail = pltpu.make_async_copy(reg, extra, sems.at[T + 1])
    head.start()
    for t in range(T):
        copy(t).start()
    tail.start()
    cols[...] = jnp.zeros_like(cols)
    zero = jnp.zeros((N, N), BF16)
    for a in range(T // 2):
        for piece in (high, low):
            piece[a, N : 2 * N, 0:N] = zero
            piece[a, 0:N, T * N : (T + 1) * N] = zero
    head.wait()

    def step(a, carry):
        for half in range(2):
            t = 2 * a + half
            copy(t).wait()
            rows = jnp.zeros((N, N), F32)
            for k in range(T):
                m = buf[t, k] * mask[t, k].astype(F32)
                rows = rows + m
                cols[t + k + 1] += jnp.sum(m.reshape(N // 8, 8, N), axis=0)
                h = m.astype(BF16)
                place = slice((k + half) * N, (k + half + 1) * N)
                high[a, half * N : (half + 1) * N, place] = h
                low[a, half * N : (half + 1) * N, place] = (m - h.astype(F32)).astype(BF16)
            own[pl.ds(t, 1), :] = jnp.sum(rows.T, axis=0, keepdims=True)
        return carry

    lax.fori_loop(0, T // 2, step, 0)
    tail.wait()
    own[...] += jnp.sum(cols[:T], axis=1) + extra[...]


def band_pieces(pattern, weights, reg):
    pattern, weights, reg = in_hbm(pattern), in_hbm(weights), in_hbm(reg)
    return call(
        band_kernel,
        (shape(*BAND, dtype=BF16), shape(*BAND, dtype=BF16), shape(T, N)),
        [HBM, HBM, HBM],
        [
            pltpu.SMEM((T, T), jnp.int32),
            pltpu.VMEM((T, T, N, N), F32),
            pltpu.VMEM((2 * T, 8, N), F32),
            pltpu.VMEM((T, N), F32),
            pltpu.SemaphoreType.DMA((T + 2,)),
        ],
        flops=2048 * T * T * N * N,
        moved=8 * T * T * N * N,
    )(pattern, weights, reg)


def put_pieces(pieces, t, value):
    h = value.astype(BF16)
    pieces[0:R, t * N : (t + 1) * N] = h
    pieces[R : 2 * R, t * N : (t + 1) * N] = (value - h.astype(F32)).astype(BF16)


def product(pieces, cols, high, low, mult):
    both = mult(pieces[:, cols], high)
    return (both[:R] + mult(pieces[0:R, cols], low)) + both[R:]


def to_next(pieces, high, low, out):
    for b in range(T // 2):
        total = None
        for a in range(b, T // 2):
            at = slice((7 + 2 * b - 2 * a) * N, (9 + 2 * b - 2 * a) * N)
            term = product(pieces, slice(a * 2 * N, (a + 1) * 2 * N), high[a, :, at], low[a, :, at], dot)
            total = term if total is None else total + term
        out[2 * b, 0:R] = total[:, :N]
        out[2 * b + 1, 0:R] = total[:, N:]


def within(pieces, high, low, out):
    out[0] = jnp.zeros((R, N), F32)
    for p in range(T // 2):
        total = None
        width = 2 * N if p < T // 2 - 1 else N
        for a in range(p + 1):
            at = slice(2 * (p - a) * N, 2 * (p - a) * N + width)
            term = product(pieces, slice(a * 2 * N, (a + 1) * 2 * N), high[a, :, at], low[a, :, at], dot)
            total = term if total is None else total + term
        out[2 * p + 1] = total[:, :N]
        if width > N:
            out[2 * p + 2] = total[:, N:]
    for a in range(T // 2):
        at = slice(0, (7 - 2 * a) * N)
        term = product(pieces, slice((2 * a + 1) * N, T * N), high[a, :, at], low[a, :, at], dot_t)
        out[2 * a] += term[:, :N]
        out[2 * a + 1] += term[:, N:]


def turned_rows(a):
    return slice(a * (a + 1) * N, (a + 1) * (a + 2) * N)


def turn(high, low, turned_high, turned_low):
    for piece, out in ((high, turned_high), (low, turned_low)):
        for a in range(T // 2):
            out[turned_rows(a), :] = piece[a, :, (7 - 2 * a) * N :].T


def from_next(pieces, high, low, out):
    for a in range(T // 2):
        rows = turned_rows(a)
        term = product(pieces, slice(0, (2 * a + 2) * N), high[rows, :], low[rows, :], dot)
        out[2 * a] += term[:, :N]
        out[2 * a + 1] += term[:, N:]


def moments(first, second):
    high = low = jnp.zeros((R, N), F32)
    for t in range(T):
        high, err = two_sum(high, first[t] * second[t])
        low = low + err
    return high, low


PIECES = pltpu.VMEM((2 * R, T * N), BF16)
ONE_WAY = 2 * 3 * 40 * R * N * N


def choose(flag, first, second):
    return jnp.where(jnp.broadcast_to(flag[0:1, :], (R, N)) > 0, first, second)


def hand_out(flag, vec, high, low, one, two, sent, pieces):
    for t in range(T):
        put_pieces(pieces, t, vec[t])
    to_next(pieces, high, low, sent)
    for t in range(T):
        one[t] = choose(flag, sent[t], vec[t])
        two[t] = choose(flag, vec[t], sent[t])


BLOCKS = shape(T, R, N)
SENT = pltpu.VMEM((T, R, N), F32)
TURNED = shape((T // 2) * (T // 2 + 1) * N, 2 * N, dtype=BF16)


def on_parity(parity):
    return pl.when(lax.axis_index("tm") % 2 == parity)


EXTRA = 8


def first_kernel(rhs, own, inflow, high, low, two, pieces):
    @on_parity(0)
    def _():
        for t in range(T):
            two[t, 0:R] = rhs[t]
            two[t, R:] = jnp.broadcast_to(own[t : t + 1, :], (EXTRA, N))

    @on_parity(1)
    def _():
        diag = own[...] + inflow[...]
        for t in range(T):
            put_pieces(pieces, t, rhs[t] / diag[t : t + 1, :])
            two[t, R:] = jnp.ones((EXTRA, N), F32)
        to_next(pieces, high, low, two)


def first(*args):
    return call(first_kernel, shape(T, R + EXTRA, N), [VMEM] * 5, [PIECES], flops=ONE_WAY)(*args)


def start_kernel(rhs, own, inflow_odd, inflow_even, high, low, diag, vec, one, out, found, *rest):
    *turned, pieces = rest

    @on_parity(0)
    def _():
        diag[...] = own[...] + inflow_even[...]

    @on_parity(1)
    def _():
        diag[...] = own[...] + inflow_odd[...]

    for t in range(T):
        value = rhs[t] / diag[t : t + 1, :]
        vec[t] = value
        put_pieces(pieces, t, value)

    @on_parity(0)
    def _():
        to_next(pieces, high, low, one)

    @on_parity(1)
    def _():
        one[...] = vec[...]

    turn(high, low, *turned)
    within(pieces, high, low, out)
    h, l = moments(vec, rhs)
    found[0, 0] = h
    found[0, 1] = l


def start(*args):
    return call(
        start_kernel,
        (shape(T, N), BLOCKS, BLOCKS, BLOCKS, shape(1, 2, R, N), TURNED, TURNED),
        [VMEM] * 6,
        [PIECES],
        flops=3 * ONE_WAY,
    )(*args)


def local_kernel(count, *refs):
    vecs, (image, high, low, out, found, pieces) = refs[:count], refs[count:]
    for t in range(T):
        put_pieces(pieces, t, vecs[-1][t])
    within(pieces, high, low, out)
    for i, vec in enumerate(vecs):
        h, l = moments(vec, image)
        found[i, 0] = h
        found[i, 1] = l


def local(vecs, image, high, low):
    return call(
        functools.partial(local_kernel, len(vecs)),
        (BLOCKS, shape(len(vecs), 2, R, N)),
        [VMEM] * (len(vecs) + 3),
        [PIECES],
        flops=2 * ONE_WAY,
    )(*vecs, image, high, low)


def add_received(flag, got_one, got_two, partial, turned_high, turned_low, image, pieces):
    for t in range(T):
        put_pieces(pieces, t, choose(flag, got_one[t], got_two[t]))
        image[t] = partial[t] + choose(flag, got_two[t], got_one[t])
    from_next(pieces, turned_high, turned_low, image)


def move_on(flag, diag, high, low, image, vec, one, two, sent, pieces):
    for t in range(T):
        vec[t] = image[t] / diag[t : t + 1, :]
    hand_out(flag, vec, high, low, one, two, sent, pieces)


def second_kernel(
    flag, ahead, got_one, got_two, partial, turned_high, turned_low, diag, high, low, image, vec, one, two, sent, pieces
):
    for t in range(T):
        value = got_two[t, 0:R]
        made = value / (got_two[t, R : R + 1] + ahead[t : t + 1, :])
        put_pieces(pieces, t, choose(flag, got_one[t], made))
        image[t] = partial[t] + choose(flag, value, got_one[t])
    from_next(pieces, turned_high, turned_low, image)
    move_on(flag, diag, high, low, image, vec, one, two, sent, pieces)


def second_step(*args):
    return call(second_kernel, (BLOCKS,) * 4, [VMEM] * 10, [SENT, PIECES], flops=2 * ONE_WAY)(*args)


def step_kernel(
    flag, got_one, got_two, partial, turned_high, turned_low, diag, high, low, image, vec, one, two, sent, pieces
):
    add_received(flag, got_one, got_two, partial, turned_high, turned_low, image, pieces)
    move_on(flag, diag, high, low, image, vec, one, two, sent, pieces)


def next_step(*args):
    return call(step_kernel, (BLOCKS,) * 4, [VMEM] * 9, [SENT, PIECES], flops=2 * ONE_WAY)(*args)


PAIRS = 5


def fold(high, low):
    value = (high, low)
    size = high.shape[0]
    while size > 8:
        size //= 2
        value = dd_add(tuple(v[:size] for v in value), tuple(v[size:] for v in value))
    for turn_by in (4, 2, 1):
        value = dd_add(value, tuple(pltpu.roll(v, turn_by, 0) for v in value))
    return value


def gram_kernel(
    flag, got_one, got_two, partial, turned_high, turned_low, v0, v1, v2, m0, m1, m2, image, out, pieces
):
    add_received(flag, got_one, got_two, partial, turned_high, turned_low, image, pieces)
    last = [moments(v, image) for v in (v0, v1, v2)]
    every = [(m[i, 0], m[i, 1]) for m in (m0, m1, m2) for i in range(m.shape[0])] + last + last[-1:]
    for q in range(PAIRS):
        pair = every[2 * q : 2 * q + 2]
        h, l = fold(*(jnp.concatenate([f[i] for f in pair], axis=0).T for i in range(2)))
        out[:, q * N : (q + 1) * N] = (h + l)[0:1]


def gram(*args):
    return call(gram_kernel, (BLOCKS, shape(1, PAIRS * N)), [VMEM] * 12, [PIECES], flops=ONE_WAY)(*args)


def solve(matrix, right):
    (a00, a01, a02), (a10, a11, a12), (a20, a21, a22) = matrix
    b0, b1, b2 = right
    inv0 = 1.0 / a00
    f1, f2 = a10 * inv0, a20 * inv0
    c11, c12, e1 = a11 - f1 * a01, a12 - f1 * a02, b1 - f1 * b0
    c21, c22, e2 = a21 - f2 * a01, a22 - f2 * a02, b2 - f2 * b0
    inv1 = 1.0 / c11
    g = c21 * inv1
    x2 = (e2 - g * e1) / (c22 - g * c12)
    x1 = (e1 - c12 * x2) * inv1
    x0 = (b0 - a01 * x1 - a02 * x2) * inv0
    return x0, x1, x2


def result_kernel(parts, v0, v1, v2, y0, y1, y2, y3, sol, res):
    flat = []
    for q in range(PAIRS):
        part = parts[:, q * N : (q + 1) * N]
        h, l = (v[0:1] for v in fold(part, jnp.zeros_like(part)))
        flat += [(h, l), (pltpu.roll(h, R, 1), pltpu.roll(l, R, 1))]
    g00, g01, g11, g02, g12, g22, g03, g13, g23 = flat[:9]
    full = ((g00, g01, g02, g03), (g01, g11, g12, g13), (g02, g12, g22, g23))
    minus = lambda a, b: dd_add(a, (-b[0], -b[1]))
    matrix = [[minus(row[j], row[j + 1]) for j in range(3)] for row in full]
    right = [row[1] for row in full]
    near = [[m[0] + m[1] for m in row] for row in matrix]
    coef = [jnp.zeros_like(g00[0])] * 3
    for _ in range(3):
        left = []
        for row, value in zip(matrix, right):
            for m, c in zip(row, coef):
                p, e = two_prod(m[0], c)
                value = minus(value, (p, e + m[1] * c))
            left.append(value[0] + value[1])
        coef = [c + s for c, s in zip(coef, solve(near, left))]
    rows = jnp.concatenate([c[:, :N] for c in coef] + [jnp.zeros((N - 3, N), F32)], axis=0).T
    d0, d1, d2 = (jnp.broadcast_to(rows[:R, i : i + 1], (R, N)) for i in range(3))
    for t in range(T):
        sol[t] = v0[t] + (d0 * v0[t] + d1 * v1[t] + d2 * v2[t])
        first, second = y1[t], y2[t]
        res[t] = first - (d0 * (y0[t] - first) + d1 * (first - second) + d2 * (second - y3[t]))


def result(parts, vecs, images):
    return call(result_kernel, (shape(T, R, N), shape(T, R, N)), [VMEM] * 8)(parts, *vecs, *images)


def all_parts(value):
    count = lax.axis_size("tm")
    spread = lax.all_to_all(jnp.broadcast_to(value[None], (count,) + value.shape), "tm", 0, 0)
    return spread.reshape(count, value.shape[1])


def swap_within(value):
    return lax.ppermute(value, "tm", [(i, i ^ 1) for i in range(lax.axis_size("tm"))])


def swap_across(value):
    count = lax.axis_size("tm")
    return lax.ppermute(value, "tm", [(i, (i + (1 if i % 2 else -1)) % count) for i in range(count)])


def shards(weights, pattern, shift_reg, rhs):
    flag = jnp.broadcast_to((1 - lax.axis_index("tm") % 2).astype(F32), (8, N))
    flag, pattern = lax.optimization_barrier((flag, pattern))
    ahead = ahead_sums(pattern, weights)
    inflow_odd, inflow_even = swap_within(ahead), swap_across(ahead)
    high, low, own = band_pieces(pattern, weights, shift_reg)
    got_two = swap_across(first(rhs, own, inflow_odd, high, low))
    diag, vec, one, partial, part, *turned = start(rhs, own, inflow_odd, inflow_even, high, low)
    got = swap_within(one), got_two
    vecs, images, found = [vec], [rhs], [part]
    for step in range(2):
        given = (flag, *got) if step else (flag, ahead, *got)
        image, vec, one, two = (next_step if step else second_step)(*given, partial, *turned, diag, high, low)
        got = swap_within(one), swap_across(two)
        images.append(image)
        vecs.append(vec)
        partial, part = local(vecs, image, high, low)
        found.append(part)
    image, part = gram(flag, *got, partial, *turned, *vecs, *found)
    return result(all_parts(part), vecs, images + [image])


def solution(mesh):
    return jax.shard_map(
        shards,
        mesh=mesh,
        in_specs=(P("tm", None, None, None), P("tm", None), P("tm", None), P("tm", "scen", None)),
        out_specs=(P("tm", "scen", None), P("tm", "scen", None)),
        check_vma=False,
    )
```

```python
import functools

import jax
import jax.numpy as jnp
from jax import lax
from jax.experimental import pallas as pl
from jax.experimental.pallas import tpu as pltpu
from jax.sharding import PartitionSpec as P

F32 = jnp.float32
BF16 = jnp.bfloat16
MIB = 1024 * 1024
N = 128
T = 8
R = 64
VMEM = pl.BlockSpec(memory_space=pltpu.VMEM)
HBM = pl.BlockSpec(memory_space=pltpu.HBM)

BAND = (T // 2, 2 * N, (T + 1) * N)


def call(body, outs, specs=None, scratch=(), limit=16, flops=0, moved=0):
    return pl.pallas_call(
        body,
        out_shape=outs,
        in_specs=specs,
        out_specs=jax.tree.map(lambda _: VMEM, outs),
        scratch_shapes=list(scratch),
        compiler_params=pltpu.CompilerParams(vmem_limit_bytes=limit * MIB),
        cost_estimate=pl.CostEstimate(flops=flops, bytes_accessed=moved, transcendentals=0),
    )


def in_hbm(value):
    return pltpu.with_memory_space_constraint(value, pltpu.HBM)


def shape(*dims, dtype=F32):
    return jax.ShapeDtypeStruct(dims, dtype)


def dot(a, b):
    return lax.dot_general(a, b, (((1,), (0,)), ((), ())), preferred_element_type=F32)


def dot_t(a, b):
    return lax.dot_general(a, b, (((1,), (1,)), ((), ())), preferred_element_type=F32)


def two_sum(a, b):
    s = a + b
    t = s - a
    return s, (a - (s - t)) + (b - t)


def dd_add(a, b):
    s, e = two_sum(a[0], b[0])
    return s, e + (a[1] + b[1])


def halves(a):
    t = a * 4097.0
    h = t - (t - a)
    return h, a - h


def two_prod(a, b):
    p = a * b
    ah, al = halves(a)
    bh, bl = halves(b)
    return p, ((ah * bh - p) + ah * bl + al * bh) + al * bl


def ahead_kernel(pattern, weights, ahead, mask, buf, cols, sems):
    head = pltpu.make_async_copy(pattern, mask, sems.at[T])
    head.start()
    copies = []
    for t in range(T):
        some = slice(T - 1 - t, T)
        copies.append(pltpu.make_async_copy(weights.at[t, some], buf.at[t, some], sems.at[t]))
    for copy in copies:
        copy.start()
    for t in range(T):
        copies[t].wait()
        for k in range(T - 1 - t, T):
            cols[t, k] = jnp.sum(buf[t, k].reshape(N // 8, 8, N), axis=0)
    head.wait()
    for b in range(T):
        total = jnp.zeros((8, N), F32)
        for t in range(b, T):
            k = T - 1 - t + b
            total = total + cols[t, k] * mask[t, k].astype(F32)
        ahead[b : b + 1, :] = jnp.sum(total, axis=0, keepdims=True)


def ahead_sums(pattern, weights):
    pattern, weights = in_hbm(pattern), in_hbm(weights)
    return call(
        ahead_kernel,
        shape(T, N),
        [HBM, HBM],
        [
            pltpu.SMEM((T, T), jnp.int32),
            pltpu.VMEM((T, T, N, N), F32),
            pltpu.VMEM((T, T, 8, N), F32),
            pltpu.SemaphoreType.DMA((T + 1,)),
        ],
        flops=4 * T * T * N * N,
        moved=4 * T * T * N * N,
    )(pattern, weights)


def band_kernel(pattern, weights, reg, high, low, own, mask, buf, cols, extra, sems):
    def copy(t):
        return pltpu.make_async_copy(weights.at[t], buf.at[t], sems.at[t])

    head = pltpu.make_async_copy(pattern, mask, sems.at[T])
    tail = pltpu.make_async_copy(reg, extra, sems.at[T + 1])
    head.start()
    for t in range(T):
        copy(t).start()
    tail.start()
    cols[...] = jnp.zeros_like(cols)
    zero = jnp.zeros((N, N), BF16)
    for a in range(T // 2):
        for piece in (high, low):
            piece[a, N : 2 * N, 0:N] = zero
            piece[a, 0:N, T * N : (T + 1) * N] = zero
    head.wait()

    def step(a, carry):
        for half in range(2):
            t = 2 * a + half
            copy(t).wait()
            rows = jnp.zeros((N, N), F32)
            for k in range(T):
                m = buf[t, k] * mask[t, k].astype(F32)
                rows = rows + m
                cols[t + k + 1] += jnp.sum(m.reshape(N // 8, 8, N), axis=0)
                h = m.astype(BF16)
                place = slice((k + half) * N, (k + half + 1) * N)
                high[a, half * N : (half + 1) * N, place] = h
                low[a, half * N : (half + 1) * N, place] = (m - h.astype(F32)).astype(BF16)
            own[pl.ds(t, 1), :] = jnp.sum(rows.T, axis=0, keepdims=True)
        return carry

    lax.fori_loop(0, T // 2, step, 0)
    tail.wait()
    own[...] += jnp.sum(cols[:T], axis=1) + extra[...]


def band_pieces(pattern, weights, reg):
    pattern, weights, reg = in_hbm(pattern), in_hbm(weights), in_hbm(reg)
    return call(
        band_kernel,
        (shape(*BAND, dtype=BF16), shape(*BAND, dtype=BF16), shape(T, N)),
        [HBM, HBM, HBM],
        [
            pltpu.SMEM((T, T), jnp.int32),
            pltpu.VMEM((T, T, N, N), F32),
            pltpu.VMEM((2 * T, 8, N), F32),
            pltpu.VMEM((T, N), F32),
            pltpu.SemaphoreType.DMA((T + 2,)),
        ],
        flops=2048 * T * T * N * N,
        moved=8 * T * T * N * N,
    )(pattern, weights, reg)


def put_pieces(pieces, t, value):
    h = value.astype(BF16)
    pieces[0:R, t * N : (t + 1) * N] = h
    pieces[R : 2 * R, t * N : (t + 1) * N] = (value - h.astype(F32)).astype(BF16)


def product(pieces, cols, high, low, mult):
    both = mult(pieces[:, cols], high)
    return (both[:R] + mult(pieces[0:R, cols], low)) + both[R:]


def to_next(pieces, high, low, out):
    for b in range(T // 2):
        total = None
        for a in range(b, T // 2):
            at = slice((7 + 2 * b - 2 * a) * N, (9 + 2 * b - 2 * a) * N)
            term = product(pieces, slice(a * 2 * N, (a + 1) * 2 * N), high[a, :, at], low[a, :, at], dot)
            total = term if total is None else total + term
        out[2 * b] = total[:, :N]
        out[2 * b + 1] = total[:, N:]


def within(pieces, high, low, out):
    out[0] = jnp.zeros((R, N), F32)
    for p in range(T // 2):
        total = None
        width = 2 * N if p < T // 2 - 1 else N
        for a in range(p + 1):
            at = slice(2 * (p - a) * N, 2 * (p - a) * N + width)
            term = product(pieces, slice(a * 2 * N, (a + 1) * 2 * N), high[a, :, at], low[a, :, at], dot)
            total = term if total is None else total + term
        out[2 * p + 1] = total[:, :N]
        if width > N:
            out[2 * p + 2] = total[:, N:]
    for a in range(T // 2):
        at = slice(0, (7 - 2 * a) * N)
        term = product(pieces, slice((2 * a + 1) * N, T * N), high[a, :, at], low[a, :, at], dot_t)
        out[2 * a] += term[:, :N]
        out[2 * a + 1] += term[:, N:]


def turned_rows(a):
    return slice(a * (a + 1) * N, (a + 1) * (a + 2) * N)


def turn(high, low, turned_high, turned_low):
    for piece, out in ((high, turned_high), (low, turned_low)):
        for a in range(T // 2):
            out[turned_rows(a), :] = piece[a, :, (7 - 2 * a) * N :].T


def from_next(pieces, high, low, out):
    for a in range(T // 2):
        rows = turned_rows(a)
        term = product(pieces, slice(0, (2 * a + 2) * N), high[rows, :], low[rows, :], dot)
        out[2 * a] += term[:, :N]
        out[2 * a + 1] += term[:, N:]


def moments(first, second):
    high = low = jnp.zeros((R, N), F32)
    for t in range(T):
        high, err = two_sum(high, first[t] * second[t])
        low = low + err
    return high, low


PIECES = pltpu.VMEM((2 * R, T * N), BF16)
ONE_WAY = 2 * 3 * 40 * R * N * N


def choose(flag, first, second):
    return jnp.where(jnp.broadcast_to(flag[0:1, :], (R, N)) > 0, first, second)


def hand_out(flag, vec, high, low, one, two, sent, pieces):
    for t in range(T):
        put_pieces(pieces, t, vec[t])
    to_next(pieces, high, low, sent)
    for t in range(T):
        one[t] = choose(flag, sent[t], vec[t])
        two[t] = choose(flag, vec[t], sent[t])


BLOCKS = shape(T, R, N)
SENT = pltpu.VMEM((T, R, N), F32)
TURNED = shape((T // 2) * (T // 2 + 1) * N, 2 * N, dtype=BF16)


def on_parity(parity):
    return pl.when(lax.axis_index("tm") % 2 == parity)


def first_kernel(rhs, own, inflow, high, low, diag, vec, two, pieces):
    diag[...] = own[...] + inflow[...]

    @on_parity(0)
    def _():
        for t in range(T):
            value = rhs[t] / diag[t : t + 1, :]
            vec[t] = value
            two[t] = value

    @on_parity(1)
    def _():
        for t in range(T):
            value = rhs[t] / diag[t : t + 1, :]
            vec[t] = value
            put_pieces(pieces, t, value)
        to_next(pieces, high, low, two)


def first(*args):
    return call(first_kernel, (shape(T, N), BLOCKS, BLOCKS), [VMEM] * 5, [PIECES], flops=ONE_WAY)(*args)


def local_kernel(count, *refs):
    vecs, (image, high, low, out, found, *more, pieces) = refs[:count], refs[count:]
    for t in range(T):
        put_pieces(pieces, t, vecs[-1][t])
    if more:
        one, *turned = more

        @on_parity(0)
        def _():
            to_next(pieces, high, low, one)

        @on_parity(1)
        def _():
            one[...] = vecs[0][...]

        turn(high, low, *turned)
    within(pieces, high, low, out)
    for i, vec in enumerate(vecs):
        h, l = moments(vec, image)
        found[i, 0] = h
        found[i, 1] = l


def local(vecs, image, high, low):
    more = (BLOCKS, TURNED, TURNED) if len(vecs) == 1 else ()
    return call(
        functools.partial(local_kernel, len(vecs)),
        (BLOCKS, shape(len(vecs), 2, R, N)) + more,
        [VMEM] * (len(vecs) + 3),
        [PIECES],
        flops=2 * ONE_WAY,
    )(*vecs, image, high, low)


def add_received(flag, got_one, got_two, partial, turned_high, turned_low, image, pieces):
    for t in range(T):
        put_pieces(pieces, t, choose(flag, got_one[t], got_two[t]))
        image[t] = partial[t] + choose(flag, got_two[t], got_one[t])
    from_next(pieces, turned_high, turned_low, image)


def step_kernel(flag, got_one, got_two, partial, diag, high, low, turned_high, turned_low, image, vec, one, two, sent, pieces):
    add_received(flag, got_one, got_two, partial, turned_high, turned_low, image, pieces)
    for t in range(T):
        vec[t] = image[t] / diag[t : t + 1, :]
    hand_out(flag, vec, high, low, one, two, sent, pieces)


def next_step(*args):
    return call(step_kernel, (BLOCKS,) * 4, [VMEM] * 9, [SENT, PIECES], flops=2 * ONE_WAY)(*args)


PAIRS = 5


def fold(high, low):
    value = (high, low)
    size = high.shape[0]
    while size > 8:
        size //= 2
        value = dd_add(tuple(v[:size] for v in value), tuple(v[size:] for v in value))
    for turn_by in (4, 2, 1):
        value = dd_add(value, tuple(pltpu.roll(v, turn_by, 0) for v in value))
    return value


def gram_kernel(
    flag, got_one, got_two, partial, turned_high, turned_low, v0, v1, v2, m0, m1, m2, image, out, pieces
):
    add_received(flag, got_one, got_two, partial, turned_high, turned_low, image, pieces)
    last = [moments(v, image) for v in (v0, v1, v2)]
    every = [(m[i, 0], m[i, 1]) for m in (m0, m1, m2) for i in range(m.shape[0])] + last + last[-1:]
    for q in range(PAIRS):
        pair = every[2 * q : 2 * q + 2]
        h, l = fold(*(jnp.concatenate([f[i] for f in pair], axis=0).T for i in range(2)))
        out[:, q * N : (q + 1) * N] = (h + l)[0:1]


def gram(*args):
    return call(gram_kernel, (BLOCKS, shape(1, PAIRS * N)), [VMEM] * 12, [PIECES], flops=ONE_WAY)(*args)


def solve(matrix, right):
    (a00, a01, a02), (a10, a11, a12), (a20, a21, a22) = matrix
    b0, b1, b2 = right
    inv0 = 1.0 / a00
    f1, f2 = a10 * inv0, a20 * inv0
    c11, c12, e1 = a11 - f1 * a01, a12 - f1 * a02, b1 - f1 * b0
    c21, c22, e2 = a21 - f2 * a01, a22 - f2 * a02, b2 - f2 * b0
    inv1 = 1.0 / c11
    g = c21 * inv1
    x2 = (e2 - g * e1) / (c22 - g * c12)
    x1 = (e1 - c12 * x2) * inv1
    x0 = (b0 - a01 * x1 - a02 * x2) * inv0
    return x0, x1, x2


def result_kernel(parts, v0, v1, v2, y0, y1, y2, y3, sol, res):
    flat = []
    for q in range(PAIRS):
        part = parts[:, q * N : (q + 1) * N]
        h, l = (v[0:1] for v in fold(part, jnp.zeros_like(part)))
        flat += [(h, l), (pltpu.roll(h, R, 1), pltpu.roll(l, R, 1))]
    g00, g01, g11, g02, g12, g22, g03, g13, g23 = flat[:9]
    full = ((g00, g01, g02, g03), (g01, g11, g12, g13), (g02, g12, g22, g23))
    minus = lambda a, b: dd_add(a, (-b[0], -b[1]))
    matrix = [[minus(row[j], row[j + 1]) for j in range(3)] for row in full]
    right = [row[1] for row in full]
    near = [[m[0] + m[1] for m in row] for row in matrix]
    coef = [jnp.zeros_like(g00[0])] * 3
    for _ in range(3):
        left = []
        for row, value in zip(matrix, right):
            for m, c in zip(row, coef):
                p, e = two_prod(m[0], c)
                value = minus(value, (p, e + m[1] * c))
            left.append(value[0] + value[1])
        coef = [c + s for c, s in zip(coef, solve(near, left))]
    rows = jnp.concatenate([c[:, :N] for c in coef] + [jnp.zeros((N - 3, N), F32)], axis=0).T
    d0, d1, d2 = (jnp.broadcast_to(rows[:R, i : i + 1], (R, N)) for i in range(3))
    for t in range(T):
        sol[t] = v0[t] + (d0 * v0[t] + d1 * v1[t] + d2 * v2[t])
        first, second = y1[t], y2[t]
        res[t] = first - (d0 * (y0[t] - first) + d1 * (first - second) + d2 * (second - y3[t]))


def result(parts, vecs, images):
    return call(result_kernel, (shape(T, R, N), shape(T, R, N)), [VMEM] * 8)(parts, *vecs, *images)


def shift(value, steps):
    count = lax.axis_size("tm")
    return lax.ppermute(value, "tm", [(i, (i + steps) % count) for i in range(count)])


def all_parts(value):
    count = lax.axis_size("tm")
    half, quarter = count // 2, count // 8
    turns = [*range(half + quarter, count), *range(half - quarter, half + quarter), *range(half - quarter)]
    spread = lax.all_to_all(
        jnp.broadcast_to(value[None], (count,) + value.shape), "tm", 0, 0, axis_index_groups=[turns]
    )
    return spread.reshape(count, value.shape[1])


def swap_within(value):
    return lax.ppermute(value, "tm", [(i, i ^ 1) for i in range(lax.axis_size("tm"))])


def swap_across(value):
    count = lax.axis_size("tm")
    return lax.ppermute(value, "tm", [(i, (i + (1 if i % 2 else -1)) % count) for i in range(count)])


def shards(weights, pattern, shift_reg, rhs):
    flag = jnp.broadcast_to((1 - lax.axis_index("tm") % 2).astype(F32), (8, N))
    flag, pattern = lax.optimization_barrier((flag, pattern))
    inflow = shift(ahead_sums(pattern, weights), 1)
    high, low, own = band_pieces(pattern, weights, shift_reg)
    diag, vec, two = first(rhs, own, inflow, high, low)
    got_two = swap_across(two)
    partial, part, one, *turned = local([vec], rhs, high, low)
    got = swap_within(one), got_two
    vecs, images, found = [vec], [rhs], [part]
    for step in range(2):
        image, vec, one, two = next_step(flag, *got, partial, diag, high, low, *turned)
        got = swap_within(one), swap_across(two)
        images.append(image)
        vecs.append(vec)
        partial, part = local(vecs, image, high, low)
        found.append(part)
    image, part = gram(flag, *got, partial, *turned, *vecs, *found)
    return result(all_parts(part), vecs, images + [image])


def solution(mesh):
    return jax.shard_map(
        shards,
        mesh=mesh,
        in_specs=(P("tm", None, None, None), P("tm", None), P("tm", None), P("tm", "scen", None)),
        out_specs=(P("tm", "scen", None), P("tm", "scen", None)),
        check_vma=False,
    )
```

```python
import functools

import jax
import jax.numpy as jnp
from jax import lax
from jax.experimental import pallas as pl
from jax.experimental.pallas import tpu as pltpu
from jax.sharding import PartitionSpec as P

F32 = jnp.float32
BF16 = jnp.bfloat16
MIB = 1024 * 1024
N = 128
T = 8
R = 64
VMEM = pl.BlockSpec(memory_space=pltpu.VMEM)
HBM = pl.BlockSpec(memory_space=pltpu.HBM)

BAND = (T // 2, 2 * N, (T + 1) * N)


def call(body, outs, specs=None, scratch=(), limit=16, flops=0, moved=0):
    return pl.pallas_call(
        body,
        out_shape=outs,
        in_specs=specs,
        out_specs=jax.tree.map(lambda _: VMEM, outs),
        scratch_shapes=list(scratch),
        compiler_params=pltpu.CompilerParams(vmem_limit_bytes=limit * MIB),
        cost_estimate=pl.CostEstimate(flops=flops, bytes_accessed=moved, transcendentals=0),
    )


def in_hbm(value):
    return pltpu.with_memory_space_constraint(value, pltpu.HBM)


def shape(*dims, dtype=F32):
    return jax.ShapeDtypeStruct(dims, dtype)


def dot(a, b):
    return lax.dot_general(a, b, (((1,), (0,)), ((), ())), preferred_element_type=F32)


def dot_t(a, b):
    return lax.dot_general(a, b, (((1,), (1,)), ((), ())), preferred_element_type=F32)


def two_sum(a, b):
    s = a + b
    t = s - a
    return s, (a - (s - t)) + (b - t)


def dd_add(a, b):
    s, e = two_sum(a[0], b[0])
    return s, e + (a[1] + b[1])


def halves(a):
    t = a * 4097.0
    h = t - (t - a)
    return h, a - h


def two_prod(a, b):
    p = a * b
    ah, al = halves(a)
    bh, bl = halves(b)
    return p, ((ah * bh - p) + ah * bl + al * bh) + al * bl


def ahead_kernel(pattern, weights, ahead, mask, buf, cols, sems):
    head = pltpu.make_async_copy(pattern, mask, sems.at[T])
    head.start()
    copies = []
    for t in range(T):
        some = slice(T - 1 - t, T)
        copies.append(pltpu.make_async_copy(weights.at[t, some], buf.at[t, some], sems.at[t]))
    for copy in copies:
        copy.start()
    for t in range(T):
        copies[t].wait()
        for k in range(T - 1 - t, T):
            cols[t, k] = jnp.sum(buf[t, k].reshape(N // 8, 8, N), axis=0)
    head.wait()
    for b in range(T):
        total = jnp.zeros((8, N), F32)
        for t in range(b, T):
            k = T - 1 - t + b
            total = total + cols[t, k] * mask[t, k].astype(F32)
        ahead[b : b + 1, :] = jnp.sum(total, axis=0, keepdims=True)


def ahead_sums(pattern, weights):
    pattern, weights = in_hbm(pattern), in_hbm(weights)
    return call(
        ahead_kernel,
        shape(T, N),
        [HBM, HBM],
        [
            pltpu.SMEM((T, T), jnp.int32),
            pltpu.VMEM((T, T, N, N), F32),
            pltpu.VMEM((T, T, 8, N), F32),
            pltpu.SemaphoreType.DMA((T + 1,)),
        ],
        flops=4 * T * T * N * N,
        moved=4 * T * T * N * N,
    )(pattern, weights)


def band_kernel(pattern, weights, reg, high, low, own, mask, buf, cols, extra, sems):
    def copy(t):
        return pltpu.make_async_copy(weights.at[t], buf.at[t], sems.at[t])

    head = pltpu.make_async_copy(pattern, mask, sems.at[T])
    tail = pltpu.make_async_copy(reg, extra, sems.at[T + 1])
    head.start()
    for t in range(T):
        copy(t).start()
    tail.start()
    cols[...] = jnp.zeros_like(cols)
    zero = jnp.zeros((N, N), BF16)
    for a in range(T // 2):
        for piece in (high, low):
            piece[a, N : 2 * N, 0:N] = zero
            piece[a, 0:N, T * N : (T + 1) * N] = zero
    head.wait()

    def step(a, carry):
        for half in range(2):
            t = 2 * a + half
            copy(t).wait()
            rows = jnp.zeros((N, N), F32)
            for k in range(T):
                m = buf[t, k] * mask[t, k].astype(F32)
                rows = rows + m
                cols[t + k + 1] += jnp.sum(m.reshape(N // 8, 8, N), axis=0)
                h = m.astype(BF16)
                place = slice((k + half) * N, (k + half + 1) * N)
                high[a, half * N : (half + 1) * N, place] = h
                low[a, half * N : (half + 1) * N, place] = (m - h.astype(F32)).astype(BF16)
            own[pl.ds(t, 1), :] = jnp.sum(rows.T, axis=0, keepdims=True)
        return carry

    lax.fori_loop(0, T // 2, step, 0)
    tail.wait()
    own[...] += jnp.sum(cols[:T], axis=1) + extra[...]


def band_pieces(pattern, weights, reg):
    pattern, weights, reg = in_hbm(pattern), in_hbm(weights), in_hbm(reg)
    return call(
        band_kernel,
        (shape(*BAND, dtype=BF16), shape(*BAND, dtype=BF16), shape(T, N)),
        [HBM, HBM, HBM],
        [
            pltpu.SMEM((T, T), jnp.int32),
            pltpu.VMEM((T, T, N, N), F32),
            pltpu.VMEM((2 * T, 8, N), F32),
            pltpu.VMEM((T, N), F32),
            pltpu.SemaphoreType.DMA((T + 2,)),
        ],
        flops=2048 * T * T * N * N,
        moved=8 * T * T * N * N,
    )(pattern, weights, reg)


def put_pieces(pieces, t, value):
    h = value.astype(BF16)
    pieces[0:R, t * N : (t + 1) * N] = h
    pieces[R : 2 * R, t * N : (t + 1) * N] = (value - h.astype(F32)).astype(BF16)


def product(pieces, cols, high, low, mult):
    both = mult(pieces[:, cols], high)
    return (both[:R] + mult(pieces[0:R, cols], low)) + both[R:]


def to_next(pieces, high, low, out):
    for b in range(T // 2):
        total = None
        for a in range(b, T // 2):
            at = slice((7 + 2 * b - 2 * a) * N, (9 + 2 * b - 2 * a) * N)
            term = product(pieces, slice(a * 2 * N, (a + 1) * 2 * N), high[a, :, at], low[a, :, at], dot)
            total = term if total is None else total + term
        out[2 * b] = total[:, :N]
        out[2 * b + 1] = total[:, N:]


def within(pieces, high, low, out):
    out[0] = jnp.zeros((R, N), F32)
    for p in range(T // 2):
        total = None
        width = 2 * N if p < T // 2 - 1 else N
        for a in range(p + 1):
            at = slice(2 * (p - a) * N, 2 * (p - a) * N + width)
            term = product(pieces, slice(a * 2 * N, (a + 1) * 2 * N), high[a, :, at], low[a, :, at], dot)
            total = term if total is None else total + term
        out[2 * p + 1] = total[:, :N]
        if width > N:
            out[2 * p + 2] = total[:, N:]
    for a in range(T // 2):
        at = slice(0, (7 - 2 * a) * N)
        term = product(pieces, slice((2 * a + 1) * N, T * N), high[a, :, at], low[a, :, at], dot_t)
        out[2 * a] += term[:, :N]
        out[2 * a + 1] += term[:, N:]


def turned_rows(a):
    return slice(a * (a + 1) * N, (a + 1) * (a + 2) * N)


def turn(high, low, turned_high, turned_low):
    for piece, out in ((high, turned_high), (low, turned_low)):
        for a in range(T // 2):
            out[turned_rows(a), :] = piece[a, :, (7 - 2 * a) * N :].T


def from_next(pieces, high, low, out):
    for a in range(T // 2):
        rows = turned_rows(a)
        term = product(pieces, slice(0, (2 * a + 2) * N), high[rows, :], low[rows, :], dot)
        out[2 * a] += term[:, :N]
        out[2 * a + 1] += term[:, N:]


def moments(first, second):
    high = low = jnp.zeros((R, N), F32)
    for t in range(T):
        high, err = two_sum(high, first[t] * second[t])
        low = low + err
    return high, low


PIECES = pltpu.VMEM((2 * R, T * N), BF16)
ONE_WAY = 2 * 3 * 40 * R * N * N


def choose(flag, first, second):
    return jnp.where(jnp.broadcast_to(flag[0:1, :], (R, N)) > 0, first, second)


def hand_out(flag, vec, high, low, one, two, sent, pieces):
    for t in range(T):
        put_pieces(pieces, t, vec[t])
    to_next(pieces, high, low, sent)
    for t in range(T):
        one[t] = choose(flag, sent[t], vec[t])
        two[t] = choose(flag, vec[t], sent[t])


BLOCKS = shape(T, R, N)
SENT = pltpu.VMEM((T, R, N), F32)
TURNED = shape((T // 2) * (T // 2 + 1) * N, 2 * N, dtype=BF16)


def on_parity(parity):
    return pl.when(lax.axis_index("tm") % 2 == parity)


def first_kernel(rhs, own, inflow, high, low, diag, vec, two, pieces):
    diag[...] = own[...] + inflow[...]

    @on_parity(0)
    def _():
        for t in range(T):
            value = rhs[t] / diag[t : t + 1, :]
            vec[t] = value
            two[t] = value

    @on_parity(1)
    def _():
        for t in range(T):
            value = rhs[t] / diag[t : t + 1, :]
            vec[t] = value
            put_pieces(pieces, t, value)
        to_next(pieces, high, low, two)


def first(*args):
    return call(first_kernel, (shape(T, N), BLOCKS, BLOCKS), [VMEM] * 5, [PIECES], flops=ONE_WAY)(*args)


def local_kernel(count, *refs):
    vecs, (image, high, low, out, found, *more, pieces) = refs[:count], refs[count:]
    for t in range(T):
        put_pieces(pieces, t, vecs[-1][t])
    if more:
        one, *turned = more

        @on_parity(0)
        def _():
            to_next(pieces, high, low, one)

        @on_parity(1)
        def _():
            one[...] = vecs[0][...]

        turn(high, low, *turned)
    within(pieces, high, low, out)
    for i, vec in enumerate(vecs):
        h, l = moments(vec, image)
        found[i, 0] = h
        found[i, 1] = l


def local(vecs, image, high, low):
    more = (BLOCKS, TURNED, TURNED) if len(vecs) == 1 else ()
    return call(
        functools.partial(local_kernel, len(vecs)),
        (BLOCKS, shape(len(vecs), 2, R, N)) + more,
        [VMEM] * (len(vecs) + 3),
        [PIECES],
        flops=2 * ONE_WAY,
    )(*vecs, image, high, low)


def add_received(flag, got_one, got_two, partial, turned_high, turned_low, image, pieces):
    for t in range(T):
        put_pieces(pieces, t, choose(flag, got_one[t], got_two[t]))
        image[t] = partial[t] + choose(flag, got_two[t], got_one[t])
    from_next(pieces, turned_high, turned_low, image)


def step_kernel(flag, got_one, got_two, partial, diag, high, low, turned_high, turned_low, image, vec, one, two, sent, pieces):
    add_received(flag, got_one, got_two, partial, turned_high, turned_low, image, pieces)
    for t in range(T):
        vec[t] = image[t] / diag[t : t + 1, :]
    hand_out(flag, vec, high, low, one, two, sent, pieces)


def next_step(*args):
    return call(step_kernel, (BLOCKS,) * 4, [VMEM] * 9, [SENT, PIECES], flops=2 * ONE_WAY)(*args)


PAIRS = 5


def fold(high, low):
    value = (high, low)
    size = high.shape[0]
    while size > 8:
        size //= 2
        value = dd_add(tuple(v[:size] for v in value), tuple(v[size:] for v in value))
    for turn_by in (4, 2, 1):
        value = dd_add(value, tuple(pltpu.roll(v, turn_by, 0) for v in value))
    return value


def gram_kernel(
    flag, got_one, got_two, partial, turned_high, turned_low, v0, v1, v2, m0, m1, m2, image, out, pieces
):
    add_received(flag, got_one, got_two, partial, turned_high, turned_low, image, pieces)
    last = [moments(v, image) for v in (v0, v1, v2)]
    every = [(m[i, 0], m[i, 1]) for m in (m0, m1, m2) for i in range(m.shape[0])] + last + last[-1:]
    for q in range(PAIRS):
        pair = every[2 * q : 2 * q + 2]
        h, l = fold(*(jnp.concatenate([f[i] for f in pair], axis=0).T for i in range(2)))
        out[:, q * N : (q + 1) * N] = (h + l)[0:1]


def gram(*args):
    return call(gram_kernel, (BLOCKS, shape(1, PAIRS * N)), [VMEM] * 12, [PIECES], flops=ONE_WAY)(*args)


def solve(matrix, right):
    (a00, a01, a02), (a10, a11, a12), (a20, a21, a22) = matrix
    b0, b1, b2 = right
    inv0 = 1.0 / a00
    f1, f2 = a10 * inv0, a20 * inv0
    c11, c12, e1 = a11 - f1 * a01, a12 - f1 * a02, b1 - f1 * b0
    c21, c22, e2 = a21 - f2 * a01, a22 - f2 * a02, b2 - f2 * b0
    inv1 = 1.0 / c11
    g = c21 * inv1
    x2 = (e2 - g * e1) / (c22 - g * c12)
    x1 = (e1 - c12 * x2) * inv1
    x0 = (b0 - a01 * x1 - a02 * x2) * inv0
    return x0, x1, x2


def result_kernel(parts, v0, v1, v2, y0, y1, y2, y3, sol, res):
    flat = []
    for q in range(PAIRS):
        part = parts[:, q * N : (q + 1) * N]
        h, l = (v[0:1] for v in fold(part, jnp.zeros_like(part)))
        flat += [(h, l), (pltpu.roll(h, R, 1), pltpu.roll(l, R, 1))]
    g00, g01, g11, g02, g12, g22, g03, g13, g23 = flat[:9]
    full = ((g00, g01, g02, g03), (g01, g11, g12, g13), (g02, g12, g22, g23))
    minus = lambda a, b: dd_add(a, (-b[0], -b[1]))
    matrix = [[minus(row[j], row[j + 1]) for j in range(3)] for row in full]
    right = [row[1] for row in full]
    near = [[m[0] + m[1] for m in row] for row in matrix]
    coef = [jnp.zeros_like(g00[0])] * 3
    for _ in range(3):
        left = []
        for row, value in zip(matrix, right):
            for m, c in zip(row, coef):
                p, e = two_prod(m[0], c)
                value = minus(value, (p, e + m[1] * c))
            left.append(value[0] + value[1])
        coef = [c + s for c, s in zip(coef, solve(near, left))]
    rows = jnp.concatenate([c[:, :N] for c in coef] + [jnp.zeros((N - 3, N), F32)], axis=0).T
    d0, d1, d2 = (jnp.broadcast_to(rows[:R, i : i + 1], (R, N)) for i in range(3))
    for t in range(T):
        sol[t] = v0[t] + (d0 * v0[t] + d1 * v1[t] + d2 * v2[t])
        first, second = y1[t], y2[t]
        res[t] = first - (d0 * (y0[t] - first) + d1 * (first - second) + d2 * (second - y3[t]))


def result(parts, vecs, images):
    return call(result_kernel, (shape(T, R, N), shape(T, R, N)), [VMEM] * 8)(parts, *vecs, *images)


def shift(value, steps):
    count = lax.axis_size("tm")
    return lax.ppermute(value, "tm", [(i, (i + steps) % count) for i in range(count)])


def all_parts(value):
    count = lax.axis_size("tm")
    half, eighth = count // 2, count // 8
    last = [half - 1, half]
    near = [i for i in range(half - eighth, half + eighth) if i not in last]
    turns = [*range(half + eighth, count), *near, *last, *range(half - eighth)]
    spread = lax.all_to_all(
        jnp.broadcast_to(value[None], (count,) + value.shape), "tm", 0, 0, axis_index_groups=[turns]
    )
    return spread.reshape(count, value.shape[1])


def swap_within(value):
    return lax.ppermute(value, "tm", [(i, i ^ 1) for i in range(lax.axis_size("tm"))])


def swap_across(value):
    count = lax.axis_size("tm")
    return lax.ppermute(value, "tm", [(i, (i + (1 if i % 2 else -1)) % count) for i in range(count)])


def shards(weights, pattern, shift_reg, rhs):
    flag = jnp.broadcast_to((1 - lax.axis_index("tm") % 2).astype(F32), (8, N))
    flag, pattern = lax.optimization_barrier((flag, pattern))
    inflow = shift(ahead_sums(pattern, weights), 1)
    high, low, own = band_pieces(pattern, weights, shift_reg)
    diag, vec, two = first(rhs, own, inflow, high, low)
    got_two = swap_across(two)
    partial, part, one, *turned = local([vec], rhs, high, low)
    got = swap_within(one), got_two
    vecs, images, found = [vec], [rhs], [part]
    for step in range(2):
        image, vec, one, two = next_step(flag, *got, partial, diag, high, low, *turned)
        got = swap_within(one), swap_across(two)
        images.append(image)
        vecs.append(vec)
        partial, part = local(vecs, image, high, low)
        found.append(part)
    image, part = gram(flag, *got, partial, *turned, *vecs, *found)
    return result(all_parts(part), vecs, images + [image])


def solution(mesh):
    return jax.shard_map(
        shards,
        mesh=mesh,
        in_specs=(P("tm", None, None, None), P("tm", None), P("tm", None), P("tm", "scen", None)),
        out_specs=(P("tm", "scen", None), P("tm", "scen", None)),
        check_vma=False,
    )
```

```python
import functools

import jax
import jax.numpy as jnp
from jax import lax
from jax.experimental import pallas as pl
from jax.experimental.pallas import tpu as pltpu
from jax.sharding import PartitionSpec as P

F32 = jnp.float32
BF16 = jnp.bfloat16
MIB = 1024 * 1024
N = 128
T = 8
R = 64
VMEM = pl.BlockSpec(memory_space=pltpu.VMEM)
HBM = pl.BlockSpec(memory_space=pltpu.HBM)

BAND = (T // 2, 2 * N, (T + 1) * N)


def call(body, outs, specs=None, scratch=(), limit=16, flops=0, moved=0):
    return pl.pallas_call(
        body,
        out_shape=outs,
        in_specs=specs,
        out_specs=jax.tree.map(lambda _: VMEM, outs),
        scratch_shapes=list(scratch),
        compiler_params=pltpu.CompilerParams(vmem_limit_bytes=limit * MIB),
        cost_estimate=pl.CostEstimate(flops=flops, bytes_accessed=moved, transcendentals=0),
    )


def in_hbm(value):
    return pltpu.with_memory_space_constraint(value, pltpu.HBM)


def shape(*dims, dtype=F32):
    return jax.ShapeDtypeStruct(dims, dtype)


BLOCKS = shape(T, R, N)
TURNED = shape((T // 2) * (T // 2 + 1) * N, 2 * N, dtype=BF16)


def dot(a, b):
    return lax.dot_general(a, b, (((1,), (0,)), ((), ())), preferred_element_type=F32)


def dot_t(a, b):
    return lax.dot_general(a, b, (((1,), (1,)), ((), ())), preferred_element_type=F32)


def two_sum(a, b):
    s = a + b
    t = s - a
    return s, (a - (s - t)) + (b - t)


def dd_add(a, b):
    s, e = two_sum(a[0], b[0])
    return s, e + (a[1] + b[1])


def halves(a):
    t = a * 4097.0
    h = t - (t - a)
    return h, a - h


def two_prod(a, b):
    p = a * b
    ah, al = halves(a)
    bh, bl = halves(b)
    return p, ((ah * bh - p) + ah * bl + al * bh) + al * bl


def ahead_kernel(pattern, weights, ahead, mask, buf, cols, sems):
    head = pltpu.make_async_copy(pattern, mask, sems.at[T])
    head.start()
    copies = []
    for t in range(T):
        some = slice(T - 1 - t, T)
        copies.append(pltpu.make_async_copy(weights.at[t, some], buf.at[t, some], sems.at[t]))
    for copy in copies:
        copy.start()
    for t in range(T):
        copies[t].wait()
        for k in range(T - 1 - t, T):
            cols[t, k] = jnp.sum(buf[t, k].reshape(N // 8, 8, N), axis=0)
    head.wait()
    for b in range(T):
        total = jnp.zeros((8, N), F32)
        for t in range(b, T):
            k = T - 1 - t + b
            total = total + cols[t, k] * mask[t, k].astype(F32)
        ahead[b : b + 1, :] = jnp.sum(total, axis=0, keepdims=True)


def ahead_sums(pattern, weights):
    pattern, weights = in_hbm(pattern), in_hbm(weights)
    return call(
        ahead_kernel,
        shape(T, N),
        [HBM, HBM],
        [
            pltpu.SMEM((T, T), jnp.int32),
            pltpu.VMEM((T, T, N, N), F32),
            pltpu.VMEM((T, T, 8, N), F32),
            pltpu.SemaphoreType.DMA((T + 1,)),
        ],
        flops=4 * T * T * N * N,
        moved=4 * T * T * N * N,
    )(pattern, weights)


def band_kernel(pattern, weights, reg, high, low, own, turned_high, turned_low, mask, buf, cols, extra, sems):
    def copy(t):
        return pltpu.make_async_copy(weights.at[t], buf.at[t], sems.at[t])

    head = pltpu.make_async_copy(pattern, mask, sems.at[T])
    tail = pltpu.make_async_copy(reg, extra, sems.at[T + 1])
    head.start()
    for t in range(T):
        copy(t).start()
    tail.start()
    cols[...] = jnp.zeros_like(cols)
    zero = jnp.zeros((N, N), BF16)
    for a in range(T // 2):
        for piece in (high, low):
            piece[a, N : 2 * N, 0:N] = zero
            piece[a, 0:N, T * N : (T + 1) * N] = zero
    head.wait()

    def step(a, carry):
        for half in range(2):
            t = 2 * a + half
            copy(t).wait()
            rows = jnp.zeros((N, N), F32)
            for k in range(T):
                m = buf[t, k] * mask[t, k].astype(F32)
                rows = rows + m
                cols[t + k + 1] += jnp.sum(m.reshape(N // 8, 8, N), axis=0)
                h = m.astype(BF16)
                place = slice((k + half) * N, (k + half + 1) * N)
                high[a, half * N : (half + 1) * N, place] = h
                low[a, half * N : (half + 1) * N, place] = (m - h.astype(F32)).astype(BF16)
            own[pl.ds(t, 1), :] = jnp.sum(rows.T, axis=0, keepdims=True)
        return carry

    lax.fori_loop(0, T // 2, step, 0)
    tail.wait()
    own[...] += jnp.sum(cols[:T], axis=1) + extra[...]
    turn(high, low, turned_high, turned_low)


def band_pieces(pattern, weights, reg):
    pattern, weights, reg = in_hbm(pattern), in_hbm(weights), in_hbm(reg)
    return call(
        band_kernel,
        (shape(*BAND, dtype=BF16), shape(*BAND, dtype=BF16), shape(T, N), TURNED, TURNED),
        [HBM, HBM, HBM],
        [
            pltpu.SMEM((T, T), jnp.int32),
            pltpu.VMEM((T, T, N, N), F32),
            pltpu.VMEM((2 * T, 8, N), F32),
            pltpu.VMEM((T, N), F32),
            pltpu.SemaphoreType.DMA((T + 2,)),
        ],
        flops=2048 * T * T * N * N,
        moved=8 * T * T * N * N,
    )(pattern, weights, reg)


def put_pieces(pieces, t, value):
    h = value.astype(BF16)
    pieces[0:R, t * N : (t + 1) * N] = h
    pieces[R : 2 * R, t * N : (t + 1) * N] = (value - h.astype(F32)).astype(BF16)


def product(pieces, cols, high, low, mult):
    both = mult(pieces[:, cols], high)
    return (both[:R] + mult(pieces[0:R, cols], low)) + both[R:]


def to_next(pieces, high, low, out):
    for b in range(T // 2):
        total = None
        for a in range(b, T // 2):
            at = slice((7 + 2 * b - 2 * a) * N, (9 + 2 * b - 2 * a) * N)
            term = product(pieces, slice(a * 2 * N, (a + 1) * 2 * N), high[a, :, at], low[a, :, at], dot)
            total = term if total is None else total + term
        out[2 * b] = total[:, :N]
        out[2 * b + 1] = total[:, N:]


def within(pieces, high, low, out):
    out[0] = jnp.zeros((R, N), F32)
    for p in range(T // 2):
        total = None
        width = 2 * N if p < T // 2 - 1 else N
        for a in range(p + 1):
            at = slice(2 * (p - a) * N, 2 * (p - a) * N + width)
            term = product(pieces, slice(a * 2 * N, (a + 1) * 2 * N), high[a, :, at], low[a, :, at], dot)
            total = term if total is None else total + term
        out[2 * p + 1] = total[:, :N]
        if width > N:
            out[2 * p + 2] = total[:, N:]
    for a in range(T // 2):
        at = slice(0, (7 - 2 * a) * N)
        term = product(pieces, slice((2 * a + 1) * N, T * N), high[a, :, at], low[a, :, at], dot_t)
        out[2 * a] += term[:, :N]
        out[2 * a + 1] += term[:, N:]


def turned_rows(a):
    return slice(a * (a + 1) * N, (a + 1) * (a + 2) * N)


def turn(high, low, turned_high, turned_low):
    for piece, out in ((high, turned_high), (low, turned_low)):
        for a in range(T // 2):
            out[turned_rows(a), :] = piece[a, :, (7 - 2 * a) * N :].T


def from_next(pieces, high, low, out):
    for a in range(T // 2):
        rows = turned_rows(a)
        term = product(pieces, slice(0, (2 * a + 2) * N), high[rows, :], low[rows, :], dot)
        out[2 * a] += term[:, :N]
        out[2 * a + 1] += term[:, N:]


def moments(first, second):
    high = low = jnp.zeros((R, N), F32)
    for t in range(T):
        high, err = two_sum(high, first[t] * second[t])
        low = low + err
    return high, low


PIECES = pltpu.VMEM((2 * R, T * N), BF16)
ONE_WAY = 2 * 3 * 40 * R * N * N


def on_parity(parity):
    return pl.when(lax.axis_index("tm") % 2 == parity)


def hand_out(vec, high, low, one, two, pieces):
    for t in range(T):
        put_pieces(pieces, t, vec[t])

    @on_parity(0)
    def _():
        to_next(pieces, high, low, one)
        two[...] = vec[...]

    @on_parity(1)
    def _():
        to_next(pieces, high, low, two)
        one[...] = vec[...]


def first_kernel(rhs, own, inflow, high, low, diag, vec, two, pieces):
    diag[...] = own[...] + inflow[...]

    @on_parity(0)
    def _():
        for t in range(T):
            value = rhs[t] / diag[t : t + 1, :]
            vec[t] = value
            two[t] = value

    @on_parity(1)
    def _():
        for t in range(T):
            value = rhs[t] / diag[t : t + 1, :]
            vec[t] = value
            put_pieces(pieces, t, value)
        to_next(pieces, high, low, two)


def first(*args):
    return call(first_kernel, (shape(T, N), BLOCKS, BLOCKS), [VMEM] * 5, [PIECES], flops=ONE_WAY)(*args)


def local_kernel(count, *refs):
    vecs, (image, high, low, out, found, *more, pieces) = refs[:count], refs[count:]
    for t in range(T):
        put_pieces(pieces, t, vecs[-1][t])
    if more:
        (one,) = more

        @on_parity(0)
        def _():
            to_next(pieces, high, low, one)

        @on_parity(1)
        def _():
            one[...] = vecs[0][...]

    within(pieces, high, low, out)
    for i, vec in enumerate(vecs):
        h, l = moments(vec, image)
        found[i, 0] = h
        found[i, 1] = l


def local(vecs, image, high, low):
    more = (BLOCKS,) if len(vecs) == 1 else ()
    return call(
        functools.partial(local_kernel, len(vecs)),
        (BLOCKS, shape(len(vecs), 2, R, N)) + more,
        [VMEM] * (len(vecs) + 3),
        [PIECES],
        flops=2 * ONE_WAY,
    )(*vecs, image, high, low)


def add_received(got_one, got_two, partial, turned_high, turned_low, image, pieces):
    for parity, ahead, arrived in ((0, got_one, got_two), (1, got_two, got_one)):

        @on_parity(parity)
        def _():
            for t in range(T):
                put_pieces(pieces, t, ahead[t])
                image[t] = partial[t] + arrived[t]

    from_next(pieces, turned_high, turned_low, image)


def step_kernel(got_one, got_two, partial, diag, high, low, turned_high, turned_low, image, vec, one, two, pieces):
    add_received(got_one, got_two, partial, turned_high, turned_low, image, pieces)
    for t in range(T):
        vec[t] = image[t] / diag[t : t + 1, :]
    hand_out(vec, high, low, one, two, pieces)


def next_step(*args):
    return call(step_kernel, (BLOCKS,) * 4, [VMEM] * 8, [PIECES], flops=2 * ONE_WAY)(*args)


PAIRS = 5


def fold(high, low):
    value = (high, low)
    size = high.shape[0]
    while size > 8:
        size //= 2
        value = dd_add(tuple(v[:size] for v in value), tuple(v[size:] for v in value))
    for turn_by in (4, 2, 1):
        value = dd_add(value, tuple(pltpu.roll(v, turn_by, 0) for v in value))
    return value


def gram_kernel(
    got_one, got_two, partial, turned_high, turned_low, v0, v1, v2, m0, m1, m2, image, out, pieces
):
    add_received(got_one, got_two, partial, turned_high, turned_low, image, pieces)
    last = [moments(v, image) for v in (v0, v1, v2)]
    every = [(m[i, 0], m[i, 1]) for m in (m0, m1, m2) for i in range(m.shape[0])] + last + last[-1:]
    for q in range(PAIRS):
        pair = every[2 * q : 2 * q + 2]
        h, l = fold(*(jnp.concatenate([f[i] for f in pair], axis=0).T for i in range(2)))
        out[:, q * N : (q + 1) * N] = (h + l)[0:1]


def gram(*args):
    return call(gram_kernel, (BLOCKS, shape(1, PAIRS * N)), [VMEM] * 11, [PIECES], flops=ONE_WAY)(*args)


def solve(matrix, right):
    (a00, a01, a02), (a10, a11, a12), (a20, a21, a22) = matrix
    b0, b1, b2 = right
    inv0 = 1.0 / a00
    f1, f2 = a10 * inv0, a20 * inv0
    c11, c12, e1 = a11 - f1 * a01, a12 - f1 * a02, b1 - f1 * b0
    c21, c22, e2 = a21 - f2 * a01, a22 - f2 * a02, b2 - f2 * b0
    inv1 = 1.0 / c11
    g = c21 * inv1
    x2 = (e2 - g * e1) / (c22 - g * c12)
    x1 = (e1 - c12 * x2) * inv1
    x0 = (b0 - a01 * x1 - a02 * x2) * inv0
    return x0, x1, x2


def result_kernel(parts, v0, v1, v2, y0, y1, y2, y3, sol, res):
    flat = []
    for q in range(PAIRS):
        part = parts[:, q * N : (q + 1) * N]
        h, l = (v[0:1] for v in fold(part, jnp.zeros_like(part)))
        flat += [(h, l), (pltpu.roll(h, R, 1), pltpu.roll(l, R, 1))]
    g00, g01, g11, g02, g12, g22, g03, g13, g23 = flat[:9]
    full = ((g00, g01, g02, g03), (g01, g11, g12, g13), (g02, g12, g22, g23))
    minus = lambda a, b: dd_add(a, (-b[0], -b[1]))
    matrix = [[minus(row[j], row[j + 1]) for j in range(3)] for row in full]
    right = [row[1] for row in full]
    near = [[m[0] + m[1] for m in row] for row in matrix]
    coef = [jnp.zeros_like(g00[0])] * 3
    for _ in range(3):
        left = []
        for row, value in zip(matrix, right):
            for m, c in zip(row, coef):
                p, e = two_prod(m[0], c)
                value = minus(value, (p, e + m[1] * c))
            left.append(value[0] + value[1])
        coef = [c + s for c, s in zip(coef, solve(near, left))]
    rows = jnp.concatenate([c[:, :N] for c in coef] + [jnp.zeros((N - 3, N), F32)], axis=0).T
    d0, d1, d2 = (jnp.broadcast_to(rows[:R, i : i + 1], (R, N)) for i in range(3))
    for t in range(T):
        sol[t] = v0[t] + (d0 * v0[t] + d1 * v1[t] + d2 * v2[t])
        first, second = y1[t], y2[t]
        res[t] = first - (d0 * (y0[t] - first) + d1 * (first - second) + d2 * (second - y3[t]))


def result(parts, vecs, images):
    return call(result_kernel, (shape(T, R, N), shape(T, R, N)), [VMEM] * 8)(parts, *vecs, *images)


def shift(value, steps):
    count = lax.axis_size("tm")
    return lax.ppermute(value, "tm", [(i, (i + steps) % count) for i in range(count)])


def all_parts(value):
    count = lax.axis_size("tm")
    last = [count // 2 - 1, count // 2]
    turns = sorted(range(count), key=lambda i: (i in last, 2 * (i // 8) + 3 * (i % 4), i))
    spread = lax.all_to_all(
        jnp.broadcast_to(value[None], (count,) + value.shape), "tm", 0, 0, axis_index_groups=[turns]
    )
    return spread.reshape(count, value.shape[1])


def swap_within(value):
    return lax.ppermute(value, "tm", [(i, i ^ 1) for i in range(lax.axis_size("tm"))])


def swap_across(value):
    count = lax.axis_size("tm")
    return lax.ppermute(value, "tm", [(i, (i + (1 if i % 2 else -1)) % count) for i in range(count)])


def shards(weights, pattern, shift_reg, rhs):
    inflow = shift(ahead_sums(pattern, weights), 1)
    high, low, own, *turned = band_pieces(pattern, weights, shift_reg)
    diag, vec, two = first(rhs, own, inflow, high, low)
    got_two = swap_across(two)
    partial, part, one = local([vec], rhs, high, low)
    got = swap_within(one), got_two
    vecs, images, found = [vec], [rhs], [part]
    for step in range(2):
        image, vec, one, two = next_step(*got, partial, diag, high, low, *turned)
        got = swap_within(one), swap_across(two)
        images.append(image)
        vecs.append(vec)
        partial, part = local(vecs, image, high, low)
        found.append(part)
    image, part = gram(*got, partial, *turned, *vecs, *found)
    return result(all_parts(part), vecs, images + [image])


def solution(mesh):
    return jax.shard_map(
        shards,
        mesh=mesh,
        in_specs=(P("tm", None, None, None), P("tm", None), P("tm", None), P("tm", "scen", None)),
        out_specs=(P("tm", "scen", None), P("tm", "scen", None)),
        check_vma=False,
    )
```

```python
import functools

import jax
import jax.numpy as jnp
from jax import lax
from jax.experimental import pallas as pl
from jax.experimental.pallas import tpu as pltpu
from jax.sharding import PartitionSpec as P

F32 = jnp.float32
BF16 = jnp.bfloat16
MIB = 1024 * 1024
N = 128
T = 8
R = 64
VMEM = pl.BlockSpec(memory_space=pltpu.VMEM)
HBM = pl.BlockSpec(memory_space=pltpu.HBM)

BAND = (T // 2, 2 * N, (T + 1) * N)


def call(body, outs, specs=None, scratch=(), limit=16, flops=0, moved=0):
    return pl.pallas_call(
        body,
        out_shape=outs,
        in_specs=specs,
        out_specs=jax.tree.map(lambda _: VMEM, outs),
        scratch_shapes=list(scratch),
        compiler_params=pltpu.CompilerParams(vmem_limit_bytes=limit * MIB),
        cost_estimate=pl.CostEstimate(flops=flops, bytes_accessed=moved, transcendentals=0),
    )


def in_hbm(value):
    return pltpu.with_memory_space_constraint(value, pltpu.HBM)


def shape(*dims, dtype=F32):
    return jax.ShapeDtypeStruct(dims, dtype)


def dot(a, b):
    return lax.dot_general(a, b, (((1,), (0,)), ((), ())), preferred_element_type=F32)


def dot_t(a, b):
    return lax.dot_general(a, b, (((1,), (1,)), ((), ())), preferred_element_type=F32)


def two_sum(a, b):
    s = a + b
    t = s - a
    return s, (a - (s - t)) + (b - t)


def dd_add(a, b):
    s, e = two_sum(a[0], b[0])
    return s, e + (a[1] + b[1])


def halves(a):
    t = a * 4097.0
    h = t - (t - a)
    return h, a - h


def two_prod(a, b):
    p = a * b
    ah, al = halves(a)
    bh, bl = halves(b)
    return p, ((ah * bh - p) + ah * bl + al * bh) + al * bl


def ahead_kernel(pattern, weights, ahead, mask, buf, cols, sems):
    head = pltpu.make_async_copy(pattern, mask, sems.at[T])
    head.start()
    copies = []
    for t in range(T):
        some = slice(T - 1 - t, T)
        copies.append(pltpu.make_async_copy(weights.at[t, some], buf.at[t, some], sems.at[t]))
    for copy in copies:
        copy.start()
    for t in range(T):
        copies[t].wait()
        for k in range(T - 1 - t, T):
            cols[t, k] = jnp.sum(buf[t, k].reshape(N // 8, 8, N), axis=0)
    head.wait()
    for b in range(T):
        total = jnp.zeros((8, N), F32)
        for t in range(b, T):
            k = T - 1 - t + b
            total = total + cols[t, k] * mask[t, k].astype(F32)
        ahead[b : b + 1, :] = jnp.sum(total, axis=0, keepdims=True)


def ahead_sums(pattern, weights):
    pattern, weights = in_hbm(pattern), in_hbm(weights)
    return call(
        ahead_kernel,
        shape(T, N),
        [HBM, HBM],
        [
            pltpu.SMEM((T, T), jnp.int32),
            pltpu.VMEM((T, T, N, N), F32),
            pltpu.VMEM((T, T, 8, N), F32),
            pltpu.SemaphoreType.DMA((T + 1,)),
        ],
        flops=4 * T * T * N * N,
        moved=4 * T * T * N * N,
    )(pattern, weights)


def band_kernel(pattern, weights, reg, high, low, own, mask, buf, cols, extra, sems):
    def copy(t):
        return pltpu.make_async_copy(weights.at[t], buf.at[t], sems.at[t])

    head = pltpu.make_async_copy(pattern, mask, sems.at[T])
    tail = pltpu.make_async_copy(reg, extra, sems.at[T + 1])
    head.start()
    for t in range(T):
        copy(t).start()
    tail.start()
    cols[...] = jnp.zeros_like(cols)
    zero = jnp.zeros((N, N), BF16)
    for a in range(T // 2):
        for piece in (high, low):
            piece[a, N : 2 * N, 0:N] = zero
            piece[a, 0:N, T * N : (T + 1) * N] = zero
    head.wait()

    def step(a, carry):
        for half in range(2):
            t = 2 * a + half
            copy(t).wait()
            rows = jnp.zeros((N, N), F32)
            for k in range(T):
                m = buf[t, k] * mask[t, k].astype(F32)
                rows = rows + m
                cols[t + k + 1] += jnp.sum(m.reshape(N // 8, 8, N), axis=0)
                h = m.astype(BF16)
                place = slice((k + half) * N, (k + half + 1) * N)
                high[a, half * N : (half + 1) * N, place] = h
                low[a, half * N : (half + 1) * N, place] = (m - h.astype(F32)).astype(BF16)
            own[pl.ds(t, 1), :] = jnp.sum(rows.T, axis=0, keepdims=True)
        return carry

    lax.fori_loop(0, T // 2, step, 0)
    tail.wait()
    own[...] += jnp.sum(cols[:T], axis=1) + extra[...]


def band_pieces(pattern, weights, reg):
    pattern, weights, reg = in_hbm(pattern), in_hbm(weights), in_hbm(reg)
    return call(
        band_kernel,
        (shape(*BAND, dtype=BF16), shape(*BAND, dtype=BF16), shape(T, N)),
        [HBM, HBM, HBM],
        [
            pltpu.SMEM((T, T), jnp.int32),
            pltpu.VMEM((T, T, N, N), F32),
            pltpu.VMEM((2 * T, 8, N), F32),
            pltpu.VMEM((T, N), F32),
            pltpu.SemaphoreType.DMA((T + 2,)),
        ],
        flops=2048 * T * T * N * N,
        moved=8 * T * T * N * N,
    )(pattern, weights, reg)


def put_pieces(pieces, t, value):
    h = value.astype(BF16)
    pieces[0:R, t * N : (t + 1) * N] = h
    pieces[R : 2 * R, t * N : (t + 1) * N] = (value - h.astype(F32)).astype(BF16)


def product(pieces, cols, high, low, mult):
    both = mult(pieces[:, cols], high)
    return (both[:R] + mult(pieces[0:R, cols], low)) + both[R:]


def to_next(pieces, high, low, out):
    for b in range(T // 2):
        total = None
        for a in range(b, T // 2):
            at = slice((7 + 2 * b - 2 * a) * N, (9 + 2 * b - 2 * a) * N)
            term = product(pieces, slice(a * 2 * N, (a + 1) * 2 * N), high[a, :, at], low[a, :, at], dot)
            total = term if total is None else total + term
        out[2 * b] = total[:, :N]
        out[2 * b + 1] = total[:, N:]


def within(pieces, high, low, out):
    out[0] = jnp.zeros((R, N), F32)
    for p in range(T // 2):
        total = None
        width = 2 * N if p < T // 2 - 1 else N
        for a in range(p + 1):
            at = slice(2 * (p - a) * N, 2 * (p - a) * N + width)
            term = product(pieces, slice(a * 2 * N, (a + 1) * 2 * N), high[a, :, at], low[a, :, at], dot)
            total = term if total is None else total + term
        out[2 * p + 1] = total[:, :N]
        if width > N:
            out[2 * p + 2] = total[:, N:]
    for a in range(T // 2):
        at = slice(0, (7 - 2 * a) * N)
        term = product(pieces, slice((2 * a + 1) * N, T * N), high[a, :, at], low[a, :, at], dot_t)
        out[2 * a] += term[:, :N]
        out[2 * a + 1] += term[:, N:]


def turned_rows(a):
    return slice(a * (a + 1) * N, (a + 1) * (a + 2) * N)


def turn(high, low, turned_high, turned_low):
    for piece, out in ((high, turned_high), (low, turned_low)):
        for a in range(T // 2):
            out[turned_rows(a), :] = piece[a, :, (7 - 2 * a) * N :].T


def from_next(pieces, high, low, out):
    for a in range(T // 2):
        rows = turned_rows(a)
        term = product(pieces, slice(0, (2 * a + 2) * N), high[rows, :], low[rows, :], dot)
        out[2 * a] += term[:, :N]
        out[2 * a + 1] += term[:, N:]


def moments(first, second):
    high = low = jnp.zeros((R, N), F32)
    for t in range(T):
        high, err = two_sum(high, first[t] * second[t])
        low = low + err
    return high, low


PIECES = pltpu.VMEM((2 * R, T * N), BF16)
ONE_WAY = 2 * 3 * 40 * R * N * N


def choose(flag, first, second):
    return jnp.where(jnp.broadcast_to(flag[0:1, :], (R, N)) > 0, first, second)


def hand_out(flag, vec, high, low, one, two, sent, pieces):
    for t in range(T):
        put_pieces(pieces, t, vec[t])
    to_next(pieces, high, low, sent)
    for t in range(T):
        one[t] = choose(flag, sent[t], vec[t])
        two[t] = choose(flag, vec[t], sent[t])


BLOCKS = shape(T, R, N)
SENT = pltpu.VMEM((T, R, N), F32)
TURNED = shape((T // 2) * (T // 2 + 1) * N, 2 * N, dtype=BF16)


def on_parity(parity):
    return pl.when(lax.axis_index("tm") % 2 == parity)


def first_kernel(rhs, own, inflow, high, low, diag, vec, two, pieces):
    diag[...] = own[...] + inflow[...]

    @on_parity(0)
    def _():
        for t in range(T):
            value = rhs[t] / diag[t : t + 1, :]
            vec[t] = value
            two[t] = value

    @on_parity(1)
    def _():
        for t in range(T):
            value = rhs[t] / diag[t : t + 1, :]
            vec[t] = value
            put_pieces(pieces, t, value)
        to_next(pieces, high, low, two)


def first(*args):
    return call(first_kernel, (shape(T, N), BLOCKS, BLOCKS), [VMEM] * 5, [PIECES], flops=ONE_WAY)(*args)


def local_kernel(count, *refs):
    vecs, (image, high, low, out, found, *more, pieces) = refs[:count], refs[count:]
    for t in range(T):
        put_pieces(pieces, t, vecs[-1][t])
    if more:
        one, *turned = more

        @on_parity(0)
        def _():
            to_next(pieces, high, low, one)

        @on_parity(1)
        def _():
            one[...] = vecs[0][...]

        turn(high, low, *turned)
    within(pieces, high, low, out)
    for i, vec in enumerate(vecs):
        h, l = moments(vec, image)
        found[i, 0] = h
        found[i, 1] = l


def local(vecs, image, high, low):
    more = (BLOCKS, TURNED, TURNED) if len(vecs) == 1 else ()
    return call(
        functools.partial(local_kernel, len(vecs)),
        (BLOCKS, shape(len(vecs), 2, R, N)) + more,
        [VMEM] * (len(vecs) + 3),
        [PIECES],
        flops=2 * ONE_WAY,
    )(*vecs, image, high, low)


def add_received(flag, got_one, got_two, partial, turned_high, turned_low, image, pieces):
    for t in range(T):
        put_pieces(pieces, t, choose(flag, got_one[t], got_two[t]))
        image[t] = partial[t] + choose(flag, got_two[t], got_one[t])
    from_next(pieces, turned_high, turned_low, image)


def step_kernel(flag, got_one, got_two, partial, diag, high, low, turned_high, turned_low, image, vec, one, two, sent, pieces):
    add_received(flag, got_one, got_two, partial, turned_high, turned_low, image, pieces)
    for t in range(T):
        vec[t] = image[t] / diag[t : t + 1, :]
    hand_out(flag, vec, high, low, one, two, sent, pieces)


def next_step(*args):
    return call(step_kernel, (BLOCKS,) * 4, [VMEM] * 9, [SENT, PIECES], flops=2 * ONE_WAY)(*args)


PAIRS = 5


def fold(high, low):
    value = (high, low)
    size = high.shape[0]
    while size > 8:
        size //= 2
        value = dd_add(tuple(v[:size] for v in value), tuple(v[size:] for v in value))
    for turn_by in (4, 2, 1):
        value = dd_add(value, tuple(pltpu.roll(v, turn_by, 0) for v in value))
    return value


def gram_kernel(
    flag, got_one, got_two, partial, turned_high, turned_low, v0, v1, v2, m0, m1, m2, image, out, pieces
):
    add_received(flag, got_one, got_two, partial, turned_high, turned_low, image, pieces)
    last = [moments(v, image) for v in (v0, v1, v2)]
    every = [(m[i, 0], m[i, 1]) for m in (m0, m1, m2) for i in range(m.shape[0])] + last + last[-1:]
    for q in range(PAIRS):
        pair = every[2 * q : 2 * q + 2]
        h, l = fold(*(jnp.concatenate([f[i] for f in pair], axis=0).T for i in range(2)))
        out[:, q * N : (q + 1) * N] = (h + l)[0:1]


def gram(*args):
    return call(gram_kernel, (BLOCKS, shape(1, PAIRS * N)), [VMEM] * 12, [PIECES], flops=ONE_WAY)(*args)


def solve(matrix, right):
    (a00, a01, a02), (a10, a11, a12), (a20, a21, a22) = matrix
    b0, b1, b2 = right
    inv0 = 1.0 / a00
    f1, f2 = a10 * inv0, a20 * inv0
    c11, c12, e1 = a11 - f1 * a01, a12 - f1 * a02, b1 - f1 * b0
    c21, c22, e2 = a21 - f2 * a01, a22 - f2 * a02, b2 - f2 * b0
    inv1 = 1.0 / c11
    g = c21 * inv1
    x2 = (e2 - g * e1) / (c22 - g * c12)
    x1 = (e1 - c12 * x2) * inv1
    x0 = (b0 - a01 * x1 - a02 * x2) * inv0
    return x0, x1, x2


def result_kernel(parts, v0, v1, v2, y0, y1, y2, y3, sol, res):
    flat = []
    for q in range(PAIRS):
        part = parts[:, q * N : (q + 1) * N]
        h, l = (v[0:1] for v in fold(part, jnp.zeros_like(part)))
        flat += [(h, l), (pltpu.roll(h, R, 1), pltpu.roll(l, R, 1))]
    g00, g01, g11, g02, g12, g22, g03, g13, g23 = flat[:9]
    full = ((g00, g01, g02, g03), (g01, g11, g12, g13), (g02, g12, g22, g23))
    minus = lambda a, b: dd_add(a, (-b[0], -b[1]))
    matrix = [[minus(row[j], row[j + 1]) for j in range(3)] for row in full]
    right = [row[1] for row in full]
    near = [[m[0] + m[1] for m in row] for row in matrix]
    coef = [jnp.zeros_like(g00[0])] * 3
    for _ in range(3):
        left = []
        for row, value in zip(matrix, right):
            for m, c in zip(row, coef):
                p, e = two_prod(m[0], c)
                value = minus(value, (p, e + m[1] * c))
            left.append(value[0] + value[1])
        coef = [c + s for c, s in zip(coef, solve(near, left))]
    rows = jnp.concatenate([c[:, :N] for c in coef] + [jnp.zeros((N - 3, N), F32)], axis=0).T
    d0, d1, d2 = (jnp.broadcast_to(rows[:R, i : i + 1], (R, N)) for i in range(3))
    for t in range(T):
        sol[t] = v0[t] + (d0 * v0[t] + d1 * v1[t] + d2 * v2[t])
        first, second = y1[t], y2[t]
        res[t] = first - (d0 * (y0[t] - first) + d1 * (first - second) + d2 * (second - y3[t]))


def result(parts, vecs, images):
    return call(result_kernel, (shape(T, R, N), shape(T, R, N)), [VMEM] * 8)(parts, *vecs, *images)


def shift(value, steps):
    count = lax.axis_size("tm")
    return lax.ppermute(value, "tm", [(i, (i + steps) % count) for i in range(count)])


def all_parts(value):
    count = lax.axis_size("tm")
    half, eighth = count // 2, count // 8
    edges = [i for i in range(half - eighth, count) if i % eighth in (0, eighth - 1)]
    edges.sort(key=lambda i: (i in (half - 1, half), i))
    inner = [i for i in range(half - eighth, count) if i not in edges]
    turns = [*inner, *edges, *range(half - eighth)]
    spread = lax.all_to_all(
        jnp.broadcast_to(value[None], (count,) + value.shape), "tm", 0, 0, axis_index_groups=[turns]
    )
    return spread.reshape(count, value.shape[1])


def swap_within(value):
    return lax.ppermute(value, "tm", [(i, i ^ 1) for i in range(lax.axis_size("tm"))])


def swap_across(value):
    count = lax.axis_size("tm")
    return lax.ppermute(value, "tm", [(i, (i + (1 if i % 2 else -1)) % count) for i in range(count)])


def shards(weights, pattern, shift_reg, rhs):
    flag = jnp.broadcast_to((1 - lax.axis_index("tm") % 2).astype(F32), (8, N))
    flag, pattern = lax.optimization_barrier((flag, pattern))
    inflow = shift(ahead_sums(pattern, weights), 1)
    high, low, own = band_pieces(pattern, weights, shift_reg)
    diag, vec, two = first(rhs, own, inflow, high, low)
    got_two = swap_across(two)
    partial, part, one, *turned = local([vec], rhs, high, low)
    got = swap_within(one), got_two
    vecs, images, found = [vec], [rhs], [part]
    for step in range(2):
        image, vec, one, two = next_step(flag, *got, partial, diag, high, low, *turned)
        got = swap_within(one), swap_across(two)
        images.append(image)
        vecs.append(vec)
        partial, part = local(vecs, image, high, low)
        found.append(part)
    image, part = gram(flag, *got, partial, *turned, *vecs, *found)
    return result(all_parts(part), vecs, images + [image])


def solution(mesh):
    return jax.shard_map(
        shards,
        mesh=mesh,
        in_specs=(P("tm", None, None, None), P("tm", None), P("tm", None), P("tm", "scen", None)),
        out_specs=(P("tm", "scen", None), P("tm", "scen", None)),
        check_vma=False,
    )
```

```python
import functools

import jax
import jax.numpy as jnp
from jax import lax
from jax.experimental import pallas as pl
from jax.experimental.pallas import tpu as pltpu
from jax.sharding import PartitionSpec as P

F32 = jnp.float32
BF16 = jnp.bfloat16
MIB = 1024 * 1024
N = 128
T = 8
R = 64
VMEM = pl.BlockSpec(memory_space=pltpu.VMEM)
HBM = pl.BlockSpec(memory_space=pltpu.HBM)

BAND = (T // 2, 2 * N, (T + 1) * N)


def call(body, outs, specs=None, scratch=(), limit=16, flops=0, moved=0):
    return pl.pallas_call(
        body,
        out_shape=outs,
        in_specs=specs,
        out_specs=jax.tree.map(lambda _: VMEM, outs),
        scratch_shapes=list(scratch),
        compiler_params=pltpu.CompilerParams(vmem_limit_bytes=limit * MIB),
        cost_estimate=pl.CostEstimate(flops=flops, bytes_accessed=moved, transcendentals=0),
    )


def in_hbm(value):
    return pltpu.with_memory_space_constraint(value, pltpu.HBM)


def shape(*dims, dtype=F32):
    return jax.ShapeDtypeStruct(dims, dtype)


def dot(a, b):
    return lax.dot_general(a, b, (((1,), (0,)), ((), ())), preferred_element_type=F32)


def dot_t(a, b):
    return lax.dot_general(a, b, (((1,), (1,)), ((), ())), preferred_element_type=F32)


def two_sum(a, b):
    s = a + b
    t = s - a
    return s, (a - (s - t)) + (b - t)


def dd_add(a, b):
    s, e = two_sum(a[0], b[0])
    return s, e + (a[1] + b[1])


def halves(a):
    t = a * 4097.0
    h = t - (t - a)
    return h, a - h


def two_prod(a, b):
    p = a * b
    ah, al = halves(a)
    bh, bl = halves(b)
    return p, ((ah * bh - p) + ah * bl + al * bh) + al * bl


def ahead_kernel(pattern, weights, ahead, mask, buf, cols, sems):
    head = pltpu.make_async_copy(pattern, mask, sems.at[T])
    head.start()
    copies = []
    for t in range(T):
        some = slice(T - 1 - t, T)
        copies.append(pltpu.make_async_copy(weights.at[t, some], buf.at[t, some], sems.at[t]))
    for copy in copies:
        copy.start()
    for t in range(T):
        copies[t].wait()
        for k in range(T - 1 - t, T):
            cols[t, k] = jnp.sum(buf[t, k].reshape(N // 8, 8, N), axis=0)
    head.wait()
    for b in range(T):
        total = jnp.zeros((8, N), F32)
        for t in range(b, T):
            k = T - 1 - t + b
            total = total + cols[t, k] * mask[t, k].astype(F32)
        ahead[b : b + 1, :] = jnp.sum(total, axis=0, keepdims=True)


def ahead_sums(pattern, weights):
    pattern, weights = in_hbm(pattern), in_hbm(weights)
    return call(
        ahead_kernel,
        shape(T, N),
        [HBM, HBM],
        [
            pltpu.SMEM((T, T), jnp.int32),
            pltpu.VMEM((T, T, N, N), F32),
            pltpu.VMEM((T, T, 8, N), F32),
            pltpu.SemaphoreType.DMA((T + 1,)),
        ],
        flops=4 * T * T * N * N,
        moved=4 * T * T * N * N,
    )(pattern, weights)


def band_kernel(pattern, weights, reg, high, low, own, mask, buf, cols, extra, sems):
    def copy(t):
        return pltpu.make_async_copy(weights.at[t], buf.at[t], sems.at[t])

    head = pltpu.make_async_copy(pattern, mask, sems.at[T])
    tail = pltpu.make_async_copy(reg, extra, sems.at[T + 1])
    head.start()
    for t in range(T):
        copy(t).start()
    tail.start()
    cols[...] = jnp.zeros_like(cols)
    zero = jnp.zeros((N, N), BF16)
    for a in range(T // 2):
        for piece in (high, low):
            piece[a, N : 2 * N, 0:N] = zero
            piece[a, 0:N, T * N : (T + 1) * N] = zero
    head.wait()

    def step(a, carry):
        for half in range(2):
            t = 2 * a + half
            copy(t).wait()
            rows = jnp.zeros((N, N), F32)
            for k in range(T):
                m = buf[t, k] * mask[t, k].astype(F32)
                rows = rows + m
                cols[t + k + 1] += jnp.sum(m.reshape(N // 8, 8, N), axis=0)
                h = m.astype(BF16)
                place = slice((k + half) * N, (k + half + 1) * N)
                high[a, half * N : (half + 1) * N, place] = h
                low[a, half * N : (half + 1) * N, place] = (m - h.astype(F32)).astype(BF16)
            own[pl.ds(t, 1), :] = jnp.sum(rows.T, axis=0, keepdims=True)
        return carry

    lax.fori_loop(0, T // 2, step, 0)
    tail.wait()
    own[...] += jnp.sum(cols[:T], axis=1) + extra[...]


def band_pieces(pattern, weights, reg):
    pattern, weights, reg = in_hbm(pattern), in_hbm(weights), in_hbm(reg)
    return call(
        band_kernel,
        (shape(*BAND, dtype=BF16), shape(*BAND, dtype=BF16), shape(T, N)),
        [HBM, HBM, HBM],
        [
            pltpu.SMEM((T, T), jnp.int32),
            pltpu.VMEM((T, T, N, N), F32),
            pltpu.VMEM((2 * T, 8, N), F32),
            pltpu.VMEM((T, N), F32),
            pltpu.SemaphoreType.DMA((T + 2,)),
        ],
        flops=2048 * T * T * N * N,
        moved=8 * T * T * N * N,
    )(pattern, weights, reg)


def put_pieces(pieces, t, value):
    h = value.astype(BF16)
    pieces[0:R, t * N : (t + 1) * N] = h
    pieces[R : 2 * R, t * N : (t + 1) * N] = (value - h.astype(F32)).astype(BF16)


def product(pieces, cols, high, low, mult):
    both = mult(pieces[:, cols], high)
    return (both[:R] + mult(pieces[0:R, cols], low)) + both[R:]


def to_next(pieces, high, low, put):
    for b in range(T // 2):
        total = None
        for a in range(b, T // 2):
            at = slice((7 + 2 * b - 2 * a) * N, (9 + 2 * b - 2 * a) * N)
            term = product(pieces, slice(a * 2 * N, (a + 1) * 2 * N), high[a, :, at], low[a, :, at], dot)
            total = term if total is None else total + term
        put(2 * b, total[:, :N])
        put(2 * b + 1, total[:, N:])


def within(pieces, high, low, out):
    out[0] = jnp.zeros((R, N), F32)
    for p in range(T // 2):
        total = None
        width = 2 * N if p < T // 2 - 1 else N
        for a in range(p + 1):
            at = slice(2 * (p - a) * N, 2 * (p - a) * N + width)
            term = product(pieces, slice(a * 2 * N, (a + 1) * 2 * N), high[a, :, at], low[a, :, at], dot)
            total = term if total is None else total + term
        out[2 * p + 1] = total[:, :N]
        if width > N:
            out[2 * p + 2] = total[:, N:]
    for a in range(T // 2):
        at = slice(0, (7 - 2 * a) * N)
        term = product(pieces, slice((2 * a + 1) * N, T * N), high[a, :, at], low[a, :, at], dot_t)
        out[2 * a] += term[:, :N]
        out[2 * a + 1] += term[:, N:]


def turned_rows(a):
    return slice(a * (a + 1) * N, (a + 1) * (a + 2) * N)


def turn(high, low, turned_high, turned_low):
    for piece, out in ((high, turned_high), (low, turned_low)):
        for a in range(T // 2):
            out[turned_rows(a), :] = piece[a, :, (7 - 2 * a) * N :].T


def from_next(pieces, high, low, put):
    for a in range(T // 2):
        rows = turned_rows(a)
        term = product(pieces, slice(0, (2 * a + 2) * N), high[rows, :], low[rows, :], dot)
        put(2 * a, term[:, :N])
        put(2 * a + 1, term[:, N:])


def store(out):
    def put(t, value):
        out[t] = value

    return put


def moments(first, second):
    high = low = jnp.zeros((R, N), F32)
    for t in range(T):
        high, err = two_sum(high, first[t] * second[t])
        low = low + err
    return high, low


PIECES = pltpu.VMEM((2 * R, T * N), BF16)
ONE_WAY = 2 * 3 * 40 * R * N * N


def choose(flag, first, second):
    return jnp.where(jnp.broadcast_to(flag[0:1, :], (R, N)) > 0, first, second)


BLOCKS = shape(T, R, N)
TURNED = shape((T // 2) * (T // 2 + 1) * N, 2 * N, dtype=BF16)


def on_parity(parity):
    return pl.when(lax.axis_index("tm") % 2 == parity)


def first_kernel(rhs, own, inflow, high, low, diag, vec, two, pieces):
    diag[...] = own[...] + inflow[...]

    @on_parity(0)
    def _():
        for t in range(T):
            value = rhs[t] / diag[t : t + 1, :]
            vec[t] = value
            two[t] = value

    @on_parity(1)
    def _():
        for t in range(T):
            value = rhs[t] / diag[t : t + 1, :]
            vec[t] = value
            put_pieces(pieces, t, value)
        to_next(pieces, high, low, store(two))


def first(*args):
    return call(first_kernel, (shape(T, N), BLOCKS, BLOCKS), [VMEM] * 5, [PIECES], flops=ONE_WAY)(*args)


def local_kernel(count, *refs):
    vecs, (image, high, low, out, found, *more, pieces) = refs[:count], refs[count:]
    for t in range(T):
        put_pieces(pieces, t, vecs[-1][t])
    if more:
        one, *turned = more

        @on_parity(0)
        def _():
            to_next(pieces, high, low, store(one))

        @on_parity(1)
        def _():
            one[...] = vecs[0][...]

        turn(high, low, *turned)
    within(pieces, high, low, out)
    for i, vec in enumerate(vecs):
        h, l = moments(vec, image)
        found[i, 0] = h
        found[i, 1] = l


def local(vecs, image, high, low):
    more = (BLOCKS, TURNED, TURNED) if len(vecs) == 1 else ()
    return call(
        functools.partial(local_kernel, len(vecs)),
        (BLOCKS, shape(len(vecs), 2, R, N)) + more,
        [VMEM] * (len(vecs) + 3),
        [PIECES],
        flops=2 * ONE_WAY,
    )(*vecs, image, high, low)


def add_received(flag, got_one, got_two, partial, turned_high, turned_low, pieces, put):
    for t in range(T):
        put_pieces(pieces, t, choose(flag, got_one[t], got_two[t]))

    def add(t, term):
        put(t, (partial[t] + choose(flag, got_two[t], got_one[t])) + term)

    from_next(pieces, turned_high, turned_low, add)


def step_kernel(
    flag, got_one, got_two, partial, diag, high, low, turned_high, turned_low, image, vec, one, two, pieces, made
):
    def take(t, value):
        image[t] = value
        value = value / diag[t : t + 1, :]
        vec[t] = value
        put_pieces(made, t, value)

    def give(t, value):
        one[t] = choose(flag, value, vec[t])
        two[t] = choose(flag, vec[t], value)

    add_received(flag, got_one, got_two, partial, turned_high, turned_low, pieces, take)
    to_next(made, high, low, give)


def next_step(*args):
    return call(step_kernel, (BLOCKS,) * 4, [VMEM] * 9, [PIECES, PIECES], flops=2 * ONE_WAY)(*args)


PAIRS = 5


def fold(high, low):
    value = (high, low)
    size = high.shape[0]
    while size > 8:
        size //= 2
        value = dd_add(tuple(v[:size] for v in value), tuple(v[size:] for v in value))
    for turn_by in (4, 2, 1):
        value = dd_add(value, tuple(pltpu.roll(v, turn_by, 0) for v in value))
    return value


def gram_kernel(
    flag, got_one, got_two, partial, turned_high, turned_low, v0, v1, v2, m0, m1, m2, image, out, pieces
):
    add_received(flag, got_one, got_two, partial, turned_high, turned_low, pieces, store(image))
    last = [moments(v, image) for v in (v0, v1, v2)]
    every = [(m[i, 0], m[i, 1]) for m in (m0, m1, m2) for i in range(m.shape[0])] + last + last[-1:]
    for q in range(PAIRS):
        pair = every[2 * q : 2 * q + 2]
        h, l = fold(*(jnp.concatenate([f[i] for f in pair], axis=0).T for i in range(2)))
        out[:, q * N : (q + 1) * N] = (h + l)[0:1]


def gram(*args):
    return call(gram_kernel, (BLOCKS, shape(1, PAIRS * N)), [VMEM] * 12, [PIECES], flops=ONE_WAY)(*args)


def solve(matrix, right):
    (a00, a01, a02), (a10, a11, a12), (a20, a21, a22) = matrix
    b0, b1, b2 = right
    inv0 = 1.0 / a00
    f1, f2 = a10 * inv0, a20 * inv0
    c11, c12, e1 = a11 - f1 * a01, a12 - f1 * a02, b1 - f1 * b0
    c21, c22, e2 = a21 - f2 * a01, a22 - f2 * a02, b2 - f2 * b0
    inv1 = 1.0 / c11
    g = c21 * inv1
    x2 = (e2 - g * e1) / (c22 - g * c12)
    x1 = (e1 - c12 * x2) * inv1
    x0 = (b0 - a01 * x1 - a02 * x2) * inv0
    return x0, x1, x2


def result_kernel(parts, v0, v1, v2, y0, y1, y2, y3, sol, res):
    flat = []
    for q in range(PAIRS):
        part = parts[:, q * N : (q + 1) * N]
        h, l = (v[0:1] for v in fold(part, jnp.zeros_like(part)))
        flat += [(h, l), (pltpu.roll(h, R, 1), pltpu.roll(l, R, 1))]
    g00, g01, g11, g02, g12, g22, g03, g13, g23 = flat[:9]
    full = ((g00, g01, g02, g03), (g01, g11, g12, g13), (g02, g12, g22, g23))
    minus = lambda a, b: dd_add(a, (-b[0], -b[1]))
    matrix = [[minus(row[j], row[j + 1]) for j in range(3)] for row in full]
    right = [row[1] for row in full]
    near = [[m[0] + m[1] for m in row] for row in matrix]
    coef = [jnp.zeros_like(g00[0])] * 3
    for _ in range(3):
        left = []
        for row, value in zip(matrix, right):
            for m, c in zip(row, coef):
                p, e = two_prod(m[0], c)
                value = minus(value, (p, e + m[1] * c))
            left.append(value[0] + value[1])
        coef = [c + s for c, s in zip(coef, solve(near, left))]
    rows = jnp.concatenate([c[:, :N] for c in coef] + [jnp.zeros((N - 3, N), F32)], axis=0).T
    d0, d1, d2 = (jnp.broadcast_to(rows[:R, i : i + 1], (R, N)) for i in range(3))
    for t in range(T):
        sol[t] = v0[t] + (d0 * v0[t] + d1 * v1[t] + d2 * v2[t])
        first, second = y1[t], y2[t]
        res[t] = first - (d0 * (y0[t] - first) + d1 * (first - second) + d2 * (second - y3[t]))


def result(parts, vecs, images):
    return call(result_kernel, (shape(T, R, N), shape(T, R, N)), [VMEM] * 8)(parts, *vecs, *images)


def shift(value, steps):
    count = lax.axis_size("tm")
    return lax.ppermute(value, "tm", [(i, (i + steps) % count) for i in range(count)])


def all_parts(value):
    count = lax.axis_size("tm")
    half, eighth = count // 2, count // 8
    last = [half - 1, half]
    near = [i for i in range(half - eighth, half + eighth) if i not in last]
    turns = [*range(half + eighth, count), *near, *last, *range(half - eighth)]
    spread = lax.all_to_all(
        jnp.broadcast_to(value[None], (count,) + value.shape), "tm", 0, 0, axis_index_groups=[turns]
    )
    return spread.reshape(count, value.shape[1])


def swap_within(value):
    return lax.ppermute(value, "tm", [(i, i ^ 1) for i in range(lax.axis_size("tm"))])


def swap_across(value):
    count = lax.axis_size("tm")
    return lax.ppermute(value, "tm", [(i, (i + (1 if i % 2 else -1)) % count) for i in range(count)])


def shards(weights, pattern, shift_reg, rhs):
    flag = jnp.broadcast_to((1 - lax.axis_index("tm") % 2).astype(F32), (8, N))
    flag, pattern = lax.optimization_barrier((flag, pattern))
    inflow = shift(ahead_sums(pattern, weights), 1)
    high, low, own = band_pieces(pattern, weights, shift_reg)
    diag, vec, two = first(rhs, own, inflow, high, low)
    got_two = swap_across(two)
    partial, part, one, *turned = local([vec], rhs, high, low)
    got = swap_within(one), got_two
    vecs, images, found = [vec], [rhs], [part]
    for step in range(2):
        image, vec, one, two = next_step(flag, *got, partial, diag, high, low, *turned)
        got = swap_within(one), swap_across(two)
        images.append(image)
        vecs.append(vec)
        partial, part = local(vecs, image, high, low)
        found.append(part)
    image, part = gram(flag, *got, partial, *turned, *vecs, *found)
    return result(all_parts(part), vecs, images + [image])


def solution(mesh):
    return jax.shard_map(
        shards,
        mesh=mesh,
        in_specs=(P("tm", None, None, None), P("tm", None), P("tm", None), P("tm", "scen", None)),
        out_specs=(P("tm", "scen", None), P("tm", "scen", None)),
        check_vma=False,
    )
```

```python
import functools

import jax
import jax.numpy as jnp
from jax import lax
from jax.experimental import pallas as pl
from jax.experimental.pallas import tpu as pltpu
from jax.sharding import PartitionSpec as P

F32 = jnp.float32
BF16 = jnp.bfloat16
MIB = 1024 * 1024
N = 128
T = 8
R = 64
VMEM = pl.BlockSpec(memory_space=pltpu.VMEM)
HBM = pl.BlockSpec(memory_space=pltpu.HBM)

BAND = (T // 2, 2 * N, (T + 1) * N)


def call(body, outs, specs=None, scratch=(), limit=16, flops=0, moved=0):
    return pl.pallas_call(
        body,
        out_shape=outs,
        in_specs=specs,
        out_specs=jax.tree.map(lambda _: VMEM, outs),
        scratch_shapes=list(scratch),
        compiler_params=pltpu.CompilerParams(vmem_limit_bytes=limit * MIB),
        cost_estimate=pl.CostEstimate(flops=flops, bytes_accessed=moved, transcendentals=0),
    )


def in_hbm(value):
    return pltpu.with_memory_space_constraint(value, pltpu.HBM)


def shape(*dims, dtype=F32):
    return jax.ShapeDtypeStruct(dims, dtype)


def dot(a, b):
    return lax.dot_general(a, b, (((1,), (0,)), ((), ())), preferred_element_type=F32)


def dot_t(a, b):
    return lax.dot_general(a, b, (((1,), (1,)), ((), ())), preferred_element_type=F32)


def two_sum(a, b):
    s = a + b
    t = s - a
    return s, (a - (s - t)) + (b - t)


def dd_add(a, b):
    s, e = two_sum(a[0], b[0])
    return s, e + (a[1] + b[1])


def halves(a):
    t = a * 4097.0
    h = t - (t - a)
    return h, a - h


def two_prod(a, b):
    p = a * b
    ah, al = halves(a)
    bh, bl = halves(b)
    return p, ((ah * bh - p) + ah * bl + al * bh) + al * bl


def ahead_kernel(pattern, weights, ahead, mask, buf, cols, sems):
    head = pltpu.make_async_copy(pattern, mask, sems.at[T])
    head.start()
    copies = []
    for t in range(T):
        some = slice(T - 1 - t, T)
        copies.append(pltpu.make_async_copy(weights.at[t, some], buf.at[t, some], sems.at[t]))
    for copy in copies:
        copy.start()
    for t in range(T):
        copies[t].wait()
        for k in range(T - 1 - t, T):
            cols[t, k] = jnp.sum(buf[t, k].reshape(N // 8, 8, N), axis=0)
    head.wait()
    for b in range(T):
        total = jnp.zeros((8, N), F32)
        for t in range(b, T):
            k = T - 1 - t + b
            total = total + cols[t, k] * mask[t, k].astype(F32)
        ahead[b : b + 1, :] = jnp.sum(total, axis=0, keepdims=True)


def ahead_sums(pattern, weights):
    pattern, weights = in_hbm(pattern), in_hbm(weights)
    return call(
        ahead_kernel,
        shape(T, N),
        [HBM, HBM],
        [
            pltpu.SMEM((T, T), jnp.int32),
            pltpu.VMEM((T, T, N, N), F32),
            pltpu.VMEM((T, T, 8, N), F32),
            pltpu.SemaphoreType.DMA((T + 1,)),
        ],
        flops=4 * T * T * N * N,
        moved=4 * T * T * N * N,
    )(pattern, weights)


def band_kernel(pattern, weights, reg, high, low, own, mask, buf, cols, extra, sems):
    def copy(t):
        return pltpu.make_async_copy(weights.at[t], buf.at[t], sems.at[t])

    head = pltpu.make_async_copy(pattern, mask, sems.at[T])
    tail = pltpu.make_async_copy(reg, extra, sems.at[T + 1])
    head.start()
    for t in range(T):
        copy(t).start()
    tail.start()
    cols[...] = jnp.zeros_like(cols)
    zero = jnp.zeros((N, N), BF16)
    for a in range(T // 2):
        for piece in (high, low):
            piece[a, N : 2 * N, 0:N] = zero
            piece[a, 0:N, T * N : (T + 1) * N] = zero
    head.wait()

    def step(a, carry):
        for half in range(2):
            t = 2 * a + half
            copy(t).wait()
            rows = jnp.zeros((N, N), F32)
            for k in range(T):
                m = buf[t, k] * mask[t, k].astype(F32)
                rows = rows + m
                cols[t + k + 1] += jnp.sum(m.reshape(N // 8, 8, N), axis=0)
                h = m.astype(BF16)
                place = slice((k + half) * N, (k + half + 1) * N)
                high[a, half * N : (half + 1) * N, place] = h
                low[a, half * N : (half + 1) * N, place] = (m - h.astype(F32)).astype(BF16)
            own[pl.ds(t, 1), :] = jnp.sum(rows.T, axis=0, keepdims=True)
        return carry

    lax.fori_loop(0, T // 2, step, 0)
    tail.wait()
    own[...] += jnp.sum(cols[:T], axis=1) + extra[...]


def band_pieces(pattern, weights, reg):
    pattern, weights, reg = in_hbm(pattern), in_hbm(weights), in_hbm(reg)
    return call(
        band_kernel,
        (shape(*BAND, dtype=BF16), shape(*BAND, dtype=BF16), shape(T, N)),
        [HBM, HBM, HBM],
        [
            pltpu.SMEM((T, T), jnp.int32),
            pltpu.VMEM((T, T, N, N), F32),
            pltpu.VMEM((2 * T, 8, N), F32),
            pltpu.VMEM((T, N), F32),
            pltpu.SemaphoreType.DMA((T + 2,)),
        ],
        flops=2048 * T * T * N * N,
        moved=8 * T * T * N * N,
    )(pattern, weights, reg)


def put_pieces(pieces, t, value):
    h = value.astype(BF16)
    pieces[0:R, t * N : (t + 1) * N] = h
    pieces[R : 2 * R, t * N : (t + 1) * N] = (value - h.astype(F32)).astype(BF16)


def product(pieces, cols, high, low, mult):
    both = mult(pieces[:, cols], high)
    return (both[:R] + mult(pieces[0:R, cols], low)) + both[R:]


def to_next(pieces, high, low, put):
    for b in range(T // 2):
        total = None
        for a in range(b, T // 2):
            at = slice((7 + 2 * b - 2 * a) * N, (9 + 2 * b - 2 * a) * N)
            term = product(pieces, slice(a * 2 * N, (a + 1) * 2 * N), high[a, :, at], low[a, :, at], dot)
            total = term if total is None else total + term
        put(2 * b, total[:, :N])
        put(2 * b + 1, total[:, N:])


def within(pieces, high, low, out):
    out[0] = jnp.zeros((R, N), F32)
    for p in range(T // 2):
        total = None
        width = 2 * N if p < T // 2 - 1 else N
        for a in range(p + 1):
            at = slice(2 * (p - a) * N, 2 * (p - a) * N + width)
            term = product(pieces, slice(a * 2 * N, (a + 1) * 2 * N), high[a, :, at], low[a, :, at], dot)
            total = term if total is None else total + term
        out[2 * p + 1] = total[:, :N]
        if width > N:
            out[2 * p + 2] = total[:, N:]
    for a in range(T // 2):
        at = slice(0, (7 - 2 * a) * N)
        term = product(pieces, slice((2 * a + 1) * N, T * N), high[a, :, at], low[a, :, at], dot_t)
        out[2 * a] += term[:, :N]
        out[2 * a + 1] += term[:, N:]


def turned_rows(a):
    return slice(a * (a + 1) * N, (a + 1) * (a + 2) * N)


def turn(high, low, turned_high, turned_low):
    for piece, out in ((high, turned_high), (low, turned_low)):
        for a in range(T // 2):
            out[turned_rows(a), :] = piece[a, :, (7 - 2 * a) * N :].T


def from_next(pieces, high, low, put):
    for a in range(T // 2):
        rows = turned_rows(a)
        term = product(pieces, slice(0, (2 * a + 2) * N), high[rows, :], low[rows, :], dot)
        put(2 * a, term[:, :N])
        put(2 * a + 1, term[:, N:])


def store(out):
    def put(t, value):
        out[t] = value

    return put


def moments(first, second):
    high = low = jnp.zeros((R, N), F32)
    for t in range(T):
        high, err = two_sum(high, first[t] * second[t])
        low = low + err
    return high, low


PIECES = pltpu.VMEM((2 * R, T * N), BF16)
ONE_WAY = 2 * 3 * 40 * R * N * N


def choose(flag, first, second):
    return jnp.where(jnp.broadcast_to(flag[0:1, :], (R, N)) > 0, first, second)


BLOCKS = shape(T, R, N)
TURNED = shape((T // 2) * (T // 2 + 1) * N, 2 * N, dtype=BF16)


def on_parity(parity):
    return pl.when(lax.axis_index("tm") % 2 == parity)


def first_kernel(rhs, own, inflow, high, low, diag, vec, two, pieces):
    diag[...] = own[...] + inflow[...]

    @on_parity(0)
    def _():
        for t in range(T):
            value = rhs[t] / diag[t : t + 1, :]
            vec[t] = value
            two[t] = value

    @on_parity(1)
    def _():
        for t in range(T):
            value = rhs[t] / diag[t : t + 1, :]
            vec[t] = value
            put_pieces(pieces, t, value)
        to_next(pieces, high, low, store(two))


def first(*args):
    return call(first_kernel, (shape(T, N), BLOCKS, BLOCKS), [VMEM] * 5, [PIECES], flops=ONE_WAY)(*args)


def local_kernel(count, *refs):
    vecs, (image, high, low, out, found, *more, pieces) = refs[:count], refs[count:]
    for t in range(T):
        put_pieces(pieces, t, vecs[-1][t])
    if more:
        one, *turned = more

        @on_parity(0)
        def _():
            to_next(pieces, high, low, store(one))

        @on_parity(1)
        def _():
            one[...] = vecs[0][...]

        turn(high, low, *turned)
    within(pieces, high, low, out)
    for i, vec in enumerate(vecs):
        h, l = moments(vec, image)
        found[i, 0] = h
        found[i, 1] = l


def local(vecs, image, high, low):
    more = (BLOCKS, TURNED, TURNED) if len(vecs) == 1 else ()
    return call(
        functools.partial(local_kernel, len(vecs)),
        (BLOCKS, shape(len(vecs), 2, R, N)) + more,
        [VMEM] * (len(vecs) + 3),
        [PIECES],
        flops=2 * ONE_WAY,
    )(*vecs, image, high, low)


def add_received(flag, got_one, got_two, partial, turned_high, turned_low, pieces, put):
    for t in range(T):
        put_pieces(pieces, t, choose(flag, got_one[t], got_two[t]))

    def add(t, term):
        put(t, (partial[t] + choose(flag, got_two[t], got_one[t])) + term)

    from_next(pieces, turned_high, turned_low, add)


def step_kernel(
    flag, got_one, got_two, partial, diag, high, low, turned_high, turned_low, image, vec, one, two, pieces, made
):
    def take(t, value):
        image[t] = value
        value = value / diag[t : t + 1, :]
        vec[t] = value
        put_pieces(made, t, value)

    def give(t, value):
        one[t] = choose(flag, value, vec[t])
        two[t] = choose(flag, vec[t], value)

    add_received(flag, got_one, got_two, partial, turned_high, turned_low, pieces, take)
    to_next(made, high, low, give)


def next_step(*args):
    return call(step_kernel, (BLOCKS,) * 4, [VMEM] * 9, [PIECES, PIECES], flops=2 * ONE_WAY)(*args)


PAIRS = 5


def fold(high, low):
    value = (high, low)
    size = high.shape[0]
    while size > 8:
        size //= 2
        value = dd_add(tuple(v[:size] for v in value), tuple(v[size:] for v in value))
    for turn_by in (4, 2, 1):
        value = dd_add(value, tuple(pltpu.roll(v, turn_by, 0) for v in value))
    return value


def gram_kernel(
    flag, got_one, got_two, partial, turned_high, turned_low, v0, v1, v2, m0, m1, m2, image, out, pieces
):
    add_received(flag, got_one, got_two, partial, turned_high, turned_low, pieces, store(image))
    last = [moments(v, image) for v in (v0, v1, v2)]
    every = [(m[i, 0], m[i, 1]) for m in (m0, m1, m2) for i in range(m.shape[0])] + last + last[-1:]
    for q in range(PAIRS):
        pair = every[2 * q : 2 * q + 2]
        h, l = fold(*(jnp.concatenate([f[i] for f in pair], axis=0).T for i in range(2)))
        out[:, q * N : (q + 1) * N] = (h + l)[0:1]


def gram(*args):
    return call(gram_kernel, (BLOCKS, shape(1, PAIRS * N)), [VMEM] * 12, [PIECES], flops=ONE_WAY)(*args)


def solve(matrix, right):
    (a00, a01, a02), (a10, a11, a12), (a20, a21, a22) = matrix
    b0, b1, b2 = right
    inv0 = 1.0 / a00
    f1, f2 = a10 * inv0, a20 * inv0
    c11, c12, e1 = a11 - f1 * a01, a12 - f1 * a02, b1 - f1 * b0
    c21, c22, e2 = a21 - f2 * a01, a22 - f2 * a02, b2 - f2 * b0
    inv1 = 1.0 / c11
    g = c21 * inv1
    x2 = (e2 - g * e1) / (c22 - g * c12)
    x1 = (e1 - c12 * x2) * inv1
    x0 = (b0 - a01 * x1 - a02 * x2) * inv0
    return x0, x1, x2


def result_kernel(parts, v0, v1, v2, y0, y1, y2, y3, sol, res):
    flat = []
    for q in range(PAIRS):
        part = parts[:, q * N : (q + 1) * N]
        h, l = (v[0:1] for v in fold(part, jnp.zeros_like(part)))
        flat += [(h, l), (pltpu.roll(h, R, 1), pltpu.roll(l, R, 1))]
    g00, g01, g11, g02, g12, g22, g03, g13, g23 = flat[:9]
    full = ((g00, g01, g02, g03), (g01, g11, g12, g13), (g02, g12, g22, g23))
    minus = lambda a, b: dd_add(a, (-b[0], -b[1]))
    matrix = [[minus(row[j], row[j + 1]) for j in range(3)] for row in full]
    right = [row[1] for row in full]
    near = [[m[0] + m[1] for m in row] for row in matrix]
    coef = [jnp.zeros_like(g00[0])] * 3
    for _ in range(3):
        left = []
        for row, value in zip(matrix, right):
            for m, c in zip(row, coef):
                p, e = two_prod(m[0], c)
                value = minus(value, (p, e + m[1] * c))
            left.append(value[0] + value[1])
        coef = [c + s for c, s in zip(coef, solve(near, left))]
    rows = jnp.concatenate([c[:, :N] for c in coef] + [jnp.zeros((N - 3, N), F32)], axis=0).T
    d0, d1, d2 = (jnp.broadcast_to(rows[:R, i : i + 1], (R, N)) for i in range(3))
    for t in range(T):
        sol[t] = v0[t] + (d0 * v0[t] + d1 * v1[t] + d2 * v2[t])
        first, second = y1[t], y2[t]
        res[t] = first - (d0 * (y0[t] - first) + d1 * (first - second) + d2 * (second - y3[t]))


def result(parts, vecs, images):
    return call(result_kernel, (shape(T, R, N), shape(T, R, N)), [VMEM] * 8)(parts, *vecs, *images)


def shift(value, steps):
    count = lax.axis_size("tm")
    return lax.ppermute(value, "tm", [(i, (i + steps) % count) for i in range(count)])


def all_parts(value):
    count = lax.axis_size("tm")
    half, eighth = count // 2, count // 8
    last = [half - 1, half]
    near = [i for i in range(half - eighth, half + eighth) if i not in last]
    early = sorted(range(half - eighth), key=lambda i: (2 * (i // eighth) + 3 * (i % 4), i))
    turns = [*range(half + eighth, count), *near, *last, *early]
    spread = lax.all_to_all(
        jnp.broadcast_to(value[None], (count,) + value.shape), "tm", 0, 0, axis_index_groups=[turns]
    )
    return spread.reshape(count, value.shape[1])


def swap_within(value):
    return lax.ppermute(value, "tm", [(i, i ^ 1) for i in range(lax.axis_size("tm"))])


def swap_across(value):
    count = lax.axis_size("tm")
    return lax.ppermute(value, "tm", [(i, (i + (1 if i % 2 else -1)) % count) for i in range(count)])


def shards(weights, pattern, shift_reg, rhs):
    flag = jnp.broadcast_to((1 - lax.axis_index("tm") % 2).astype(F32), (8, N))
    flag, pattern = lax.optimization_barrier((flag, pattern))
    inflow = shift(ahead_sums(pattern, weights), 1)
    high, low, own = band_pieces(pattern, weights, shift_reg)
    diag, vec, two = first(rhs, own, inflow, high, low)
    got_two = swap_across(two)
    partial, part, one, *turned = local([vec], rhs, high, low)
    got = swap_within(one), got_two
    vecs, images, found = [vec], [rhs], [part]
    for step in range(2):
        image, vec, one, two = next_step(flag, *got, partial, diag, high, low, *turned)
        got = swap_within(one), swap_across(two)
        images.append(image)
        vecs.append(vec)
        partial, part = local(vecs, image, high, low)
        found.append(part)
    image, part = gram(flag, *got, partial, *turned, *vecs, *found)
    return result(all_parts(part), vecs, images + [image])


def solution(mesh):
    return jax.shard_map(
        shards,
        mesh=mesh,
        in_specs=(P("tm", None, None, None), P("tm", None), P("tm", None), P("tm", "scen", None)),
        out_specs=(P("tm", "scen", None), P("tm", "scen", None)),
        check_vma=False,
    )
```

```python
import functools

import jax
import jax.numpy as jnp
from jax import lax
from jax.experimental import pallas as pl
from jax.experimental.pallas import tpu as pltpu
from jax.sharding import PartitionSpec as P

F32 = jnp.float32
BF16 = jnp.bfloat16
MIB = 1024 * 1024
N = 128
T = 8
R = 64
VMEM = pl.BlockSpec(memory_space=pltpu.VMEM)
HBM = pl.BlockSpec(memory_space=pltpu.HBM)

BAND = (T // 2, 2 * N, (T + 1) * N)


def call(body, outs, specs=None, scratch=(), limit=16, flops=0, moved=0):
    return pl.pallas_call(
        body,
        out_shape=outs,
        in_specs=specs,
        out_specs=jax.tree.map(lambda _: VMEM, outs),
        scratch_shapes=list(scratch),
        compiler_params=pltpu.CompilerParams(vmem_limit_bytes=limit * MIB),
        cost_estimate=pl.CostEstimate(flops=flops, bytes_accessed=moved, transcendentals=0),
    )


def in_hbm(value):
    return pltpu.with_memory_space_constraint(value, pltpu.HBM)


def shape(*dims, dtype=F32):
    return jax.ShapeDtypeStruct(dims, dtype)


def dot(a, b):
    return lax.dot_general(a, b, (((1,), (0,)), ((), ())), preferred_element_type=F32)


def dot_t(a, b):
    return lax.dot_general(a, b, (((1,), (1,)), ((), ())), preferred_element_type=F32)


def two_sum(a, b):
    s = a + b
    t = s - a
    return s, (a - (s - t)) + (b - t)


def dd_add(a, b):
    s, e = two_sum(a[0], b[0])
    return s, e + (a[1] + b[1])


def halves(a):
    t = a * 4097.0
    h = t - (t - a)
    return h, a - h


def two_prod(a, b):
    p = a * b
    ah, al = halves(a)
    bh, bl = halves(b)
    return p, ((ah * bh - p) + ah * bl + al * bh) + al * bl


def ahead_kernel(pattern, weights, ahead, buf, mask, cols, sems):
    head = pltpu.make_async_copy(pattern, mask, sems.at[T])
    head.start()
    copies = []
    for t in range(T):
        some = slice(T - 1 - t, T)
        copies.append(pltpu.make_async_copy(weights.at[t, some], buf.at[t, some], sems.at[t]))
    for copy in copies:
        copy.start()
    for t in range(T):
        copies[t].wait()
        for k in range(T - 1 - t, T):
            cols[t, k] = jnp.sum(buf[t, k].reshape(N // 8, 8, N), axis=0)
    head.wait()
    for b in range(T):
        total = jnp.zeros((8, N), F32)
        for t in range(b, T):
            k = T - 1 - t + b
            total = total + cols[t, k] * mask[t, k].astype(F32)
        ahead[b : b + 1, :] = jnp.sum(total, axis=0, keepdims=True)


def ahead_sums(pattern, weights):
    pattern, weights = in_hbm(pattern), in_hbm(weights)
    return call(
        ahead_kernel,
        (shape(T, N), shape(T, T, N, N)),
        [HBM, HBM],
        [
            pltpu.SMEM((T, T), jnp.int32),
            pltpu.VMEM((T, T, 8, N), F32),
            pltpu.SemaphoreType.DMA((T + 1,)),
        ],
        flops=4 * T * T * N * N,
        moved=4 * T * T * N * N,
    )(pattern, weights)


def band_kernel(pattern, weights, kept, reg, high, low, own, mask, buf, cols, extra, sems):
    def copy(t):
        some = slice(0, T - 1 - t)
        return pltpu.make_async_copy(weights.at[t, some], buf.at[t, some], sems.at[t])

    head = pltpu.make_async_copy(pattern, mask, sems.at[T])
    tail = pltpu.make_async_copy(reg, extra, sems.at[T + 1])
    head.start()
    for t in range(T - 1):
        copy(t).start()
    tail.start()
    cols[...] = jnp.zeros_like(cols)
    zero = jnp.zeros((N, N), BF16)
    for a in range(T // 2):
        for piece in (high, low):
            piece[a, N : 2 * N, 0:N] = zero
            piece[a, 0:N, T * N : (T + 1) * N] = zero
    head.wait()

    for a in range(T // 2):
        for half in range(2):
            t = 2 * a + half
            if t < T - 1:
                copy(t).wait()
            rows = jnp.zeros((N, N), F32)
            for k in range(T):
                m = (kept if k >= T - 1 - t else buf)[t, k] * mask[t, k].astype(F32)
                rows = rows + m
                cols[t + k + 1] += jnp.sum(m.reshape(N // 8, 8, N), axis=0)
                h = m.astype(BF16)
                place = slice((k + half) * N, (k + half + 1) * N)
                high[a, half * N : (half + 1) * N, place] = h
                low[a, half * N : (half + 1) * N, place] = (m - h.astype(F32)).astype(BF16)
            own[t : t + 1, :] = jnp.sum(rows.T, axis=0, keepdims=True)
    tail.wait()
    own[...] += jnp.sum(cols[:T], axis=1) + extra[...]


def band_pieces(pattern, weights, kept, reg):
    pattern, weights, reg = in_hbm(pattern), in_hbm(weights), in_hbm(reg)
    return call(
        band_kernel,
        (shape(*BAND, dtype=BF16), shape(*BAND, dtype=BF16), shape(T, N)),
        [HBM, HBM, VMEM, HBM],
        [
            pltpu.SMEM((T, T), jnp.int32),
            pltpu.VMEM((T, T, N, N), F32),
            pltpu.VMEM((2 * T, 8, N), F32),
            pltpu.VMEM((T, N), F32),
            pltpu.SemaphoreType.DMA((T + 2,)),
        ],
        flops=2048 * T * T * N * N,
        moved=8 * T * T * N * N,
    )(pattern, weights, kept, reg)


def put_pieces(pieces, t, value):
    h = value.astype(BF16)
    pieces[0:R, t * N : (t + 1) * N] = h
    pieces[R : 2 * R, t * N : (t + 1) * N] = (value - h.astype(F32)).astype(BF16)


def product(pieces, cols, high, low, mult):
    both = mult(pieces[:, cols], high)
    return (both[:R] + mult(pieces[0:R, cols], low)) + both[R:]


def to_next(pieces, high, low, put):
    for b in range(T // 2):
        total = None
        for a in range(b, T // 2):
            at = slice((7 + 2 * b - 2 * a) * N, (9 + 2 * b - 2 * a) * N)
            term = product(pieces, slice(a * 2 * N, (a + 1) * 2 * N), high[a, :, at], low[a, :, at], dot)
            total = term if total is None else total + term
        put(2 * b, total[:, :N])
        put(2 * b + 1, total[:, N:])


def within(pieces, high, low, out):
    out[0] = jnp.zeros((R, N), F32)
    for p in range(T // 2):
        total = None
        width = 2 * N if p < T // 2 - 1 else N
        for a in range(p + 1):
            at = slice(2 * (p - a) * N, 2 * (p - a) * N + width)
            term = product(pieces, slice(a * 2 * N, (a + 1) * 2 * N), high[a, :, at], low[a, :, at], dot)
            total = term if total is None else total + term
        out[2 * p + 1] = total[:, :N]
        if width > N:
            out[2 * p + 2] = total[:, N:]
    for a in range(T // 2):
        at = slice(0, (7 - 2 * a) * N)
        term = product(pieces, slice((2 * a + 1) * N, T * N), high[a, :, at], low[a, :, at], dot_t)
        out[2 * a] += term[:, :N]
        out[2 * a + 1] += term[:, N:]


def turned_rows(a):
    return slice(a * (a + 1) * N, (a + 1) * (a + 2) * N)


def turn(high, low, turned_high, turned_low):
    for piece, out in ((high, turned_high), (low, turned_low)):
        for a in range(T // 2):
            out[turned_rows(a), :] = piece[a, :, (7 - 2 * a) * N :].T


def from_next(pieces, high, low, put):
    for a in range(T // 2):
        rows = turned_rows(a)
        term = product(pieces, slice(0, (2 * a + 2) * N), high[rows, :], low[rows, :], dot)
        put(2 * a, term[:, :N])
        put(2 * a + 1, term[:, N:])


def store(out):
    def put(t, value):
        out[t] = value

    return put


def moments(first, second):
    high = low = jnp.zeros((R, N), F32)
    for t in range(T):
        high, err = two_sum(high, first[t] * second[t])
        low = low + err
    return high, low


PIECES = pltpu.VMEM((2 * R, T * N), BF16)
ONE_WAY = 2 * 3 * 40 * R * N * N


def choose(flag, first, second):
    return jnp.where(jnp.broadcast_to(flag[0:1, :], (R, N)) > 0, first, second)


BLOCKS = shape(T, R, N)
TURNED = shape((T // 2) * (T // 2 + 1) * N, 2 * N, dtype=BF16)


def on_parity(parity):
    return pl.when(lax.axis_index("tm") % 2 == parity)


def first_kernel(rhs, own, inflow, high, low, diag, vec, two, pieces):
    diag[...] = own[...] + inflow[...]

    @on_parity(0)
    def _():
        for t in range(T):
            value = rhs[t] / diag[t : t + 1, :]
            vec[t] = value
            two[t] = value

    @on_parity(1)
    def _():
        for t in range(T):
            value = rhs[t] / diag[t : t + 1, :]
            vec[t] = value
            put_pieces(pieces, t, value)
        to_next(pieces, high, low, store(two))


def first(*args):
    return call(first_kernel, (shape(T, N), BLOCKS, BLOCKS), [VMEM] * 5, [PIECES], flops=ONE_WAY)(*args)


def local_kernel(count, *refs):
    vecs, (image, high, low, out, found, *more, pieces) = refs[:count], refs[count:]
    for t in range(T):
        put_pieces(pieces, t, vecs[-1][t])
    if more:
        one, *turned = more

        @on_parity(0)
        def _():
            to_next(pieces, high, low, store(one))

        @on_parity(1)
        def _():
            one[...] = vecs[0][...]

        turn(high, low, *turned)
    within(pieces, high, low, out)
    for i, vec in enumerate(vecs):
        h, l = moments(vec, image)
        found[i, 0] = h
        found[i, 1] = l


def local(vecs, image, high, low):
    more = (BLOCKS, TURNED, TURNED) if len(vecs) == 1 else ()
    return call(
        functools.partial(local_kernel, len(vecs)),
        (BLOCKS, shape(len(vecs), 2, R, N)) + more,
        [VMEM] * (len(vecs) + 3),
        [PIECES],
        flops=2 * ONE_WAY,
    )(*vecs, image, high, low)


def add_received(flag, got_one, got_two, partial, turned_high, turned_low, pieces, put):
    for t in range(T):
        put_pieces(pieces, t, choose(flag, got_one[t], got_two[t]))

    def add(t, term):
        put(t, (partial[t] + choose(flag, got_two[t], got_one[t])) + term)

    from_next(pieces, turned_high, turned_low, add)


def step_kernel(
    flag, got_one, got_two, partial, diag, high, low, turned_high, turned_low, image, vec, one, two, pieces, made
):
    def take(t, value):
        image[t] = value
        value = value / diag[t : t + 1, :]
        vec[t] = value
        put_pieces(made, t, value)

    def give(t, value):
        one[t] = choose(flag, value, vec[t])
        two[t] = choose(flag, vec[t], value)

    add_received(flag, got_one, got_two, partial, turned_high, turned_low, pieces, take)
    to_next(made, high, low, give)


def next_step(*args):
    return call(step_kernel, (BLOCKS,) * 4, [VMEM] * 9, [PIECES, PIECES], flops=2 * ONE_WAY)(*args)


PAIRS = 5


def fold(high, low):
    value = (high, low)
    size = high.shape[0]
    while size > 8:
        size //= 2
        value = dd_add(tuple(v[:size] for v in value), tuple(v[size:] for v in value))
    for turn_by in (4, 2, 1):
        value = dd_add(value, tuple(pltpu.roll(v, turn_by, 0) for v in value))
    return value


def gram_kernel(
    flag, got_one, got_two, partial, turned_high, turned_low, v0, v1, v2, m0, m1, m2, image, out, pieces
):
    add_received(flag, got_one, got_two, partial, turned_high, turned_low, pieces, store(image))
    last = [moments(v, image) for v in (v0, v1, v2)]
    every = [(m[i, 0], m[i, 1]) for m in (m0, m1, m2) for i in range(m.shape[0])] + last + last[-1:]
    for q in range(PAIRS):
        pair = every[2 * q : 2 * q + 2]
        h, l = fold(*(jnp.concatenate([f[i] for f in pair], axis=0).T for i in range(2)))
        out[:, q * N : (q + 1) * N] = (h + l)[0:1]


def gram(*args):
    return call(gram_kernel, (BLOCKS, shape(1, PAIRS * N)), [VMEM] * 12, [PIECES], flops=ONE_WAY)(*args)


def solve(matrix, right):
    (a00, a01, a02), (a10, a11, a12), (a20, a21, a22) = matrix
    b0, b1, b2 = right
    inv0 = 1.0 / a00
    f1, f2 = a10 * inv0, a20 * inv0
    c11, c12, e1 = a11 - f1 * a01, a12 - f1 * a02, b1 - f1 * b0
    c21, c22, e2 = a21 - f2 * a01, a22 - f2 * a02, b2 - f2 * b0
    inv1 = 1.0 / c11
    g = c21 * inv1
    x2 = (e2 - g * e1) / (c22 - g * c12)
    x1 = (e1 - c12 * x2) * inv1
    x0 = (b0 - a01 * x1 - a02 * x2) * inv0
    return x0, x1, x2


def result_kernel(parts, v0, v1, v2, y0, y1, y2, y3, sol, res):
    flat = []
    for q in range(PAIRS):
        part = parts[:, q * N : (q + 1) * N]
        h, l = (v[0:1] for v in fold(part, jnp.zeros_like(part)))
        flat += [(h, l), (pltpu.roll(h, R, 1), pltpu.roll(l, R, 1))]
    g00, g01, g11, g02, g12, g22, g03, g13, g23 = flat[:9]
    full = ((g00, g01, g02, g03), (g01, g11, g12, g13), (g02, g12, g22, g23))
    minus = lambda a, b: dd_add(a, (-b[0], -b[1]))
    matrix = [[minus(row[j], row[j + 1]) for j in range(3)] for row in full]
    right = [row[1] for row in full]
    near = [[m[0] + m[1] for m in row] for row in matrix]
    coef = [jnp.zeros_like(g00[0])] * 3
    for _ in range(3):
        left = []
        for row, value in zip(matrix, right):
            for m, c in zip(row, coef):
                p, e = two_prod(m[0], c)
                value = minus(value, (p, e + m[1] * c))
            left.append(value[0] + value[1])
        coef = [c + s for c, s in zip(coef, solve(near, left))]
    rows = jnp.concatenate([c[:, :N] for c in coef] + [jnp.zeros((N - 3, N), F32)], axis=0).T
    d0, d1, d2 = (jnp.broadcast_to(rows[:R, i : i + 1], (R, N)) for i in range(3))
    for t in range(T):
        sol[t] = v0[t] + (d0 * v0[t] + d1 * v1[t] + d2 * v2[t])
        first, second = y1[t], y2[t]
        res[t] = first - (d0 * (y0[t] - first) + d1 * (first - second) + d2 * (second - y3[t]))


def result(parts, vecs, images):
    return call(result_kernel, (shape(T, R, N), shape(T, R, N)), [VMEM] * 8)(parts, *vecs, *images)


def shift(value, steps):
    count = lax.axis_size("tm")
    return lax.ppermute(value, "tm", [(i, (i + steps) % count) for i in range(count)])


def all_parts(value):
    count = lax.axis_size("tm")
    half, eighth = count // 2, count // 8
    last = [half - 1, half]
    near = [i for i in range(half - eighth, half + eighth) if i not in last]
    turns = [*range(half + eighth, count), *near, *last, *range(half - eighth)]
    spread = lax.all_to_all(
        jnp.broadcast_to(value[None], (count,) + value.shape), "tm", 0, 0, axis_index_groups=[turns]
    )
    return spread.reshape(count, value.shape[1])


def swap_within(value):
    return lax.ppermute(value, "tm", [(i, i ^ 1) for i in range(lax.axis_size("tm"))])


def swap_across(value):
    count = lax.axis_size("tm")
    return lax.ppermute(value, "tm", [(i, (i + (1 if i % 2 else -1)) % count) for i in range(count)])


def shards(weights, pattern, shift_reg, rhs):
    flag = jnp.broadcast_to((1 - lax.axis_index("tm") % 2).astype(F32), (8, N))
    flag, pattern = lax.optimization_barrier((flag, pattern))
    ahead, kept = ahead_sums(pattern, weights)
    inflow = shift(ahead, 1)
    high, low, own = band_pieces(pattern, weights, kept, shift_reg)
    diag, vec, two = first(rhs, own, inflow, high, low)
    got_two = swap_across(two)
    partial, part, one, *turned = local([vec], rhs, high, low)
    got = swap_within(one), got_two
    vecs, images, found = [vec], [rhs], [part]
    for step in range(2):
        image, vec, one, two = next_step(flag, *got, partial, diag, high, low, *turned)
        got = swap_within(one), swap_across(two)
        images.append(image)
        vecs.append(vec)
        partial, part = local(vecs, image, high, low)
        found.append(part)
    image, part = gram(flag, *got, partial, *turned, *vecs, *found)
    return result(all_parts(part), vecs, images + [image])


def solution(mesh):
    return jax.shard_map(
        shards,
        mesh=mesh,
        in_specs=(P("tm", None, None, None), P("tm", None), P("tm", None), P("tm", "scen", None)),
        out_specs=(P("tm", "scen", None), P("tm", "scen", None)),
        check_vma=False,
    )
```

```python
import functools

import jax
import jax.numpy as jnp
from jax import lax
from jax.experimental import pallas as pl
from jax.experimental.pallas import tpu as pltpu
from jax.sharding import PartitionSpec as P

F32 = jnp.float32
BF16 = jnp.bfloat16
MIB = 1024 * 1024
N = 128
T = 8
R = 64
VMEM = pl.BlockSpec(memory_space=pltpu.VMEM)
HBM = pl.BlockSpec(memory_space=pltpu.HBM)

BAND = (T // 2, 2 * N, (T + 1) * N)


def call(body, outs, specs=None, scratch=(), limit=16, flops=0, moved=0):
    return pl.pallas_call(
        body,
        out_shape=outs,
        in_specs=specs,
        out_specs=jax.tree.map(lambda _: VMEM, outs),
        scratch_shapes=list(scratch),
        compiler_params=pltpu.CompilerParams(vmem_limit_bytes=limit * MIB),
        cost_estimate=pl.CostEstimate(flops=flops, bytes_accessed=moved, transcendentals=0),
    )


def in_hbm(value):
    return pltpu.with_memory_space_constraint(value, pltpu.HBM)


def shape(*dims, dtype=F32):
    return jax.ShapeDtypeStruct(dims, dtype)


def dot(a, b):
    return lax.dot_general(a, b, (((1,), (0,)), ((), ())), preferred_element_type=F32)


def dot_t(a, b):
    return lax.dot_general(a, b, (((1,), (1,)), ((), ())), preferred_element_type=F32)


def two_sum(a, b):
    s = a + b
    t = s - a
    return s, (a - (s - t)) + (b - t)


def dd_add(a, b):
    s, e = two_sum(a[0], b[0])
    return s, e + (a[1] + b[1])


def halves(a):
    t = a * 4097.0
    h = t - (t - a)
    return h, a - h


def two_prod(a, b):
    p = a * b
    ah, al = halves(a)
    bh, bl = halves(b)
    return p, ((ah * bh - p) + ah * bl + al * bh) + al * bl


def ahead_kernel(pattern, weights, ahead, mask, buf, cols, sems):
    head = pltpu.make_async_copy(pattern, mask, sems.at[T])
    head.start()
    copies = []
    for t in range(T):
        some = slice(T - 1 - t, T)
        copies.append(pltpu.make_async_copy(weights.at[t, some], buf.at[t, some], sems.at[t]))
    for copy in copies:
        copy.start()
    for t in range(T):
        copies[t].wait()
        for k in range(T - 1 - t, T):
            cols[t, k] = jnp.sum(buf[t, k].reshape(N // 8, 8, N), axis=0)
    head.wait()
    for b in range(T):
        total = jnp.zeros((8, N), F32)
        for t in range(b, T):
            k = T - 1 - t + b
            total = total + cols[t, k] * mask[t, k].astype(F32)
        ahead[b : b + 1, :] = jnp.sum(total, axis=0, keepdims=True)


def ahead_sums(pattern, weights):
    pattern, weights = in_hbm(pattern), in_hbm(weights)
    return call(
        ahead_kernel,
        shape(T, N),
        [HBM, HBM],
        [
            pltpu.SMEM((T, T), jnp.int32),
            pltpu.VMEM((T, T, N, N), F32),
            pltpu.VMEM((T, T, 8, N), F32),
            pltpu.SemaphoreType.DMA((T + 1,)),
        ],
        flops=4 * T * T * N * N,
        moved=4 * T * T * N * N,
    )(pattern, weights)


def band_kernel(pattern, weights, reg, high, low, own, mask, buf, cols, extra, sems):
    def copy(t):
        return pltpu.make_async_copy(weights.at[t], buf.at[t], sems.at[t])

    head = pltpu.make_async_copy(pattern, mask, sems.at[T])
    tail = pltpu.make_async_copy(reg, extra, sems.at[T + 1])
    head.start()
    for t in range(T):
        copy(t).start()
    tail.start()
    cols[...] = jnp.zeros_like(cols)
    zero = jnp.zeros((N, N), BF16)
    for a in range(T // 2):
        for piece in (high, low):
            piece[a, N : 2 * N, 0:N] = zero
            piece[a, 0:N, T * N : (T + 1) * N] = zero
    head.wait()

    def step(a, carry):
        for half in range(2):
            t = 2 * a + half
            copy(t).wait()
            rows = jnp.zeros((N, N), F32)
            for k in range(T):
                m = buf[t, k] * mask[t, k].astype(F32)
                rows = rows + m
                cols[t + k + 1] += jnp.sum(m.reshape(N // 8, 8, N), axis=0)
                h = m.astype(BF16)
                place = slice((k + half) * N, (k + half + 1) * N)
                high[a, half * N : (half + 1) * N, place] = h
                low[a, half * N : (half + 1) * N, place] = (m - h.astype(F32)).astype(BF16)
            own[pl.ds(t, 1), :] = jnp.sum(rows.T, axis=0, keepdims=True)
        return carry

    lax.fori_loop(0, T // 2, step, 0)
    tail.wait()
    own[...] += jnp.sum(cols[:T], axis=1) + extra[...]


def band_pieces(pattern, weights, reg):
    pattern, weights, reg = in_hbm(pattern), in_hbm(weights), in_hbm(reg)
    return call(
        band_kernel,
        (shape(*BAND, dtype=BF16), shape(*BAND, dtype=BF16), shape(T, N)),
        [HBM, HBM, HBM],
        [
            pltpu.SMEM((T, T), jnp.int32),
            pltpu.VMEM((T, T, N, N), F32),
            pltpu.VMEM((2 * T, 8, N), F32),
            pltpu.VMEM((T, N), F32),
            pltpu.SemaphoreType.DMA((T + 2,)),
        ],
        flops=2048 * T * T * N * N,
        moved=8 * T * T * N * N,
    )(pattern, weights, reg)


def put_pieces(pieces, t, value):
    h = value.astype(BF16)
    pieces[0:R, t * N : (t + 1) * N] = h
    pieces[R : 2 * R, t * N : (t + 1) * N] = (value - h.astype(F32)).astype(BF16)


def product(pieces, cols, high, low, mult):
    both = mult(pieces[:, cols], high)
    return (both[:R] + mult(pieces[0:R, cols], low)) + both[R:]


def to_next(pieces, high, low, put):
    for b in range(T // 2):
        total = None
        for a in range(b, T // 2):
            at = slice((7 + 2 * b - 2 * a) * N, (9 + 2 * b - 2 * a) * N)
            term = product(pieces, slice(a * 2 * N, (a + 1) * 2 * N), high[a, :, at], low[a, :, at], dot)
            total = term if total is None else total + term
        put(2 * b, total[:, :N])
        put(2 * b + 1, total[:, N:])


def within(pieces, high, low, out):
    out[0] = jnp.zeros((R, N), F32)
    for p in range(T // 2):
        total = None
        width = 2 * N if p < T // 2 - 1 else N
        for a in range(p + 1):
            at = slice(2 * (p - a) * N, 2 * (p - a) * N + width)
            term = product(pieces, slice(a * 2 * N, (a + 1) * 2 * N), high[a, :, at], low[a, :, at], dot)
            total = term if total is None else total + term
        out[2 * p + 1] = total[:, :N]
        if width > N:
            out[2 * p + 2] = total[:, N:]
    for a in range(T // 2):
        at = slice(0, (7 - 2 * a) * N)
        term = product(pieces, slice((2 * a + 1) * N, T * N), high[a, :, at], low[a, :, at], dot_t)
        out[2 * a] += term[:, :N]
        out[2 * a + 1] += term[:, N:]


def turned_rows(a):
    return slice(a * (a + 1) * N, (a + 1) * (a + 2) * N)


def turn(high, low, turned_high, turned_low):
    for piece, out in ((high, turned_high), (low, turned_low)):
        for a in range(T // 2):
            out[turned_rows(a), :] = piece[a, :, (7 - 2 * a) * N :].T


def from_next(pieces, high, low, put):
    for a in range(T // 2):
        rows = turned_rows(a)
        term = product(pieces, slice(0, (2 * a + 2) * N), high[rows, :], low[rows, :], dot)
        put(2 * a, term[:, :N])
        put(2 * a + 1, term[:, N:])


def store(out):
    def put(t, value):
        out[t] = value

    return put


def moments(first, second):
    high = low = jnp.zeros((R, N), F32)
    for t in range(T):
        high, err = two_sum(high, first[t] * second[t])
        low = low + err
    return high, low


PIECES = pltpu.VMEM((2 * R, T * N), BF16)
ONE_WAY = 2 * 3 * 40 * R * N * N


def choose(flag, first, second):
    return jnp.where(jnp.broadcast_to(flag[0:1, :], (R, N)) > 0, first, second)


BLOCKS = shape(T, R, N)
TURNED = shape((T // 2) * (T // 2 + 1) * N, 2 * N, dtype=BF16)


def on_parity(parity):
    return pl.when(lax.axis_index("tm") % 2 == parity)


def first_kernel(rhs, own, inflow, high, low, diag, vec, two, pieces):
    diag[...] = own[...] + inflow[...]

    @on_parity(0)
    def _():
        for t in range(T):
            value = rhs[t] / diag[t : t + 1, :]
            vec[t] = value
            two[t] = value

    @on_parity(1)
    def _():
        for t in range(T):
            value = rhs[t] / diag[t : t + 1, :]
            vec[t] = value
            put_pieces(pieces, t, value)
        to_next(pieces, high, low, store(two))


def first(*args):
    return call(first_kernel, (shape(T, N), BLOCKS, BLOCKS), [VMEM] * 5, [PIECES], flops=ONE_WAY)(*args)


def local_kernel(count, *refs):
    vecs, (image, high, low, out, found, *more, pieces) = refs[:count], refs[count:]
    for t in range(T):
        put_pieces(pieces, t, vecs[-1][t])
    if more:
        one, *turned = more

        @on_parity(0)
        def _():
            to_next(pieces, high, low, store(one))

        @on_parity(1)
        def _():
            one[...] = vecs[0][...]

        turn(high, low, *turned)
    within(pieces, high, low, out)
    for i, vec in enumerate(vecs):
        h, l = moments(vec, image)
        found[i, 0] = h
        found[i, 1] = l


def local(vecs, image, high, low):
    more = (BLOCKS, TURNED, TURNED) if len(vecs) == 1 else ()
    return call(
        functools.partial(local_kernel, len(vecs)),
        (BLOCKS, shape(len(vecs), 2, R, N)) + more,
        [VMEM] * (len(vecs) + 3),
        [PIECES],
        flops=2 * ONE_WAY,
    )(*vecs, image, high, low)


def add_received(flag, got_one, got_two, partial, turned_high, turned_low, pieces, put):
    for t in range(T):
        put_pieces(pieces, t, choose(flag, got_one[t], got_two[t]))

    def add(t, term):
        put(t, (partial[t] + choose(flag, got_two[t], got_one[t])) + term)

    from_next(pieces, turned_high, turned_low, add)


def step_kernel(
    flag, got_one, got_two, partial, diag, high, low, turned_high, turned_low, image, vec, one, two, pieces, made
):
    def take(t, value):
        image[t] = value
        value = value / diag[t : t + 1, :]
        vec[t] = value
        put_pieces(made, t, value)

    def give(t, value):
        one[t] = choose(flag, value, vec[t])
        two[t] = choose(flag, vec[t], value)

    add_received(flag, got_one, got_two, partial, turned_high, turned_low, pieces, take)
    to_next(made, high, low, give)


def next_step(*args):
    return call(step_kernel, (BLOCKS,) * 4, [VMEM] * 9, [PIECES, PIECES], flops=2 * ONE_WAY)(*args)


PAIRS = 5


def fold(high, low):
    value = (high, low)
    size = high.shape[0]
    while size > 8:
        size //= 2
        value = dd_add(tuple(v[:size] for v in value), tuple(v[size:] for v in value))
    for turn_by in (4, 2, 1):
        value = dd_add(value, tuple(pltpu.roll(v, turn_by, 0) for v in value))
    return value


def gram_kernel(
    flag, got_one, got_two, partial, turned_high, turned_low, v0, v1, v2, m0, m1, m2, image, out, pieces
):
    add_received(flag, got_one, got_two, partial, turned_high, turned_low, pieces, store(image))
    last = [moments(v, image) for v in (v0, v1, v2)]
    every = [(m[i, 0], m[i, 1]) for m in (m0, m1, m2) for i in range(m.shape[0])] + last + last[-1:]
    for q in range(PAIRS):
        pair = every[2 * q : 2 * q + 2]
        h, l = fold(*(jnp.concatenate([f[i] for f in pair], axis=0).T for i in range(2)))
        out[:, q * N : (q + 1) * N] = (h + l)[0:1]


def gram(*args):
    return call(gram_kernel, (BLOCKS, shape(1, PAIRS * N)), [VMEM] * 12, [PIECES], flops=ONE_WAY)(*args)


def solve(matrix, right):
    (a00, a01, a02), (a10, a11, a12), (a20, a21, a22) = matrix
    b0, b1, b2 = right
    inv0 = 1.0 / a00
    f1, f2 = a10 * inv0, a20 * inv0
    c11, c12, e1 = a11 - f1 * a01, a12 - f1 * a02, b1 - f1 * b0
    c21, c22, e2 = a21 - f2 * a01, a22 - f2 * a02, b2 - f2 * b0
    inv1 = 1.0 / c11
    g = c21 * inv1
    x2 = (e2 - g * e1) / (c22 - g * c12)
    x1 = (e1 - c12 * x2) * inv1
    x0 = (b0 - a01 * x1 - a02 * x2) * inv0
    return x0, x1, x2


def result_kernel(parts, v0, v1, v2, y0, y1, y2, y3, sol, res):
    flat = []
    for q in range(PAIRS):
        part = parts[:, q * N : (q + 1) * N]
        h, l = (v[0:1] for v in fold(part, jnp.zeros_like(part)))
        flat += [(h, l), (pltpu.roll(h, R, 1), pltpu.roll(l, R, 1))]
    g00, g01, g11, g02, g12, g22, g03, g13, g23 = flat[:9]
    full = ((g00, g01, g02, g03), (g01, g11, g12, g13), (g02, g12, g22, g23))
    minus = lambda a, b: dd_add(a, (-b[0], -b[1]))
    matrix = [[minus(row[j], row[j + 1]) for j in range(3)] for row in full]
    right = [row[1] for row in full]
    near = [[m[0] + m[1] for m in row] for row in matrix]
    coef = solve(near, [value[0] + value[1] for value in right])
    for _ in range(2):
        left = []
        for row, value in zip(matrix, right):
            for m, c in zip(row, coef):
                p, e = two_prod(m[0], c)
                value = minus(value, (p, e + m[1] * c))
            left.append(value[0] + value[1])
        coef = [c + s for c, s in zip(coef, solve(near, left))]
    rows = jnp.concatenate([c[:, :N] for c in coef] + [jnp.zeros((N - 3, N), F32)], axis=0).T
    d0, d1, d2 = (jnp.broadcast_to(rows[:R, i : i + 1], (R, N)) for i in range(3))
    for t in range(T):
        sol[t] = v0[t] + (d0 * v0[t] + d1 * v1[t] + d2 * v2[t])
        first, second = y1[t], y2[t]
        res[t] = first - (d0 * (y0[t] - first) + d1 * (first - second) + d2 * (second - y3[t]))


def result(parts, vecs, images):
    return call(result_kernel, (shape(T, R, N), shape(T, R, N)), [VMEM] * 8)(parts, *vecs, *images)


def shift(value, steps):
    count = lax.axis_size("tm")
    return lax.ppermute(value, "tm", [(i, (i + steps) % count) for i in range(count)])


def all_parts(value):
    count = lax.axis_size("tm")
    half, eighth = count // 2, count // 8
    last = [half - 1, half]
    near = [i for i in range(half - eighth, half + eighth) if i not in last]
    turns = [*range(half + eighth, count), *near, *last, *range(half - eighth)]
    spread = lax.all_to_all(
        jnp.broadcast_to(value[None], (count,) + value.shape), "tm", 0, 0, axis_index_groups=[turns]
    )
    return spread.reshape(count, value.shape[1])


def swap_within(value):
    return lax.ppermute(value, "tm", [(i, i ^ 1) for i in range(lax.axis_size("tm"))])


def swap_across(value):
    count = lax.axis_size("tm")
    return lax.ppermute(value, "tm", [(i, (i + (1 if i % 2 else -1)) % count) for i in range(count)])


def shards(weights, pattern, shift_reg, rhs):
    flag = jnp.broadcast_to((1 - lax.axis_index("tm") % 2).astype(F32), (8, N))
    flag, pattern = lax.optimization_barrier((flag, pattern))
    inflow = shift(ahead_sums(pattern, weights), 1)
    high, low, own = band_pieces(pattern, weights, shift_reg)
    diag, vec, two = first(rhs, own, inflow, high, low)
    got_two = swap_across(two)
    partial, part, one, *turned = local([vec], rhs, high, low)
    got = swap_within(one), got_two
    vecs, images, found = [vec], [rhs], [part]
    for step in range(2):
        image, vec, one, two = next_step(flag, *got, partial, diag, high, low, *turned)
        got = swap_within(one), swap_across(two)
        images.append(image)
        vecs.append(vec)
        partial, part = local(vecs, image, high, low)
        found.append(part)
    image, part = gram(flag, *got, partial, *turned, *vecs, *found)
    return result(all_parts(part), vecs, images + [image])


def solution(mesh):
    return jax.shard_map(
        shards,
        mesh=mesh,
        in_specs=(P("tm", None, None, None), P("tm", None), P("tm", None), P("tm", "scen", None)),
        out_specs=(P("tm", "scen", None), P("tm", "scen", None)),
        check_vma=False,
    )
```
